128 devices in a mesh: spatial: 8 (over z, core), filter: 8 (over y, x_lo), sample: 2 (over x_hi).
Axes of the slice: x: 4 (x_hi: 2, x_lo: 2; x = x_hi * 2 + x_lo), y: 4, z: 4, core: 2. Of those that a mesh axis runs over, the one named last changes fastest.
Arguments:
- volume: bfloat16 [2, 64, 32, 16, 128], P('sample', None, 'spatial', 'filter'), may hold values from -6 to 6
- weight_first: bfloat16 [27, 64, 128], replicated, may hold values from -0.15625 to 0.15625
- weight_second: bfloat16 [27, 128, 256], P(None, None, 'filter'), may hold values from -0.109375 to 0.109375
- cotangent: bfloat16 [2, 256, 32, 16, 128], P('sample', 'filter', 'spatial'), may hold values from -6 to 6
Outputs:
- mapped: float32 [2, 256, 32, 16, 128], P('sample', 'filter', 'spatial')
- second_grad: float32 [27, 128, 256], P(None, None, 'filter')
- first_grad: float32 [27, 64, 128], replicated
- volume_grad: float32 [2, 64, 32, 16, 128], P('sample', None, 'spatial', 'filter')
The draws below stay inside these ranges and needn't reach their ends.
All inputs are finite; a program needn't handle non-finite values.
Results may differ from the reference program's by a relative error of at most 0.003.
Values may be sent and summed in bfloat16 or wider, within the bound.
A program may use at most 256 MiB of HBM per device.

```python
import math
import jax
import jax.numpy as jnp

CIN = 64
CMID = 128
COUT = 256
GZ = 128
SAMPLES = 2
GX = 32
GY = 16


def block_scale(rng, shape, shards, low, top_value):
    level = 1.0
    for axis_at, blocks in shards:
        heights = jax.random.uniform(jax.random.fold_in(jax.random.fold_in(rng, 6), axis_at), (blocks,), jnp.float32, low / len(shards), top_value / len(shards))
        level = level * jnp.repeat(jnp.exp(heights), shape[axis_at] // blocks).reshape((-1,) + (1,) * (len(shape) - 1 - axis_at))
    return level


def scatter_about(stream_key, dims, scale, most, split=(), held_as=jnp.bfloat16):
    result = jax.random.normal(stream_key, dims, jnp.float32) * scale
    if len(split) > 0:
        result = block_scale(stream_key, dims, split, -0.22, 0.18) * result
    return jnp.clip(result, min=-most, max=most).astype(held_as)


def setup_inputs(seed: int = 0) -> dict:
    arg_keys = jax.random.split(jax.random.key(seed), 5)
    volume = scatter_about(arg_keys[0], (SAMPLES, CIN, GX, GY, GZ), 1.0, 6.0, ((0, 2), (2, 8), (3, 8)))
    weight_first = scatter_about(arg_keys[1], (27, CIN, CMID), (27 * CIN) ** -0.5, 0.15625)
    weight_second = scatter_about(arg_keys[2], (27, CMID, COUT), (27 * CMID) ** -0.5, 0.109375, ((2, 8),))
    cotangent = scatter_about(arg_keys[3], (SAMPLES, COUT, GX, GY, GZ), 1.0, 6.0, ((0, 2), (1, 8), (2, 8)))
    return dict(volume=volume, weight_first=weight_first, weight_second=weight_second, cotangent=cotangent)


def pad_grid(field):
    return jnp.pad(field, ((0, 0), (0, 0), (1, 1), (1, 1), (1, 1)))

def forward_terms(padded, weight, depth, height, length):
    total = None
    for step_x in range(3):
        for step_y in range(3):
            for step_z in range(3):
                offset = step_x * 9 + step_y * 3 + step_z
                piece = padded[:, :, step_x:step_x + depth, step_y:step_y + height, step_z:step_z + length]
                term = jnp.einsum('io,sixyz->soxyz', weight[offset].astype(jnp.float32), piece.astype(jnp.float32))
                total = term if total is None else total + term
    return total

def backward_terms(padded, weight, depth, height, length):
    total = None
    for step_x in range(3):
        for step_y in range(3):
            for step_z in range(3):
                offset = step_x * 9 + step_y * 3 + step_z
                piece = padded[:, :, 2 - step_x:2 - step_x + depth, 2 - step_y:2 - step_y + height, 2 - step_z:2 - step_z + length]
                term = jnp.einsum('io,soxyz->sixyz', weight[offset].astype(jnp.float32), piece.astype(jnp.float32))
                total = term if total is None else total + term
    return total

def weight_terms(padded, grads, depth, height, length):
    terms = []
    for step_x in range(3):
        for step_y in range(3):
            for step_z in range(3):
                piece = padded[:, :, step_x:step_x + depth, step_y:step_y + height, step_z:step_z + length]
                terms.append(jnp.einsum('sixyz,soxyz->io', piece.astype(jnp.float32), grads.astype(jnp.float32)))
    return jnp.stack(terms)

def reference(volume, weight_first, weight_second, cotangent):
    count, _, depth, height, length = volume.shape
    scaling = 1.0 / math.sqrt(count * depth * height * length)
    vol_padded = pad_grid(volume)
    first_pre = forward_terms(vol_padded, weight_first, depth, height, length)
    hidden = jax.nn.silu(first_pre).astype(jnp.bfloat16)
    hid_padded = pad_grid(hidden)
    mapped = forward_terms(hid_padded, weight_second, depth, height, length)
    second_grad = weight_terms(hid_padded, cotangent, depth, height, length) * scaling
    back_hidden = backward_terms(pad_grid(cotangent), weight_second, depth, height, length)
    sigmoid_value = jax.nn.sigmoid(first_pre)
    back_pre = (back_hidden * (sigmoid_value * (1.0 + first_pre * (1.0 - sigmoid_value)))).astype(jnp.bfloat16)
    volume_grad = backward_terms(pad_grid(back_pre), weight_first, depth, height, length)
    first_grad = weight_terms(vol_padded, back_pre, depth, height, length) * scaling
    return (mapped, second_grad, first_grad, volume_grad)
```

```python
import functools
import math

import jax
import jax.numpy as jnp
from jax import lax
from jax.experimental import pallas as pl
from jax.experimental.pallas import tpu as pltpu
from jax.sharding import PartitionSpec as P

MESH = pl.DeviceIdType.MESH
BF = jnp.bfloat16
F32 = jnp.float32
VMEM = pl.BlockSpec(memory_space=pltpu.VMEM)
LIMIT = 56 * 1024 * 1024


def remote(src, dst, send, recv, device):
    return pltpu.make_async_remote_copy(
        src_ref=src, dst_ref=dst, send_sem=send, recv_sem=recv, device_id=device, device_id_type=MESH
    )


def greet(partners):
    barrier = pltpu.get_barrier_semaphore()
    for partner in partners:
        pl.semaphore_signal(barrier, inc=1, device_id=partner, device_id_type=MESH)
    pl.semaphore_wait(barrier, len(partners))


def places():
    ns, nf, nm = lax.axis_size("spatial"), lax.axis_size("filter"), lax.axis_size("sample")
    s, f, m = lax.axis_index("spatial"), lax.axis_index("filter"), lax.axis_index("sample")
    return ns, nf, nm, s, f, m


def call(kernel, count, outs, scratch, collective_id=None):
    params = dict(vmem_limit_bytes=LIMIT)
    if collective_id is not None:
        params.update(collective_id=collective_id, has_side_effects=True)
    return pl.pallas_call(
        kernel,
        out_shape=[jax.ShapeDtypeStruct(shape, dtype) for shape, dtype in outs],
        in_specs=[VMEM] * count,
        out_specs=[VMEM] * len(outs),
        scratch_shapes=scratch,
        compiler_params=pltpu.CompilerParams(**params),
    )


def dma(n):
    return pltpu.SemaphoreType.DMA((n,))


def exchange_inputs(
    vt, ct, wl, vs, cx, cg, wg,
    v_s, v_r, c_s, c_r, h_s, h_r, e_s, e_r, w_s, w_r, x_s, x_r, y_s, y_r, q_s, q_r,
):
    ns, nf, nm, s, f, m = places()
    depth = vt.shape[0]
    rows = 2 * nf
    part = wl.shape[0] // ns
    nz = ns // 2
    core, z = lax.rem(s, 2), s // 2
    prev, after = {"spatial": lax.rem(s + ns - 1, ns)}, {"spatial": lax.rem(s + 1, ns)}
    peers = [lax.rem(f + r, nf) for r in range(1, nf)]
    greet([{"filter": p} for p in peers] + [{"spatial": lax.rem(s + r, ns)} for r in range(1, ns)])

    halo = [
        remote(ct.at[0], cx.at[depth + 1], h_s.at[0], h_r.at[0], prev),
        remote(ct.at[depth - 1], cx.at[0], h_s.at[1], h_r.at[1], after),
    ]
    for copy in halo:
        copy.start()
    mine = pl.ds(s * part, part)
    weights = [
        remote(wl.at[mine], wg.at[f, mine], w_s.at[i], w_r.at[i], {"filter": p})
        for i, p in enumerate(peers)
    ]
    blocks = [
        remote(vt, vs.at[pl.ds(1, depth), pl.ds(1 + 2 * f, 2)], v_s.at[i], v_r.at[i], {"filter": p})
        for i, p in enumerate(peers)
    ]
    cots = [
        remote(
            ct.at[:, pl.ds(2 * p, 4)], cg.at[f, pl.ds(1, depth)], c_s.at[i], c_r.at[i], {"filter": p}
        )
        for i, p in enumerate(peers)
    ]
    for group in (weights, cots, blocks):
        for copy in group:
            copy.start()

    vs[:, 0] = jnp.zeros_like(vs[:, 0])
    vs[:, rows + 1] = jnp.zeros_like(vs[:, 0])
    vs[pl.ds(1, depth), pl.ds(1 + 2 * f, 2)] = vt[...]
    cx[pl.ds(1, depth)] = ct[...]
    cg[f, pl.ds(1, depth)] = ct[:, pl.ds(2 * f, 4)]
    wg[f, mine] = wl[mine]

    for copy in halo:
        copy.wait()

    @pl.when(s == 0)
    def _():
        cx[0] = jnp.zeros_like(cx[0])

    @pl.when(s == ns - 1)
    def _():
        cx[depth + 1] = jnp.zeros_like(cx[0])

    edges = []
    for i, p in enumerate(peers):
        for e, plane in enumerate((0, depth + 1)):
            n = 2 * i + e
            edges.append(
                remote(cx.at[plane, pl.ds(2 * p, 4)], cg.at[f, plane], e_s.at[n], e_r.at[n], {"filter": p})
            )
    for copy in edges:
        copy.start()
    for plane in (0, depth + 1):
        cg[f, plane] = cx[plane, pl.ds(2 * f, 4)]

    for copy in weights:
        copy.wait()
    along = []
    for r in range(1, nz):
        target = {"spatial": lax.rem(z + r, nz) * 2 + core}
        along.append(remote(wg.at[:, mine], wg.at[:, mine], x_s.at[r - 1], x_r.at[r - 1], target))
    for copy in along:
        copy.start()
    for copy in blocks:
        copy.wait()
    inner = pl.ds(1, rows)
    planes = [
        remote(vs.at[1, inner], vs.at[depth + 1, inner], q_s.at[0], q_r.at[0], prev),
        remote(vs.at[depth, inner], vs.at[0, inner], q_s.at[1], q_r.at[1], after),
    ]
    for copy in planes:
        copy.start()
    for copy in along:
        copy.wait()
    across = []
    for k in range(nz):
        piece = pl.ds((2 * k + core) * part, part)
        across.append(
            remote(wg.at[:, piece], wg.at[:, piece], y_s.at[k], y_r.at[k], {"spatial": s + 1 - 2 * core})
        )
    for copy in across:
        copy.start()
    for copy in planes:
        copy.wait()

    @pl.when(s == 0)
    def _():
        vs[0] = jnp.zeros_like(vs[0])

    @pl.when(s == ns - 1)
    def _():
        vs[depth + 1] = jnp.zeros_like(vs[0])

    for group in (cots, edges, across):
        for copy in group:
            copy.wait()


def shifted(cells):
    wide = cells.astype(F32)
    lane = lax.broadcasted_iota(jnp.int32, wide.shape, 1)
    below = jnp.where(lane == 0, 0.0, pltpu.roll(wide, 1, 1)).astype(BF)
    above = jnp.where(lane == 127, 0.0, pltpu.roll(wide, 127, 1)).astype(BF)
    return below, cells, above


def spread(src, dst, flip):
    count, channels, _ = src.shape

    def body(i, carry):
        below, here, above = shifted(src[i])
        first, last = (above, below) if flip else (below, above)
        dst[i, pl.ds(0, channels)] = first
        dst[i, pl.ds(channels, channels)] = here
        dst[i, pl.ds(2 * channels, channels)] = last
        return carry

    lax.fori_loop(0, count, body, 0)


def columns(ref, wide, rows_at, flip, pad):
    stack = []
    for sx in range(3):
        for sy in range(3):
            ox, oy = (2 - sx, 2 - sy) if flip else (sx, sy)
            stack.append(jnp.concatenate([ref[(x + ox) * wide + (y + oy)] for x, y in rows_at], axis=1))
    if pad:
        stack.append(jnp.zeros((pad, 128 * len(rows_at)), BF))
    return jnp.concatenate(stack, axis=0)


NT = (((1,), (1,)), ((), ()))


def middle(vs, cx, cg, wg, w1, wm, me, g2, bp, v3o, v3, c3, x3, hs, pre, acc, w1t):
    ns, nf, nm, s, f, m = places()
    depth, rows = 4, 2 * nf
    wide = rows + 2
    w1t[...] = w1[...].T
    spread(vs, v3, False)

    hs[...] = jnp.zeros_like(hs)

    def first(i, carry):
        x, y = i // (rows // 4), lax.rem(i, rows // 4) * 4
        value = jnp.dot(
            w1t[...], columns(v3, wide, [(x, y + j) for j in range(4)], False, 0),
            preferred_element_type=F32,
        )
        hidden = (value * jax.nn.sigmoid(value)).astype(BF)
        for j in range(4):
            pre[x * rows + y + j] = value[:, 128 * j : 128 * (j + 1)]
            hs[x * wide + y + 1 + j] = hidden[:, 128 * j : 128 * (j + 1)]
        return carry

    lax.fori_loop(0, depth * rows // 4, first, 0)

    acc[...] = jnp.zeros_like(acc)
    own = [(x, y) for x in range(depth) for y in range(2)]

    def back(k, carry):
        spread(cg.at[k], c3, True)
        for half in range(2):
            lanes = pl.ds(512 * half, 512)
            acc[:, lanes] += jnp.dot(
                wg[k], columns(c3, 4, own[4 * half : 4 * half + 4], True, 32), preferred_element_type=F32
            )
        return carry

    lax.fori_loop(0, nf, back, 0)
    for n, (x, y) in enumerate(own):
        u = pre[x * rows + 2 * f + y]
        sig = jax.nn.sigmoid(u)
        bp[n] = (acc[:, 128 * n : 128 * (n + 1)] * (sig * (1.0 + u * (1.0 - sig)))).astype(BF)
    for x in range(depth + 2):
        for y in range(4):
            v3o[x * 4 + y] = v3[x * wide + 2 * f + y]

    spread(cx, x3, True)
    me[...] = jnp.zeros_like(me)
    g2[...] = jnp.zeros_like(g2)

    def second(i, carry):
        x, y = i // (rows // 4), lax.rem(i, rows // 4) * 4
        at = [(x, y + j) for j in range(4)]
        field = jnp.concatenate(
            [
                jnp.concatenate([hs[x * wide + y + j + sy] for j in range(4)], axis=1)
                for sy in range(3)
            ],
            axis=0,
        )
        value = jnp.dot(wm[...], field, preferred_element_type=F32)
        lane = lax.broadcasted_iota(jnp.int32, (32, 128), 1)
        for sx in range(3):
            for j in range(4):
                lanes = slice(128 * j, 128 * (j + 1))
                base = 96 * sx
                below = pltpu.roll(value[base : base + 32, lanes], 1, 1)
                above = pltpu.roll(value[base + 64 : base + 96, lanes], 127, 1)
                me[(x + 2 - sx) * rows + y + j] += (
                    jnp.where(lane == 0, 0.0, below)
                    + value[base + 32 : base + 64, lanes]
                    + jnp.where(lane == 127, 0.0, above)
                )
        here = jnp.concatenate([hs[x * wide + y + j + 1] for j in range(4)], axis=1)
        g2[...] += lax.dot_general(here, columns(x3, wide, at, True, 32), NT, preferred_element_type=F32)
        return carry

    lax.fori_loop(0, depth * rows // 4, second, 0)


def final(bh, v3o, bp, w1v, vg, g1, b3):
    spread(bh, b3, True)
    own = [(x, y) for x in range(4) for y in range(2)]
    for half in range(2):
        lanes = pl.ds(512 * half, 512)
        vg[:, lanes] = jnp.dot(
            w1v[...], columns(b3, 4, own[4 * half : 4 * half + 4], True, 0), preferred_element_type=F32
        )
    grads = jnp.concatenate([bp[n] for n in range(8)], axis=1)
    for sx in range(3):
        for sy in range(3):
            field = jnp.concatenate([v3o[(x + sx) * 4 + y + sy] for x, y in own], axis=1)
            k = (sx * 3 + sy) * 192
            g1[k : k + 192] = lax.dot_general(field, grads, NT, preferred_element_type=F32)


def exchange_edges(bp, me, bh, mo, mr, b_s, b_r, m_s, m_r):
    ns, nf, nm, s, f, m = places()
    depth, rows = 4, 2 * nf
    down, up = lax.rem(s + ns - 1, ns), lax.rem(s + 1, ns)
    left, right = lax.rem(f + nf - 1, nf), lax.rem(f + 1, nf)
    targets = [
        {"filter": left}, {"filter": right}, {"spatial": down}, {"spatial": up},
        {"spatial": down, "filter": left}, {"spatial": down, "filter": right},
        {"spatial": up, "filter": left}, {"spatial": up, "filter": right},
    ]
    greet(targets)
    body = pl.ds(0, depth)
    inner = pl.ds(1, depth)
    two, pair = pl.ds(0, 2), pl.ds(1, 2)
    pieces = [
        (bp.at[body, 0], bh.at[inner, 3]),
        (bp.at[body, 1], bh.at[inner, 0]),
        (bp.at[0, two], bh.at[depth + 1, pair]),
        (bp.at[depth - 1, two], bh.at[0, pair]),
        (bp.at[0, 0], bh.at[depth + 1, 3]),
        (bp.at[0, 1], bh.at[depth + 1, 0]),
        (bp.at[depth - 1, 0], bh.at[0, 3]),
        (bp.at[depth - 1, 1], bh.at[0, 0]),
    ]
    copies = [
        remote(src, dst, b_s.at[i], b_r.at[i], target)
        for i, ((src, dst), target) in enumerate(zip(pieces, targets))
    ]
    copies += [
        remote(me.at[pl.ds(0, rows)], mr.at[1], m_s.at[0], m_r.at[0], {"spatial": down}),
        remote(me.at[pl.ds((depth + 1) * rows, rows)], mr.at[0], m_s.at[1], m_r.at[1], {"spatial": up}),
    ]
    for copy in copies:
        copy.start()
    bh[inner, pair] = bp[...]
    mo[...] = me[pl.ds(rows, depth * rows)]
    for copy in copies:
        copy.wait()

    @pl.when(s == 0)
    def _():
        bh[0] = jnp.zeros_like(bh[0])

    @pl.when(s == ns - 1)
    def _():
        bh[depth + 1] = jnp.zeros_like(bh[0])

    @pl.when(f == 0)
    def _():
        bh[:, 0] = jnp.zeros_like(bh[:, 0])

    @pl.when(f == nf - 1)
    def _():
        bh[:, 3] = jnp.zeros_like(bh[:, 0])

    @pl.when(s > 0)
    def _():
        mo[pl.ds(0, rows)] += mr[0]

    @pl.when(s < ns - 1)
    def _():
        mo[pl.ds((depth - 1) * rows, rows)] += mr[1]


def reduce_grads(split, g, out, ra, half, rb, total, rc, a_s, a_r, b_s, b_r, c_s, c_r, d_s, d_r, e_s, e_r):
    ns, nf, nm, s, f, m = places()
    nz = ns // 2
    core, z = lax.rem(s, 2), s // 2
    count = nz * nm
    partner = {"spatial": s + 1 - 2 * core}
    me = z * nm + m

    def peer(r):
        j = lax.rem(me + r, count)
        return j, {"spatial": (j // nm) * 2 + core, "sample": lax.rem(j, nm)}

    greet([partner] + [peer(r)[1] for r in range(1, count)] + [{"filter": lax.rem(f + r, nf)} for r in range(1, nf)])
    a = remote(g.at[1 - core], ra, a_s.at[0], a_r.at[0], partner)
    a.start()
    a.wait()
    half[...] = g[core] + ra[...]
    stage = []
    for r in range(1, count):
        j, target = peer(r)
        stage.append(remote(half.at[j], rb.at[r - 1], b_s.at[r - 1], b_r.at[r - 1], target))
    for copy in stage:
        copy.start()
    value = half[me]
    for r, copy in enumerate(stage):
        copy.wait()
        value = value + rb[r]
    total[...] = value
    first = pl.ds(0, split)
    rc[f] = total[first]
    stage = [
        remote(total.at[first], rc.at[f], c_s.at[r - 1], c_r.at[r - 1], {"filter": lax.rem(f + r, nf)})
        for r in range(1, nf)
    ]
    for copy in stage:
        copy.start()
    for copy in stage:
        copy.wait()
    value = rc[0]
    for k in range(1, nf):
        value = value + rc[k]
    out[core, me, first] = value.astype(BF)
    rest = pl.ds(split, total.shape[0] - split)
    out[core, me, rest] = total[rest].astype(BF)
    stage = []
    for r in range(1, count):
        j, target = peer(r)
        stage.append(remote(out.at[core, me], out.at[core, me], d_s.at[r - 1], d_r.at[r - 1], target))
    for copy in stage:
        copy.start()
    for copy in stage:
        copy.wait()
    e = remote(out.at[core], out.at[core], e_s.at[0], e_r.at[0], partner)
    e.start()
    e.wait()


def on_device(volume, weight_first, weight_second, cotangent):
    ns, nf, nm = lax.axis_size("spatial"), lax.axis_size("filter"), lax.axis_size("sample")
    depth, rows = 4, 2 * nf
    wide = rows + 2
    scaling = 1.0 / math.sqrt(nm * depth * ns * rows * 128)
    nz = ns // 2

    vt = volume[0].transpose(1, 2, 0, 3)
    ct = jnp.pad(cotangent[0].transpose(1, 2, 0, 3), ((0, 0), (1, 1), (0, 0), (0, 0)))
    wl = jnp.pad(weight_second.transpose(1, 0, 2).reshape(128, 864), ((0, 0), (0, 32)))
    wm = weight_second.reshape(3, 3, 3, 128, 32).transpose(0, 2, 4, 1, 3).reshape(288, 384)
    w1 = weight_first.reshape(1728, 128)
    w1v = weight_first.transpose(1, 0, 2).reshape(64, 3456)

    vs, cx, cg, wg = call(
        exchange_inputs,
        3,
        [
            ((depth + 2, wide, 64, 128), BF),
            ((depth + 2, wide, 32, 128), BF),
            ((nf, depth + 2, 4, 32, 128), BF),
            ((nf, 128, 896), BF),
        ],
        [
            dma(nf - 1), dma(nf - 1), dma(nf - 1), dma(nf - 1), dma(2), dma(2),
            dma(2 * nf - 2), dma(2 * nf - 2), dma(nf - 1), dma(nf - 1),
            dma(nz - 1), dma(nz - 1), dma(nz), dma(nz), dma(2), dma(2),
        ],
        0,
    )(vt, ct, wl)

    me, g2, bp, v3o = call(
        middle,
        6,
        [
            (((depth + 2) * rows, 32, 128), F32),
            ((128, 896), F32),
            ((8, 128, 128), BF),
            ((24, 192, 128), BF),
        ],
        [
            pltpu.VMEM(((depth + 2) * wide, 192, 128), BF),
            pltpu.VMEM((24, 96, 128), BF),
            pltpu.VMEM(((depth + 2) * wide, 96, 128), BF),
            pltpu.VMEM((depth * wide, 128, 128), BF),
            pltpu.VMEM((depth * rows, 128, 128), F32),
            pltpu.VMEM((128, 1024), F32),
            pltpu.VMEM((128, 1728), BF),
        ],
    )(
        vs.reshape(-1, 64, 128), cx.reshape(-1, 32, 128), cg.reshape(nf, 24, 32, 128), wg, w1, wm
    )

    bh, mo = call(
        exchange_edges,
        2,
        [((depth + 2, 4, 128, 128), BF), ((depth * rows, 32, 128), F32)],
        [pltpu.VMEM((2, rows, 32, 128), F32), dma(8), dma(8), dma(2), dma(2)],
        1,
    )(bp.reshape(depth, 2, 128, 128), me)

    vg, g1 = call(
        final,
        4,
        [((64, 1024), F32), ((1728, 128), F32)],
        [pltpu.VMEM((24, 384, 128), BF)],
    )(bh.reshape(24, 128, 128), v3o, bp, w1v)

    groups = 2 * nz * nm
    len1 = -(-1728 // (16 * groups)) * 16
    len2 = -(-1024 // (16 * groups)) * 16
    p1 = jnp.pad(g1, ((0, len1 * groups - 1728), (0, 0))).reshape(groups, len1, 128)
    p2 = g2.reshape(128, 7, 128).transpose(1, 0, 2).reshape(896, 128)
    p2 = jnp.pad(p2, ((0, len2 * groups - 896), (0, 0))).reshape(groups, len2, 128)
    length = len1 + len2
    parts = jnp.concatenate([p1, p2], axis=1).reshape(2, nz * nm, length, 128)
    (sums,) = call(
        functools.partial(reduce_grads, len1),
        1,
        [((2, nz * nm, length, 128), BF)],
        [
            pltpu.VMEM((nz * nm, length, 128), F32),
            pltpu.VMEM((nz * nm, length, 128), F32),
            pltpu.VMEM((nz * nm - 1, length, 128), F32),
            pltpu.VMEM((length, 128), F32),
            pltpu.VMEM((nf, len1, 128), F32),
            dma(1), dma(1), dma(nz * nm - 1), dma(nz * nm - 1), dma(nf - 1), dma(nf - 1),
            dma(nz * nm - 1), dma(nz * nm - 1), dma(1), dma(1),
        ],
        2,
    )(parts)
    sums = sums.reshape(groups, length, 128).astype(F32) * scaling
    first_grad = sums[:, :len1].reshape(-1, 128)[:1728].reshape(27, 64, 128)
    s2 = sums[:, len1:].reshape(-1, 128)[:896].reshape(7, 128, 128).transpose(1, 0, 2).reshape(128, 896)
    second_grad = s2[:, :864].reshape(128, 27, 32).transpose(1, 0, 2)
    mapped = mo.reshape(depth, rows, 32, 128).transpose(2, 0, 1, 3)[None]
    volume_grad = vg.reshape(1, 64, depth, 2, 128)
    return (mapped, second_grad, first_grad, volume_grad)


def solution(mesh):
    placed = (
        P("sample", None, "spatial", "filter", None),
        P(),
        P(None, None, "filter"),
        P("sample", "filter", "spatial", None, None),
    )
    return jax.shard_map(
        on_device,
        mesh=mesh,
        in_specs=placed,
        out_specs=(
            P("sample", "filter", "spatial", None, None),
            P(None, None, "filter"),
            P(),
            P("sample", None, "spatial", "filter", None),
        ),
        check_vma=False,
    )
```

```python
import functools
import math

import jax
import jax.numpy as jnp
from jax import lax
from jax.experimental import pallas as pl
from jax.experimental.pallas import tpu as pltpu
from jax.sharding import PartitionSpec as P

MESH = pl.DeviceIdType.MESH
BF = jnp.bfloat16
F32 = jnp.float32
VMEM = pl.BlockSpec(memory_space=pltpu.VMEM)
LIMIT = 56 * 1024 * 1024


def remote(src, dst, send, recv, device):
    return pltpu.make_async_remote_copy(
        src_ref=src, dst_ref=dst, send_sem=send, recv_sem=recv, device_id=device, device_id_type=MESH
    )


def greet(partners):
    barrier = pltpu.get_barrier_semaphore()
    for partner in partners:
        pl.semaphore_signal(barrier, inc=1, device_id=partner, device_id_type=MESH)
    pl.semaphore_wait(barrier, len(partners))


def places():
    ns, nf, nm = lax.axis_size("spatial"), lax.axis_size("filter"), lax.axis_size("sample")
    s, f, m = lax.axis_index("spatial"), lax.axis_index("filter"), lax.axis_index("sample")
    return ns, nf, nm, s, f, m


def call(kernel, count, outs, scratch, collective_id=None):
    params = dict(vmem_limit_bytes=LIMIT)
    if collective_id is not None:
        params.update(collective_id=collective_id, has_side_effects=True)
    return pl.pallas_call(
        kernel,
        out_shape=[jax.ShapeDtypeStruct(shape, dtype) for shape, dtype in outs],
        in_specs=[VMEM] * count,
        out_specs=[VMEM] * len(outs),
        scratch_shapes=scratch,
        compiler_params=pltpu.CompilerParams(**params),
    )


def dma(n):
    return pltpu.SemaphoreType.DMA((n,))


def exchange_inputs(
    vt, ct, wl, vs, cx, cg, wg,
    v_s, v_r, c_s, c_r, h_s, h_r, e_s, e_r, w_s, w_r, x_s, x_r, y_s, y_r, q_s, q_r,
):
    ns, nf, nm, s, f, m = places()
    depth = vt.shape[0]
    rows = 2 * nf
    part = wl.shape[0] // ns
    nz = ns // 2
    core, z = lax.rem(s, 2), s // 2
    prev, after = {"spatial": lax.rem(s + ns - 1, ns)}, {"spatial": lax.rem(s + 1, ns)}
    peers = [lax.rem(f + r, nf) for r in range(1, nf)]
    greet([{"filter": p} for p in peers] + [{"spatial": lax.rem(s + r, ns)} for r in range(1, ns)])

    halo = [
        remote(ct.at[0], cx.at[depth + 1], h_s.at[0], h_r.at[0], prev),
        remote(ct.at[depth - 1], cx.at[0], h_s.at[1], h_r.at[1], after),
    ]
    for copy in halo:
        copy.start()
    mine = pl.ds(s * part, part)
    weights = [
        remote(wl.at[mine], wg.at[f, mine], w_s.at[i], w_r.at[i], {"filter": p})
        for i, p in enumerate(peers)
    ]
    blocks = [
        remote(vt, vs.at[pl.ds(1, depth), pl.ds(1 + 2 * f, 2)], v_s.at[i], v_r.at[i], {"filter": p})
        for i, p in enumerate(peers)
    ]
    cots = [
        remote(
            ct.at[:, pl.ds(2 * p, 4)], cg.at[f, pl.ds(1, depth)], c_s.at[i], c_r.at[i], {"filter": p}
        )
        for i, p in enumerate(peers)
    ]
    for group in (weights, cots, blocks):
        for copy in group:
            copy.start()

    vs[:, 0] = jnp.zeros_like(vs[:, 0])
    vs[:, rows + 1] = jnp.zeros_like(vs[:, 0])
    vs[pl.ds(1, depth), pl.ds(1 + 2 * f, 2)] = vt[...]
    cx[pl.ds(1, depth)] = ct[...]
    cg[f, pl.ds(1, depth)] = ct[:, pl.ds(2 * f, 4)]
    wg[f, mine] = wl[mine]

    for copy in halo:
        copy.wait()

    @pl.when(s == 0)
    def _():
        cx[0] = jnp.zeros_like(cx[0])

    @pl.when(s == ns - 1)
    def _():
        cx[depth + 1] = jnp.zeros_like(cx[0])

    edges = []
    for i, p in enumerate(peers):
        for e, plane in enumerate((0, depth + 1)):
            n = 2 * i + e
            edges.append(
                remote(cx.at[plane, pl.ds(2 * p, 4)], cg.at[f, plane], e_s.at[n], e_r.at[n], {"filter": p})
            )
    for copy in edges:
        copy.start()
    for plane in (0, depth + 1):
        cg[f, plane] = cx[plane, pl.ds(2 * f, 4)]

    for copy in weights:
        copy.wait()
    along = []
    for r in range(1, nz):
        target = {"spatial": lax.rem(z + r, nz) * 2 + core}
        along.append(remote(wg.at[:, mine], wg.at[:, mine], x_s.at[r - 1], x_r.at[r - 1], target))
    for copy in along:
        copy.start()
    for copy in blocks:
        copy.wait()
    inner = pl.ds(1, rows)
    planes = [
        remote(vs.at[1, inner], vs.at[depth + 1, inner], q_s.at[0], q_r.at[0], prev),
        remote(vs.at[depth, inner], vs.at[0, inner], q_s.at[1], q_r.at[1], after),
    ]
    for copy in planes:
        copy.start()
    for copy in along:
        copy.wait()
    across = []
    for k in range(nz):
        piece = pl.ds((2 * k + core) * part, part)
        across.append(
            remote(wg.at[:, piece], wg.at[:, piece], y_s.at[k], y_r.at[k], {"spatial": s + 1 - 2 * core})
        )
    for copy in across:
        copy.start()
    for copy in planes:
        copy.wait()

    @pl.when(s == 0)
    def _():
        vs[0] = jnp.zeros_like(vs[0])

    @pl.when(s == ns - 1)
    def _():
        vs[depth + 1] = jnp.zeros_like(vs[0])

    for group in (cots, edges, across):
        for copy in group:
            copy.wait()


def shifted(cells):
    wide = cells.astype(F32)
    lane = lax.broadcasted_iota(jnp.int32, wide.shape, 1)
    below = jnp.where(lane == 0, 0.0, pltpu.roll(wide, 1, 1)).astype(BF)
    above = jnp.where(lane == 127, 0.0, pltpu.roll(wide, 127, 1)).astype(BF)
    return below, cells, above


def spread(src, dst, flip):
    count, channels, _ = src.shape
    step = 6 if count % 6 == 0 else 4

    def body(i, carry):
        for u in range(step):
            below, here, above = shifted(src[i * step + u])
            first, last = (above, below) if flip else (below, above)
            dst[i * step + u, pl.ds(0, channels)] = first
            dst[i * step + u, pl.ds(channels, channels)] = here
            dst[i * step + u, pl.ds(2 * channels, channels)] = last
        return carry

    lax.fori_loop(0, count // step, body, 0)


def columns(ref, wide, rows_at, flip, pad):
    stack = []
    for sx in range(3):
        for sy in range(3):
            ox, oy = (2 - sx, 2 - sy) if flip else (sx, sy)
            stack.append(jnp.concatenate([ref[(x + ox) * wide + (y + oy)] for x, y in rows_at], axis=1))
    if pad:
        stack.append(jnp.zeros((pad, 128 * len(rows_at)), BF))
    return jnp.concatenate(stack, axis=0)


NT = (((1,), (1,)), ((), ()))


def middle(vs, cx, cg, wg, w1, wm, me, g2, bp, v3o, v3, c3, x3, hs, pre, acc, w1t):
    ns, nf, nm, s, f, m = places()
    depth, rows = 4, 2 * nf
    wide = rows + 2
    w1t[...] = w1[...].T
    spread(vs, v3, False)

    hs[...] = jnp.zeros_like(hs)

    group = min(8, rows)

    def first(i, carry):
        x, y = i // (rows // group), lax.rem(i, rows // group) * group
        value = jnp.dot(
            w1t[...], columns(v3, wide, [(x, y + j) for j in range(group)], False, 0),
            preferred_element_type=F32,
        )
        hidden = (value * jax.nn.sigmoid(value)).astype(BF)
        for j in range(group):
            pre[x * rows + y + j] = value[:, 128 * j : 128 * (j + 1)]
            hs[x * wide + y + 1 + j] = hidden[:, 128 * j : 128 * (j + 1)]
        return carry

    lax.fori_loop(0, depth * rows // group, first, 0)

    acc[...] = jnp.zeros_like(acc)
    own = [(x, y) for x in range(depth) for y in range(2)]

    def back(k, carry):
        spread(cg.at[k], c3, True)
        for half in range(2):
            lanes = pl.ds(512 * half, 512)
            acc[:, lanes] += jnp.dot(
                wg[k], columns(c3, 4, own[4 * half : 4 * half + 4], True, 32), preferred_element_type=F32
            )
        return carry

    lax.fori_loop(0, nf, back, 0)
    for n, (x, y) in enumerate(own):
        u = pre[x * rows + 2 * f + y]
        sig = jax.nn.sigmoid(u)
        bp[n] = (acc[:, 128 * n : 128 * (n + 1)] * (sig * (1.0 + u * (1.0 - sig)))).astype(BF)
    for x in range(depth + 2):
        for y in range(4):
            v3o[x * 4 + y] = v3[x * wide + 2 * f + y]

    spread(cx, x3, True)
    me[...] = jnp.zeros_like(me)
    g2[...] = jnp.zeros_like(g2)

    def second(i, carry):
        x, y = i // (rows // 4), lax.rem(i, rows // 4) * 4
        at = [(x, y + j) for j in range(4)]
        field = jnp.concatenate(
            [
                jnp.concatenate([hs[x * wide + y + j + sy] for j in range(4)], axis=1)
                for sy in range(3)
            ],
            axis=0,
        )
        value = jnp.dot(wm[...], field, preferred_element_type=F32)
        lane = lax.broadcasted_iota(jnp.int32, (32, 128), 1)
        for sx in range(3):
            for j in range(4):
                lanes = slice(128 * j, 128 * (j + 1))
                base = 96 * sx
                below = pltpu.roll(value[base : base + 32, lanes], 1, 1)
                above = pltpu.roll(value[base + 64 : base + 96, lanes], 127, 1)
                me[(x + 2 - sx) * rows + y + j] += (
                    jnp.where(lane == 0, 0.0, below)
                    + value[base + 32 : base + 64, lanes]
                    + jnp.where(lane == 127, 0.0, above)
                )
        here = jnp.concatenate([hs[x * wide + y + j + 1] for j in range(4)], axis=1)
        g2[...] += lax.dot_general(here, columns(x3, wide, at, True, 32), NT, preferred_element_type=F32)
        return carry

    lax.fori_loop(0, depth * rows // 4, second, 0)


def final(bh, v3o, bp, w1v, vg, g1, b3):
    spread(bh, b3, True)
    own = [(x, y) for x in range(4) for y in range(2)]
    for half in range(2):
        lanes = pl.ds(512 * half, 512)
        vg[:, lanes] = jnp.dot(
            w1v[...], columns(b3, 4, own[4 * half : 4 * half + 4], True, 0), preferred_element_type=F32
        )
    grads = jnp.concatenate([bp[n] for n in range(8)], axis=1)
    for sx in range(3):
        for sy in range(3):
            field = jnp.concatenate([v3o[(x + sx) * 4 + y + sy] for x, y in own], axis=1)
            k = (sx * 3 + sy) * 192
            g1[k : k + 192] = lax.dot_general(field, grads, NT, preferred_element_type=F32)


def exchange_edges(bp, me, bh, mo, mr, b_s, b_r, m_s, m_r):
    ns, nf, nm, s, f, m = places()
    depth, rows = 4, 2 * nf
    down, up = lax.rem(s + ns - 1, ns), lax.rem(s + 1, ns)
    left, right = lax.rem(f + nf - 1, nf), lax.rem(f + 1, nf)
    targets = [
        {"filter": left}, {"filter": right}, {"spatial": down}, {"spatial": up},
        {"spatial": down, "filter": left}, {"spatial": down, "filter": right},
        {"spatial": up, "filter": left}, {"spatial": up, "filter": right},
    ]
    greet(targets)
    body = pl.ds(0, depth)
    inner = pl.ds(1, depth)
    two, pair = pl.ds(0, 2), pl.ds(1, 2)
    pieces = [
        (bp.at[body, 0], bh.at[inner, 3]),
        (bp.at[body, 1], bh.at[inner, 0]),
        (bp.at[0, two], bh.at[depth + 1, pair]),
        (bp.at[depth - 1, two], bh.at[0, pair]),
        (bp.at[0, 0], bh.at[depth + 1, 3]),
        (bp.at[0, 1], bh.at[depth + 1, 0]),
        (bp.at[depth - 1, 0], bh.at[0, 3]),
        (bp.at[depth - 1, 1], bh.at[0, 0]),
    ]
    copies = [
        remote(src, dst, b_s.at[i], b_r.at[i], target)
        for i, ((src, dst), target) in enumerate(zip(pieces, targets))
    ]
    copies += [
        remote(me.at[pl.ds(0, rows)], mr.at[1], m_s.at[0], m_r.at[0], {"spatial": down}),
        remote(me.at[pl.ds((depth + 1) * rows, rows)], mr.at[0], m_s.at[1], m_r.at[1], {"spatial": up}),
    ]
    for copy in copies:
        copy.start()
    bh[inner, pair] = bp[...]
    mo[...] = me[pl.ds(rows, depth * rows)]
    for copy in copies:
        copy.wait()

    @pl.when(s == 0)
    def _():
        bh[0] = jnp.zeros_like(bh[0])

    @pl.when(s == ns - 1)
    def _():
        bh[depth + 1] = jnp.zeros_like(bh[0])

    @pl.when(f == 0)
    def _():
        bh[:, 0] = jnp.zeros_like(bh[:, 0])

    @pl.when(f == nf - 1)
    def _():
        bh[:, 3] = jnp.zeros_like(bh[:, 0])

    @pl.when(s > 0)
    def _():
        mo[pl.ds(0, rows)] += mr[0]

    @pl.when(s < ns - 1)
    def _():
        mo[pl.ds((depth - 1) * rows, rows)] += mr[1]


def reduce_grads(split, g, out, ra, half, rb, total, rc, a_s, a_r, b_s, b_r, c_s, c_r, d_s, d_r, e_s, e_r):
    ns, nf, nm, s, f, m = places()
    nz = ns // 2
    core, z = lax.rem(s, 2), s // 2
    count = nz * nm
    partner = {"spatial": s + 1 - 2 * core}
    me = z * nm + m

    def peer(r):
        j = lax.rem(me + r, count)
        return j, {"spatial": (j // nm) * 2 + core, "sample": lax.rem(j, nm)}

    greet([partner] + [peer(r)[1] for r in range(1, count)] + [{"filter": lax.rem(f + r, nf)} for r in range(1, nf)])
    a = remote(g.at[1 - core], ra, a_s.at[0], a_r.at[0], partner)
    a.start()
    a.wait()
    half[...] = g[core] + ra[...]
    stage = []
    for r in range(1, count):
        j, target = peer(r)
        stage.append(remote(half.at[j], rb.at[r - 1], b_s.at[r - 1], b_r.at[r - 1], target))
    for copy in stage:
        copy.start()
    value = half[me]
    for r, copy in enumerate(stage):
        copy.wait()
        value = value + rb[r]
    total[...] = value
    first = pl.ds(0, split)
    rc[f] = total[first]
    stage = [
        remote(total.at[first], rc.at[f], c_s.at[r - 1], c_r.at[r - 1], {"filter": lax.rem(f + r, nf)})
        for r in range(1, nf)
    ]
    for copy in stage:
        copy.start()
    for copy in stage:
        copy.wait()
    value = rc[0]
    for k in range(1, nf):
        value = value + rc[k]
    out[core, me, first] = value.astype(BF)
    rest = pl.ds(split, total.shape[0] - split)
    out[core, me, rest] = total[rest].astype(BF)
    stage = []
    for r in range(1, count):
        j, target = peer(r)
        stage.append(remote(out.at[core, me], out.at[core, me], d_s.at[r - 1], d_r.at[r - 1], target))
    for copy in stage:
        copy.start()
    for copy in stage:
        copy.wait()
    e = remote(out.at[core], out.at[core], e_s.at[0], e_r.at[0], partner)
    e.start()
    e.wait()


def on_device(volume, weight_first, weight_second, cotangent):
    ns, nf, nm = lax.axis_size("spatial"), lax.axis_size("filter"), lax.axis_size("sample")
    depth, rows = 4, 2 * nf
    wide = rows + 2
    scaling = 1.0 / math.sqrt(nm * depth * ns * rows * 128)
    nz = ns // 2

    vt = volume[0].transpose(1, 2, 0, 3)
    ct = jnp.pad(cotangent[0].transpose(1, 2, 0, 3), ((0, 0), (1, 1), (0, 0), (0, 0)))
    wl = jnp.pad(weight_second.transpose(1, 0, 2).reshape(128, 864), ((0, 0), (0, 32)))
    wm = weight_second.reshape(3, 3, 3, 128, 32).transpose(0, 2, 4, 1, 3).reshape(288, 384)
    w1 = weight_first.reshape(1728, 128)
    w1v = weight_first.transpose(1, 0, 2).reshape(64, 3456)

    vs, cx, cg, wg = call(
        exchange_inputs,
        3,
        [
            ((depth + 2, wide, 64, 128), BF),
            ((depth + 2, wide, 32, 128), BF),
            ((nf, depth + 2, 4, 32, 128), BF),
            ((nf, 128, 896), BF),
        ],
        [
            dma(nf - 1), dma(nf - 1), dma(nf - 1), dma(nf - 1), dma(2), dma(2),
            dma(2 * nf - 2), dma(2 * nf - 2), dma(nf - 1), dma(nf - 1),
            dma(nz - 1), dma(nz - 1), dma(nz), dma(nz), dma(2), dma(2),
        ],
        0,
    )(vt, ct, wl)

    me, g2, bp, v3o = call(
        middle,
        6,
        [
            (((depth + 2) * rows, 32, 128), F32),
            ((128, 896), F32),
            ((8, 128, 128), BF),
            ((24, 192, 128), BF),
        ],
        [
            pltpu.VMEM(((depth + 2) * wide, 192, 128), BF),
            pltpu.VMEM((24, 96, 128), BF),
            pltpu.VMEM(((depth + 2) * wide, 96, 128), BF),
            pltpu.VMEM((depth * wide, 128, 128), BF),
            pltpu.VMEM((depth * rows, 128, 128), F32),
            pltpu.VMEM((128, 1024), F32),
            pltpu.VMEM((128, 1728), BF),
        ],
    )(
        vs.reshape(-1, 64, 128), cx.reshape(-1, 32, 128), cg.reshape(nf, 24, 32, 128), wg, w1, wm
    )

    bh, mo = call(
        exchange_edges,
        2,
        [((depth + 2, 4, 128, 128), BF), ((depth * rows, 32, 128), F32)],
        [pltpu.VMEM((2, rows, 32, 128), F32), dma(8), dma(8), dma(2), dma(2)],
        1,
    )(bp.reshape(depth, 2, 128, 128), me)

    vg, g1 = call(
        final,
        4,
        [((64, 1024), F32), ((1728, 128), F32)],
        [pltpu.VMEM((24, 384, 128), BF)],
    )(bh.reshape(24, 128, 128), v3o, bp, w1v)

    groups = 2 * nz * nm
    len1 = -(-1728 // (16 * groups)) * 16
    len2 = -(-1024 // (16 * groups)) * 16
    p1 = jnp.pad(g1, ((0, len1 * groups - 1728), (0, 0))).reshape(groups, len1, 128)
    p2 = g2.reshape(128, 7, 128).transpose(1, 0, 2).reshape(896, 128)
    p2 = jnp.pad(p2, ((0, len2 * groups - 896), (0, 0))).reshape(groups, len2, 128)
    length = len1 + len2
    parts = jnp.concatenate([p1, p2], axis=1).reshape(2, nz * nm, length, 128)
    (sums,) = call(
        functools.partial(reduce_grads, len1),
        1,
        [((2, nz * nm, length, 128), BF)],
        [
            pltpu.VMEM((nz * nm, length, 128), F32),
            pltpu.VMEM((nz * nm, length, 128), F32),
            pltpu.VMEM((nz * nm - 1, length, 128), F32),
            pltpu.VMEM((length, 128), F32),
            pltpu.VMEM((nf, len1, 128), F32),
            dma(1), dma(1), dma(nz * nm - 1), dma(nz * nm - 1), dma(nf - 1), dma(nf - 1),
            dma(nz * nm - 1), dma(nz * nm - 1), dma(1), dma(1),
        ],
        2,
    )(parts)
    sums = sums.reshape(groups, length, 128).astype(F32) * scaling
    first_grad = sums[:, :len1].reshape(-1, 128)[:1728].reshape(27, 64, 128)
    s2 = sums[:, len1:].reshape(-1, 128)[:896].reshape(7, 128, 128).transpose(1, 0, 2).reshape(128, 896)
    second_grad = s2[:, :864].reshape(128, 27, 32).transpose(1, 0, 2)
    mapped = mo.reshape(depth, rows, 32, 128).transpose(2, 0, 1, 3)[None]
    volume_grad = vg.reshape(1, 64, depth, 2, 128)
    return (mapped, second_grad, first_grad, volume_grad)


def solution(mesh):
    placed = (
        P("sample", None, "spatial", "filter", None),
        P(),
        P(None, None, "filter"),
        P("sample", "filter", "spatial", None, None),
    )
    return jax.shard_map(
        on_device,
        mesh=mesh,
        in_specs=placed,
        out_specs=(
            P("sample", "filter", "spatial", None, None),
            P(None, None, "filter"),
            P(),
            P("sample", None, "spatial", "filter", None),
        ),
        check_vma=False,
    )
```

```python
import functools
import math

import jax
import jax.numpy as jnp
from jax import lax
from jax.experimental import pallas as pl
from jax.experimental.pallas import tpu as pltpu
from jax.sharding import PartitionSpec as P

MESH = pl.DeviceIdType.MESH
BF = jnp.bfloat16
F32 = jnp.float32
VMEM = pl.BlockSpec(memory_space=pltpu.VMEM)
LIMIT = 56 * 1024 * 1024


def remote(src, dst, send, recv, device):
    return pltpu.make_async_remote_copy(
        src_ref=src, dst_ref=dst, send_sem=send, recv_sem=recv, device_id=device, device_id_type=MESH
    )


def greet(partners):
    barrier = pltpu.get_barrier_semaphore()
    for partner in partners:
        pl.semaphore_signal(barrier, inc=1, device_id=partner, device_id_type=MESH)
    pl.semaphore_wait(barrier, len(partners))


def places():
    ns, nf, nm = lax.axis_size("spatial"), lax.axis_size("filter"), lax.axis_size("sample")
    s, f, m = lax.axis_index("spatial"), lax.axis_index("filter"), lax.axis_index("sample")
    return ns, nf, nm, s, f, m


def dma(n):
    return pltpu.SemaphoreType.DMA((n,))


def shifted(cells):
    wide = cells.astype(F32)
    lane = lax.broadcasted_iota(jnp.int32, wide.shape, 1)
    below = jnp.where(lane == 0, 0.0, pltpu.roll(wide, 1, 1)).astype(BF)
    above = jnp.where(lane == 127, 0.0, pltpu.roll(wide, 127, 1)).astype(BF)
    return below, cells, above


def spread(src, dst, flip):
    count, channels, _ = src.shape
    step = 6 if count % 6 == 0 else 4

    def body(i, carry):
        for u in range(step):
            below, here, above = shifted(src[i * step + u])
            first, last = (above, below) if flip else (below, above)
            dst[i * step + u, pl.ds(0, channels)] = first
            dst[i * step + u, pl.ds(channels, channels)] = here
            dst[i * step + u, pl.ds(2 * channels, channels)] = last
        return carry

    lax.fori_loop(0, count // step, body, 0)


def columns(ref, wide, rows_at, flip, pad):
    stack = []
    for sx in range(3):
        for sy in range(3):
            ox, oy = (2 - sx, 2 - sy) if flip else (sx, sy)
            stack.append(jnp.concatenate([ref[(x + ox) * wide + (y + oy)] for x, y in rows_at], axis=1))
    if pad:
        stack.append(jnp.zeros((pad, 128 * len(rows_at)), BF))
    return jnp.concatenate(stack, axis=0)


NT = (((1,), (1,)), ((), ()))


class Links:
    def __init__(self, send, recv):
        self.send, self.recv, self.used = send, recv, 0

    def __call__(self, src, dst, device):
        n = self.used
        self.used += 1
        return remote(src, dst, self.send.at[n], self.recv.at[n], device)


def start(copies):
    for copy in copies:
        copy.start()


def wait(copies):
    for copy in copies:
        copy.wait()


def zero(ref):
    ref[...] = jnp.zeros(ref.shape, ref.dtype)


class Summed:
    def __init__(self, links, at, rows, whole, from_core, half, from_peers, total, from_filter, held):
        self.links, self.at, self.rows = links, at, rows
        self.whole, self.from_core, self.half, self.from_peers = whole, from_core, half, from_peers
        self.total, self.from_filter, self.held = total, from_filter, held

    def core(self):
        ns, nf, nm, s, f, m = self.at
        span = self.half.shape[0]
        core = lax.rem(s, 2)
        partner = {"spatial": s + 1 - 2 * core}
        self.moving = [self.links(self.whole.at[pl.ds((1 - core) * span, span)], self.from_core, partner)]
        start(self.moving)

    def peers(self):
        ns, nf, nm, s, f, m = self.at
        span, rows = self.half.shape[0], self.rows
        core, count = lax.rem(s, 2), span // rows
        me = (s // 2) * nm + m
        wait(self.moving)
        self.half[...] = self.whole[pl.ds(core * span, span)] + self.from_core[...]
        self.targets = []
        self.moving = []
        for r in range(1, count):
            j = lax.rem(me + r, count)
            device = {"spatial": (j // nm) * 2 + core, "sample": lax.rem(j, nm)}
            self.targets.append(device)
            self.moving.append(self.links(self.half.at[pl.ds(j * rows, rows)], self.from_peers.at[r - 1], device))
        start(self.moving)

    def gather_sum(self):
        ns, nf, nm, s, f, m = self.at
        wait(self.moving)
        value = self.half[pl.ds(((s // 2) * nm + m) * self.rows, self.rows)]
        for r in range(len(self.moving)):
            value = value + self.from_peers[r]
        return value

    def filters(self):
        ns, nf, nm, s, f, m = self.at
        value = self.gather_sum()
        self.total[...] = value
        self.from_filter[f] = value
        self.moving = [
            self.links(self.total, self.from_filter.at[f], {"filter": lax.rem(f + r, nf)}) for r in range(1, nf)
        ]
        start(self.moving)

    def back(self):
        ns, nf, nm, s, f, m = self.at
        if self.from_filter is None:
            value = self.gather_sum()
        else:
            wait(self.moving)
            value = self.from_filter[0]
            for k in range(1, nf):
                value = value + self.from_filter[k]
        span, rows = self.half.shape[0], self.rows
        self.base = pl.ds(lax.rem(s, 2) * span, span)
        mine = pl.ds(lax.rem(s, 2) * span + ((s // 2) * nm + m) * rows, rows)
        self.held[mine] = value.astype(BF)
        self.moving = [self.links(self.held.at[mine], self.held.at[mine], device) for device in self.targets]
        start(self.moving)

    def across(self):
        s = self.at[3]
        wait(self.moving)
        self.moving = [
            self.links(self.held.at[self.base], self.held.at[self.base], {"spatial": s + 1 - 2 * lax.rem(s, 2)})
        ]
        start(self.moving)

    def finish(self):
        wait(self.moving)


DEPTH = 4
OWN = [(x, y) for x in range(DEPTH) for y in range(2)]


def whole_step(
    scaling, vt, ct, wl, w1, mo, g2o, g1o, vg,
    vs, cx, cg, wg, v3, c3, x3, hs, pre, acc, w1t, w1v, wm, me, mr, bp, bh, b3, v3o, g2a,
    g1w, g1c, g1h, g1p, g1t, g1f, g1b, g2w, g2c, g2h, g2p, g2b, send, recv,
):
    at = ns, nf, nm, s, f, m = places()
    links = Links(send, recv)
    depth, rows = DEPTH, 2 * nf
    wide = rows + 2
    part = wl.shape[0] // ns
    nz = ns // 2
    core, z = lax.rem(s, 2), s // 2
    down, up = lax.rem(s + ns - 1, ns), lax.rem(s + 1, ns)
    left, right = lax.rem(f + nf - 1, nf), lax.rem(f + 1, nf)
    prev, after = {"spatial": down}, {"spatial": up}
    peers = [lax.rem(f + r, nf) for r in range(1, nf)]
    edges = [
        {"filter": left}, {"filter": right}, prev, after,
        {"spatial": down, "filter": left}, {"spatial": down, "filter": right},
        {"spatial": up, "filter": left}, {"spatial": up, "filter": right},
    ]
    group = []
    for r in range(1, nz * nm):
        j = lax.rem(z * nm + m + r, nz * nm)
        group.append({"spatial": (j // nm) * 2 + core, "sample": lax.rem(j, nm)})
    greet([{"filter": p} for p in peers] + edges[2:] + group)

    inner, body, two, pair = pl.ds(1, depth), pl.ds(0, depth), pl.ds(0, 2), pl.ds(1, 2)
    block = pl.ds(1 + 2 * f, 2)
    blocks = [links(vt, vs.at[inner, block], {"filter": p}) for p in peers]
    mine = pl.ds(s * part, part)
    halo = [links(ct.at[0], cx.at[depth + 1], prev), links(ct.at[depth - 1], cx.at[0], after)]
    weights = [links(wl.at[mine], wg.at[f, mine], {"filter": p}) for p in peers]
    cots = [links(ct.at[:, pl.ds(2 * p, 4)], cg.at[f, inner], {"filter": p}) for p in peers]
    for copies in (blocks, weights, halo, cots):
        start(copies)

    vs[:, 0] = jnp.zeros_like(vs[:, 0])
    vs[:, rows + 1] = jnp.zeros_like(vs[:, 0])
    vs[inner, block] = vt[...]
    cx[inner] = ct[...]
    cg[f, inner] = ct[:, pl.ds(2 * f, 4)]
    wg[f, mine] = wl[mine]
    w1t[...] = w1[...].T
    wlt = wl[...].T
    for sx in range(3):
        for sy in range(3):
            for sz in range(3):
                k = sx * 9 + sy * 3 + sz
                w1v[:, 128 * k : 128 * (k + 1)] = w1[64 * k : 64 * (k + 1)]
                j = 32 * (sx * 3 + sz)
                wm[j : j + 32, 128 * sy : 128 * (sy + 1)] = wlt[32 * k : 32 * (k + 1)]
    zero(hs)
    zero(me)
    zero(acc)
    zero(g2a)

    wait(halo)

    @pl.when(s == 0)
    def _():
        cx[0] = jnp.zeros_like(cx[0])

    @pl.when(s == ns - 1)
    def _():
        cx[depth + 1] = jnp.zeros_like(cx[0])

    cxr = cx.reshape((depth + 2) * wide, 32, 128)
    spread(cxr, x3, True)
    for plane in (0, depth + 1):
        cg[f, plane] = cx[plane, pl.ds(2 * f, 4)]

    wait(weights)
    along = [
        links(wg.at[:, mine], wg.at[:, mine], {"spatial": lax.rem(z + r, nz) * 2 + core}) for r in range(1, nz)
    ]
    start(along)

    wait(blocks)
    row = pl.ds(1, rows)
    planes = [links(vs.at[1, row], vs.at[depth + 1, row], prev), links(vs.at[depth, row], vs.at[0, row], after)]
    start(planes)
    vsr = vs.reshape((depth + 2) * wide, 64, 128)
    spread(vsr.at[pl.ds(wide, depth * wide)], v3.at[pl.ds(wide, depth * wide)], False)
    lot = min(8, rows)
    times = rows // lot

    def first(i, carry):
        x, y = i // times, lax.rem(i, times) * lot
        value = jnp.dot(
            w1t[...], columns(v3, wide, [(x, y + j) for j in range(lot)], False, 0), preferred_element_type=F32
        )
        hidden = (value * jax.nn.sigmoid(value)).astype(BF)
        for j in range(lot):
            pre[x * rows + y + j] = value[:, 128 * j : 128 * (j + 1)]
            hs[x * wide + y + 1 + j] = hidden[:, 128 * j : 128 * (j + 1)]
        return carry

    lax.fori_loop(times, 3 * times, first, 0)
    wait(along)
    across = []
    for k in range(nz):
        piece = pl.ds((2 * k + core) * part, part)
        across.append(links(wg.at[:, piece], wg.at[:, piece], {"spatial": s + 1 - 2 * core}))
    start(across)
    wait(planes)

    @pl.when(s == 0)
    def _():
        vs[0] = jnp.zeros_like(vs[0])

    @pl.when(s == ns - 1)
    def _():
        vs[depth + 1] = jnp.zeros_like(vs[0])

    for plane in (0, depth + 1):
        span = pl.ds(plane * wide, wide)
        spread(vsr.at[span], v3.at[span], False)
    lax.fori_loop(0, times, first, 0)
    lax.fori_loop(3 * times, 4 * times, first, 0)

    forward = []
    for r, copy in enumerate(cots):
        copy.wait()
        k = lax.rem(f + nf - 1 - r, nf)
        pieces = [links(cg.at[k, 1], cg.at[k, depth + 1], prev), links(cg.at[k, depth], cg.at[k, 0], after)]
        start(pieces)
        forward += pieces

    def second_weights(i, carry):
        x, y = i // times, lax.rem(i, times) * lot
        here = jnp.concatenate([hs[x * wide + y + j + 1] for j in range(lot)], axis=1)
        field = columns(x3, wide, [(x, y + j) for j in range(lot)], True, 32)
        g2a[...] += lax.dot_general(here, field, NT, preferred_element_type=F32)
        return carry

    lax.fori_loop(0, 2 * times, second_weights, 0)
    wait(across)
    wait(forward)

    @pl.when(s == 0)
    def _():
        cg[:, 0] = jnp.zeros_like(cg[:, 0])

    @pl.when(s == ns - 1)
    def _():
        cg[:, depth + 1] = jnp.zeros_like(cg[:, 0])

    cgr = cg.reshape(nf, (depth + 2) * 4, 32, 128)

    def back(k, carry):
        spread(cgr.at[k], c3, True)
        for part_at in range(2):
            lanes = pl.ds(512 * part_at, 512)
            acc[:, lanes] += jnp.dot(
                wg[k], columns(c3, 4, OWN[4 * part_at : 4 * part_at + 4], True, 32), preferred_element_type=F32
            )
        return carry

    lax.fori_loop(0, nf, back, 0)
    for n, (x, y) in enumerate(OWN):
        u = pre[x * rows + 2 * f + y]
        sig = jax.nn.sigmoid(u)
        bp[x, y] = (acc[:, 128 * n : 128 * (n + 1)] * (sig * (1.0 + u * (1.0 - sig)))).astype(BF)
    pieces = [
        (bp.at[body, 0], bh.at[inner, 3]), (bp.at[body, 1], bh.at[inner, 0]),
        (bp.at[0, two], bh.at[depth + 1, pair]), (bp.at[depth - 1, two], bh.at[0, pair]),
        (bp.at[0, 0], bh.at[depth + 1, 3]), (bp.at[0, 1], bh.at[depth + 1, 0]),
        (bp.at[depth - 1, 0], bh.at[0, 3]), (bp.at[depth - 1, 1], bh.at[0, 0]),
    ]
    cells = [links(src, dst, device) for (src, dst), device in zip(pieces, edges)]
    start(cells)
    bh[inner, pair] = bp[...]

    for x in range(depth + 2):
        for y in range(4):
            v3o[x * 4 + y] = v3[x * wide + 2 * f + y]
    grads = jnp.concatenate([bp[x, y] for x, y in OWN], axis=1)
    for j in range(9):
        sx, sy = j // 3, j % 3
        field = jnp.concatenate([v3o[(x + sx) * 4 + y + sy] for x, y in OWN], axis=1)
        g1w[192 * j : 192 * (j + 1)] = lax.dot_general(field, grads, NT, preferred_element_type=F32)
    g1w[1728:] = jnp.zeros((g1w.shape[0] - 1728, 128), F32)
    one = Summed(links, at, g1t.shape[0], g1w, g1c, g1h, g1p, g1t, g1f, g1b)
    one.core()

    lax.fori_loop(2 * times, 3 * times, second_weights, 0)
    one.peers()
    lax.fori_loop(3 * times, 4 * times, second_weights, 0)
    for t in range(7):
        g2w[128 * t : 128 * (t + 1)] = g2a[:, 128 * t : 128 * (t + 1)]
    g2w[896:] = jnp.zeros((g2w.shape[0] - 896, 128), F32)
    other = Summed(links, at, g2p.shape[1], g2w, g2c, g2h, g2p, None, None, g2b)
    other.core()

    def second(i, carry):
        x, y = i // (rows // 4), lax.rem(i, rows // 4) * 4
        field = jnp.concatenate(
            [jnp.concatenate([hs[x * wide + y + j + sy] for j in range(4)], axis=1) for sy in range(3)],
            axis=0,
        )
        value = jnp.dot(wm[...], field, preferred_element_type=F32)
        lane = lax.broadcasted_iota(jnp.int32, (32, 128), 1)
        for sx in range(3):
            for j in range(4):
                lanes = slice(128 * j, 128 * (j + 1))
                base = 96 * sx
                below = pltpu.roll(value[base : base + 32, lanes], 1, 1)
                above = pltpu.roll(value[base + 64 : base + 96, lanes], 127, 1)
                me[(x + 2 - sx) * rows + y + j] += (
                    jnp.where(lane == 0, 0.0, below)
                    + value[base + 32 : base + 64, lanes]
                    + jnp.where(lane == 127, 0.0, above)
                )
        return carry

    turn = rows // 4
    lax.fori_loop(0, turn, second, 0)
    one.filters()
    other.peers()
    lax.fori_loop(turn, 2 * turn, second, 0)
    lax.fori_loop(2 * turn, 3 * turn, second, 0)
    one.back()
    other.back()
    lax.fori_loop(3 * turn, 4 * turn, second, 0)
    outer = [
        links(me.at[pl.ds(0, rows)], mr.at[1], prev),
        links(me.at[pl.ds((depth + 1) * rows, rows)], mr.at[0], after),
    ]
    start(outer)

    wait(cells)

    @pl.when(s == 0)
    def _():
        bh[0] = jnp.zeros_like(bh[0])

    @pl.when(s == ns - 1)
    def _():
        bh[depth + 1] = jnp.zeros_like(bh[0])

    @pl.when(f == 0)
    def _():
        bh[:, 0] = jnp.zeros_like(bh[:, 0])

    @pl.when(f == nf - 1)
    def _():
        bh[:, 3] = jnp.zeros_like(bh[:, 0])

    one.across()
    other.across()
    spread(bh.reshape((depth + 2) * 4, 128, 128), b3, True)
    for part_at in range(2):
        lanes = pl.ds(512 * part_at, 512)
        vg[:, lanes] = jnp.dot(
            w1v[...], columns(b3, 4, OWN[4 * part_at : 4 * part_at + 4], True, 0), preferred_element_type=F32
        )

    mo[...] = me[pl.ds(rows, depth * rows)]
    wait(outer)

    @pl.when(s > 0)
    def _():
        mo[pl.ds(0, rows)] += mr[0]

    @pl.when(s < ns - 1)
    def _():
        mo[pl.ds((depth - 1) * rows, rows)] += mr[1]

    one.finish()
    other.finish()
    g1o[...] = g1b[0:1728].astype(F32) * scaling
    for k in range(27):
        tile = g2b[128 * (k // 4) : 128 * (k // 4 + 1)].astype(F32) * scaling
        g2o[k] = tile[:, 32 * (k % 4) : 32 * (k % 4 + 1)]


def on_device(volume, weight_first, weight_second, cotangent):
    ns, nf, nm = lax.axis_size("spatial"), lax.axis_size("filter"), lax.axis_size("sample")
    depth, rows = DEPTH, 2 * nf
    wide = rows + 2
    scaling = 1.0 / math.sqrt(nm * depth * ns * rows * 128)
    count = ns // 2 * nm

    vt = volume[0].transpose(1, 2, 0, 3)
    ct = jnp.pad(cotangent[0].transpose(1, 2, 0, 3), ((0, 0), (1, 1), (0, 0), (0, 0)))
    wl = jnp.pad(weight_second.transpose(1, 0, 2).reshape(128, 864), ((0, 0), (0, 32)))
    w1 = weight_first.reshape(1728, 128)

    len1 = -(-1728 // (32 * count)) * 16
    len2 = -(-1024 // (32 * count)) * 16
    slab = (depth + 2) * wide
    scratch = [
        ((depth + 2, wide, 64, 128), BF), ((depth + 2, wide, 32, 128), BF),
        ((nf, depth + 2, 4, 32, 128), BF), ((nf, 128, 896), BF),
        ((slab, 192, 128), BF), ((24, 96, 128), BF), ((slab, 96, 128), BF),
        ((depth * wide, 128, 128), BF), ((depth * rows, 128, 128), F32), ((128, 1024), F32),
        ((128, 1728), BF), ((64, 3456), BF), ((288, 384), BF),
        (((depth + 2) * rows, 32, 128), F32), ((2, rows, 32, 128), F32),
        ((depth, 2, 128, 128), BF), ((depth + 2, 4, 128, 128), BF), ((24, 384, 128), BF),
        ((24, 192, 128), BF), ((128, 896), F32),
        ((2 * count * len1, 128), F32), ((count * len1, 128), F32), ((count * len1, 128), F32),
        ((count - 1, len1, 128), F32), ((len1, 128), F32), ((nf, len1, 128), F32),
        ((2 * count * len1, 128), BF),
        ((2 * count * len2, 128), F32), ((count * len2, 128), F32), ((count * len2, 128), F32),
        ((count - 1, len2, 128), F32), ((2 * count * len2, 128), BF),
    ]
    copies = 128
    mo, g2o, g1o, vg = pl.pallas_call(
        functools.partial(whole_step, scaling),
        out_shape=[
            jax.ShapeDtypeStruct((depth * rows, 32, 128), F32),
            jax.ShapeDtypeStruct((27, 128, 32), F32),
            jax.ShapeDtypeStruct((1728, 128), F32),
            jax.ShapeDtypeStruct((64, 1024), F32),
        ],
        in_specs=[VMEM] * 4,
        out_specs=[VMEM] * 4,
        scratch_shapes=[pltpu.VMEM(shape, dtype) for shape, dtype in scratch] + [dma(copies), dma(copies)],
        compiler_params=pltpu.CompilerParams(
            vmem_limit_bytes=LIMIT, collective_id=0, has_side_effects=True
        ),
    )(vt, ct, wl, w1)
    mapped = mo.reshape(depth, rows, 32, 128).transpose(2, 0, 1, 3)[None]
    return (mapped, g2o, g1o.reshape(27, 64, 128), vg.reshape(1, 64, depth, 2, 128))


def solution(mesh):
    placed = (
        P("sample", None, "spatial", "filter", None),
        P(),
        P(None, None, "filter"),
        P("sample", "filter", "spatial", None, None),
    )
    return jax.shard_map(
        on_device,
        mesh=mesh,
        in_specs=placed,
        out_specs=(
            P("sample", "filter", "spatial", None, None),
            P(None, None, "filter"),
            P(),
            P("sample", None, "spatial", "filter", None),
        ),
        check_vma=False,
    )
```

```python
import functools
import math

import jax
import jax.numpy as jnp
from jax import lax
from jax.experimental import pallas as pl
from jax.experimental.pallas import tpu as pltpu
from jax.sharding import PartitionSpec as P

MESH = pl.DeviceIdType.MESH
BF = jnp.bfloat16
F32 = jnp.float32
VMEM = pl.BlockSpec(memory_space=pltpu.VMEM)
LIMIT = 56 * 1024 * 1024


def remote(src, dst, send, recv, device):
    return pltpu.make_async_remote_copy(
        src_ref=src, dst_ref=dst, send_sem=send, recv_sem=recv, device_id=device, device_id_type=MESH
    )


def greet(partners):
    barrier = pltpu.get_barrier_semaphore()
    for partner in partners:
        pl.semaphore_signal(barrier, inc=1, device_id=partner, device_id_type=MESH)
    pl.semaphore_wait(barrier, len(partners))


def places():
    ns, nf, nm = lax.axis_size("spatial"), lax.axis_size("filter"), lax.axis_size("sample")
    s, f, m = lax.axis_index("spatial"), lax.axis_index("filter"), lax.axis_index("sample")
    return ns, nf, nm, s, f, m


def dma(n):
    return pltpu.SemaphoreType.DMA((n,))


def shifted(cells):
    wide = cells.astype(F32)
    lane = lax.broadcasted_iota(jnp.int32, wide.shape, 1)
    below = jnp.where(lane == 0, 0.0, pltpu.roll(wide, 1, 1)).astype(BF)
    above = jnp.where(lane == 127, 0.0, pltpu.roll(wide, 127, 1)).astype(BF)
    return below, cells, above


def spread(src, dst, flip):
    count, channels, _ = src.shape
    step = 6 if count % 6 == 0 else 4

    def body(i, carry):
        for u in range(step):
            below, here, above = shifted(src[i * step + u])
            first, last = (above, below) if flip else (below, above)
            dst[i * step + u, pl.ds(0, channels)] = first
            dst[i * step + u, pl.ds(channels, channels)] = here
            dst[i * step + u, pl.ds(2 * channels, channels)] = last
        return carry

    lax.fori_loop(0, count // step, body, 0)


def columns(ref, wide, rows_at, flip, pad):
    stack = []
    for sx in range(3):
        for sy in range(3):
            ox, oy = (2 - sx, 2 - sy) if flip else (sx, sy)
            stack.append(jnp.concatenate([ref[(x + ox) * wide + (y + oy)] for x, y in rows_at], axis=1))
    if pad:
        stack.append(jnp.zeros((pad, 128 * len(rows_at)), BF))
    return jnp.concatenate(stack, axis=0)


NT = (((1,), (1,)), ((), ()))


class Links:
    def __init__(self, send, recv):
        self.send, self.recv, self.used = send, recv, 0

    def __call__(self, src, dst, device):
        n = self.used
        self.used += 1
        return remote(src, dst, self.send.at[n], self.recv.at[n], device)


def start(copies):
    for copy in copies:
        copy.start()


def wait(copies):
    for copy in copies:
        copy.wait()


def zero(ref):
    ref[...] = jnp.zeros(ref.shape, ref.dtype)


class Summed:
    def __init__(self, links, at, rows, whole, from_core, half, from_peers, total, from_filter, held):
        self.links, self.at, self.rows = links, at, rows
        self.whole, self.from_core, self.half, self.from_peers = whole, from_core, half, from_peers
        self.total, self.from_filter, self.held = total, from_filter, held

    def core(self):
        ns, nf, nm, s, f, m = self.at
        span = self.half.shape[0]
        core = lax.rem(s, 2)
        partner = {"spatial": s + 1 - 2 * core}
        self.moving = [self.links(self.whole.at[pl.ds((1 - core) * span, span)], self.from_core, partner)]
        start(self.moving)

    def peers(self):
        ns, nf, nm, s, f, m = self.at
        span, rows = self.half.shape[0], self.rows
        core, count = lax.rem(s, 2), span // rows
        me = (s // 2) * nm + m
        wait(self.moving)
        self.half[...] = self.whole[pl.ds(core * span, span)] + self.from_core[...]
        self.targets = []
        self.moving = []
        for r in range(1, count):
            j = lax.rem(me + r, count)
            device = {"spatial": (j // nm) * 2 + core, "sample": lax.rem(j, nm)}
            self.targets.append(device)
            self.moving.append(self.links(self.half.at[pl.ds(j * rows, rows)], self.from_peers.at[r - 1], device))
        start(self.moving)

    def gather_sum(self):
        ns, nf, nm, s, f, m = self.at
        wait(self.moving)
        value = self.half[pl.ds(((s // 2) * nm + m) * self.rows, self.rows)]
        for r in range(len(self.moving)):
            value = value + self.from_peers[r]
        return value

    def filters(self):
        ns, nf, nm, s, f, m = self.at
        value = self.gather_sum()
        self.total[...] = value
        self.from_filter[f] = value
        self.moving = [
            self.links(self.total, self.from_filter.at[f], {"filter": lax.rem(f + r, nf)}) for r in range(1, nf)
        ]
        start(self.moving)

    def back(self):
        ns, nf, nm, s, f, m = self.at
        if self.from_filter is None:
            value = self.gather_sum()
        else:
            wait(self.moving)
            value = self.from_filter[0]
            for k in range(1, nf):
                value = value + self.from_filter[k]
        span, rows = self.half.shape[0], self.rows
        self.base = pl.ds(lax.rem(s, 2) * span, span)
        mine = pl.ds(lax.rem(s, 2) * span + ((s // 2) * nm + m) * rows, rows)
        self.held[mine] = value.astype(BF)
        self.moving = [self.links(self.held.at[mine], self.held.at[mine], device) for device in self.targets]
        start(self.moving)

    def across(self):
        s = self.at[3]
        wait(self.moving)
        self.moving = [
            self.links(self.held.at[self.base], self.held.at[self.base], {"spatial": s + 1 - 2 * lax.rem(s, 2)})
        ]
        start(self.moving)

    def finish(self):
        wait(self.moving)


DEPTH = 4
OWN = [(x, y) for x in range(DEPTH) for y in range(2)]


def whole_step(
    scaling, vt, ct, wl, w1, mo, g2o, g1o, vg,
    vs, cx, cg, wg, v3, c3, x3, hs, pre, acc, w1t, w1v, wm, me, mr, bp, bh, b3, v3o, g2a,
    g1w, g1c, g1h, g1p, g1t, g1f, g1b, g2w, g2c, g2h, g2p, g2b, send, recv,
):
    at = ns, nf, nm, s, f, m = places()
    links = Links(send, recv)
    depth, rows = DEPTH, 2 * nf
    wide = rows + 2
    part = wl.shape[0] // ns
    nz = ns // 2
    core, z = lax.rem(s, 2), s // 2
    down, up = lax.rem(s + ns - 1, ns), lax.rem(s + 1, ns)
    left, right = lax.rem(f + nf - 1, nf), lax.rem(f + 1, nf)
    prev, after = {"spatial": down}, {"spatial": up}
    peers = [lax.rem(f + r, nf) for r in range(1, nf)]
    edges = [
        {"filter": left}, {"filter": right}, prev, after,
        {"spatial": down, "filter": left}, {"spatial": down, "filter": right},
        {"spatial": up, "filter": left}, {"spatial": up, "filter": right},
    ]
    group = []
    for r in range(1, nz * nm):
        j = lax.rem(z * nm + m + r, nz * nm)
        group.append({"spatial": (j // nm) * 2 + core, "sample": lax.rem(j, nm)})
    greet([{"filter": p} for p in peers] + edges[2:] + group)

    inner, body, two, pair = pl.ds(1, depth), pl.ds(0, depth), pl.ds(0, 2), pl.ds(1, 2)
    block = pl.ds(1 + 2 * f, 2)
    blocks = [links(vt, vs.at[inner, block], {"filter": p}) for p in peers]
    mine = pl.ds(s * part, part)
    halo = [links(ct.at[0], cx.at[depth + 1], prev), links(ct.at[depth - 1], cx.at[0], after)]
    weights = [links(wl.at[mine], wg.at[f, mine], {"filter": p}) for p in peers]
    cots = [links(ct.at[:, pl.ds(2 * p, 4)], cg.at[f, inner], {"filter": p}) for p in peers]
    for copies in (weights, halo, blocks):
        start(copies)

    vs[:, 0] = jnp.zeros_like(vs[:, 0])
    vs[:, rows + 1] = jnp.zeros_like(vs[:, 0])
    vs[inner, block] = vt[...]
    cx[inner] = ct[...]
    cg[f, inner] = ct[:, pl.ds(2 * f, 4)]
    wg[f, mine] = wl[mine]
    w1t[...] = w1[...].T
    wlt = wl[...].T
    for sx in range(3):
        for sy in range(3):
            for sz in range(3):
                k = sx * 9 + sy * 3 + sz
                w1v[:, 128 * k : 128 * (k + 1)] = w1[64 * k : 64 * (k + 1)]
                j = 32 * (sx * 3 + sz)
                wm[j : j + 32, 128 * sy : 128 * (sy + 1)] = wlt[32 * k : 32 * (k + 1)]
    zero(hs)
    zero(me)
    zero(acc)
    zero(g2a)

    wait(halo)

    @pl.when(s == 0)
    def _():
        cx[0] = jnp.zeros_like(cx[0])

    @pl.when(s == ns - 1)
    def _():
        cx[depth + 1] = jnp.zeros_like(cx[0])

    cxr = cx.reshape((depth + 2) * wide, 32, 128)
    spread(cxr, x3, True)
    for plane in (0, depth + 1):
        cg[f, plane] = cx[plane, pl.ds(2 * f, 4)]

    wait(weights)
    along = [
        links(wg.at[:, mine], wg.at[:, mine], {"spatial": lax.rem(z + r, nz) * 2 + core}) for r in range(1, nz)
    ]
    start(along)

    wait(blocks)
    row = pl.ds(1, rows)
    planes = [links(vs.at[1, row], vs.at[depth + 1, row], prev), links(vs.at[depth, row], vs.at[0, row], after)]
    start(planes)
    start(cots)
    vsr = vs.reshape((depth + 2) * wide, 64, 128)
    spread(vsr.at[pl.ds(wide, depth * wide)], v3.at[pl.ds(wide, depth * wide)], False)
    lot = min(8, rows)
    times = rows // lot

    def first(i, carry):
        x, y = i // times, lax.rem(i, times) * lot
        value = jnp.dot(
            w1t[...], columns(v3, wide, [(x, y + j) for j in range(lot)], False, 0), preferred_element_type=F32
        )
        hidden = (value * jax.nn.sigmoid(value)).astype(BF)
        for j in range(lot):
            pre[x * rows + y + j] = value[:, 128 * j : 128 * (j + 1)]
            hs[x * wide + y + 1 + j] = hidden[:, 128 * j : 128 * (j + 1)]
        return carry

    lax.fori_loop(times, 3 * times, first, 0)
    wait(along)
    across = []
    for k in range(nz):
        piece = pl.ds((2 * k + core) * part, part)
        across.append(links(wg.at[:, piece], wg.at[:, piece], {"spatial": s + 1 - 2 * core}))
    start(across)
    wait(planes)

    @pl.when(s == 0)
    def _():
        vs[0] = jnp.zeros_like(vs[0])

    @pl.when(s == ns - 1)
    def _():
        vs[depth + 1] = jnp.zeros_like(vs[0])

    for plane in (0, depth + 1):
        span = pl.ds(plane * wide, wide)
        spread(vsr.at[span], v3.at[span], False)
    lax.fori_loop(0, times, first, 0)
    lax.fori_loop(3 * times, 4 * times, first, 0)

    def second_weights(i, carry):
        x, y = i // times, lax.rem(i, times) * lot
        here = jnp.concatenate([hs[x * wide + y + j + 1] for j in range(lot)], axis=1)
        field = columns(x3, wide, [(x, y + j) for j in range(lot)], True, 32)
        g2a[...] += lax.dot_general(here, field, NT, preferred_element_type=F32)
        return carry

    lax.fori_loop(0, 3 * times, second_weights, 0)

    forward = []
    for r, copy in enumerate(cots):
        copy.wait()
        k = lax.rem(f + nf - 1 - r, nf)
        pieces = [links(cg.at[k, 1], cg.at[k, depth + 1], prev), links(cg.at[k, depth], cg.at[k, 0], after)]
        start(pieces)
        forward += pieces

    cgr = cg.reshape(nf, (depth + 2) * 4, 32, 128)

    def inside(k, carry):
        spread(cgr.at[k, pl.ds(4, 4 * depth)], c3.at[k, pl.ds(4, 4 * depth)], True)
        return carry

    lax.fori_loop(0, nf, inside, 0)
    lax.fori_loop(3 * times, 4 * times, second_weights, 0)
    for t in range(7):
        g2w[128 * t : 128 * (t + 1)] = g2a[:, 128 * t : 128 * (t + 1)]
    g2w[896:] = jnp.zeros((g2w.shape[0] - 896, 128), F32)
    other = Summed(links, at, g2p.shape[1], g2w, g2c, g2h, g2p, None, None, g2b)
    other.core()
    wait(across)
    wait(forward)

    @pl.when(s == 0)
    def _():
        cg[:, 0] = jnp.zeros_like(cg[:, 0])

    @pl.when(s == ns - 1)
    def _():
        cg[:, depth + 1] = jnp.zeros_like(cg[:, 0])

    def back(k, carry):
        for plane in (0, depth + 1):
            span = pl.ds(4 * plane, 4)
            spread(cgr.at[k, span], c3.at[k, span], True)
        for part_at in range(2):
            lanes = pl.ds(512 * part_at, 512)
            acc[:, lanes] += jnp.dot(
                wg[k], columns(c3.at[k], 4, OWN[4 * part_at : 4 * part_at + 4], True, 32), preferred_element_type=F32
            )
        return carry

    lax.fori_loop(0, nf, back, 0)
    for n, (x, y) in enumerate(OWN):
        u = pre[x * rows + 2 * f + y]
        sig = jax.nn.sigmoid(u)
        bp[x, y] = (acc[:, 128 * n : 128 * (n + 1)] * (sig * (1.0 + u * (1.0 - sig)))).astype(BF)
    pieces = [
        (bp.at[body, 0], bh.at[inner, 3]), (bp.at[body, 1], bh.at[inner, 0]),
        (bp.at[0, two], bh.at[depth + 1, pair]), (bp.at[depth - 1, two], bh.at[0, pair]),
        (bp.at[0, 0], bh.at[depth + 1, 3]), (bp.at[0, 1], bh.at[depth + 1, 0]),
        (bp.at[depth - 1, 0], bh.at[0, 3]), (bp.at[depth - 1, 1], bh.at[0, 0]),
    ]
    cells = [links(src, dst, device) for (src, dst), device in zip(pieces, edges)]
    start(cells)
    bh[inner, pair] = bp[...]

    for x in range(depth + 2):
        for y in range(4):
            v3o[x * 4 + y] = v3[x * wide + 2 * f + y]
    grads = jnp.concatenate([bp[x, y] for x, y in OWN], axis=1)
    for j in range(9):
        sx, sy = j // 3, j % 3
        field = jnp.concatenate([v3o[(x + sx) * 4 + y + sy] for x, y in OWN], axis=1)
        g1w[192 * j : 192 * (j + 1)] = lax.dot_general(field, grads, NT, preferred_element_type=F32)
    g1w[1728:] = jnp.zeros((g1w.shape[0] - 1728, 128), F32)
    one = Summed(links, at, g1t.shape[0], g1w, g1c, g1h, g1p, g1t, g1f, g1b)
    one.core()

    other.peers()

    def second(i, carry):
        x, y = i // (rows // 4), lax.rem(i, rows // 4) * 4
        field = jnp.concatenate(
            [jnp.concatenate([hs[x * wide + y + j + sy] for j in range(4)], axis=1) for sy in range(3)],
            axis=0,
        )
        value = jnp.dot(wm[...], field, preferred_element_type=F32)
        lane = lax.broadcasted_iota(jnp.int32, (32, 128), 1)
        for sx in range(3):
            for j in range(4):
                lanes = slice(128 * j, 128 * (j + 1))
                base = 96 * sx
                below = pltpu.roll(value[base : base + 32, lanes], 1, 1)
                above = pltpu.roll(value[base + 64 : base + 96, lanes], 127, 1)
                me[(x + 2 - sx) * rows + y + j] += (
                    jnp.where(lane == 0, 0.0, below)
                    + value[base + 32 : base + 64, lanes]
                    + jnp.where(lane == 127, 0.0, above)
                )
        return carry

    turn = rows // 4
    lax.fori_loop(0, 2 * turn, second, 0)
    one.peers()
    lax.fori_loop(2 * turn, 4 * turn, second, 0)
    outer = [
        links(me.at[pl.ds(0, rows)], mr.at[1], prev),
        links(me.at[pl.ds((depth + 1) * rows, rows)], mr.at[0], after),
    ]
    start(outer)
    one.filters()
    other.back()

    wait(cells)

    @pl.when(s == 0)
    def _():
        bh[0] = jnp.zeros_like(bh[0])

    @pl.when(s == ns - 1)
    def _():
        bh[depth + 1] = jnp.zeros_like(bh[0])

    @pl.when(f == 0)
    def _():
        bh[:, 0] = jnp.zeros_like(bh[:, 0])

    @pl.when(f == nf - 1)
    def _():
        bh[:, 3] = jnp.zeros_like(bh[:, 0])

    spread(bh.reshape((depth + 2) * 4, 128, 128), b3, True)
    for part_at in range(2):
        lanes = pl.ds(512 * part_at, 512)
        vg[:, lanes] = jnp.dot(
            w1v[...], columns(b3, 4, OWN[4 * part_at : 4 * part_at + 4], True, 0), preferred_element_type=F32
        )

    one.back()
    other.across()
    mo[...] = me[pl.ds(rows, depth * rows)]
    wait(outer)

    @pl.when(s > 0)
    def _():
        mo[pl.ds(0, rows)] += mr[0]

    @pl.when(s < ns - 1)
    def _():
        mo[pl.ds((depth - 1) * rows, rows)] += mr[1]

    one.across()
    one.finish()
    other.finish()
    g1o[...] = g1b[0:1728].astype(F32) * scaling
    for k in range(27):
        tile = g2b[128 * (k // 4) : 128 * (k // 4 + 1)].astype(F32) * scaling
        g2o[k] = tile[:, 32 * (k % 4) : 32 * (k % 4 + 1)]


def on_device(volume, weight_first, weight_second, cotangent):
    ns, nf, nm = lax.axis_size("spatial"), lax.axis_size("filter"), lax.axis_size("sample")
    depth, rows = DEPTH, 2 * nf
    wide = rows + 2
    scaling = 1.0 / math.sqrt(nm * depth * ns * rows * 128)
    count = ns // 2 * nm

    vt = volume[0].transpose(1, 2, 0, 3)
    ct = jnp.pad(cotangent[0].transpose(1, 2, 0, 3), ((0, 0), (1, 1), (0, 0), (0, 0)))
    wl = jnp.pad(weight_second.transpose(1, 0, 2).reshape(128, 864), ((0, 0), (0, 32)))
    w1 = weight_first.reshape(1728, 128)

    len1 = -(-1728 // (32 * count)) * 16
    len2 = -(-1024 // (32 * count)) * 16
    slab = (depth + 2) * wide
    scratch = [
        ((depth + 2, wide, 64, 128), BF), ((depth + 2, wide, 32, 128), BF),
        ((nf, depth + 2, 4, 32, 128), BF), ((nf, 128, 896), BF),
        ((slab, 192, 128), BF), ((nf, 24, 96, 128), BF), ((slab, 96, 128), BF),
        ((depth * wide, 128, 128), BF), ((depth * rows, 128, 128), F32), ((128, 1024), F32),
        ((128, 1728), BF), ((64, 3456), BF), ((288, 384), BF),
        (((depth + 2) * rows, 32, 128), F32), ((2, rows, 32, 128), F32),
        ((depth, 2, 128, 128), BF), ((depth + 2, 4, 128, 128), BF), ((24, 384, 128), BF),
        ((24, 192, 128), BF), ((128, 896), F32),
        ((2 * count * len1, 128), F32), ((count * len1, 128), F32), ((count * len1, 128), F32),
        ((count - 1, len1, 128), F32), ((len1, 128), F32), ((nf, len1, 128), F32),
        ((2 * count * len1, 128), BF),
        ((2 * count * len2, 128), F32), ((count * len2, 128), F32), ((count * len2, 128), F32),
        ((count - 1, len2, 128), F32), ((2 * count * len2, 128), BF),
    ]
    copies = 128
    mo, g2o, g1o, vg = pl.pallas_call(
        functools.partial(whole_step, scaling),
        out_shape=[
            jax.ShapeDtypeStruct((depth * rows, 32, 128), F32),
            jax.ShapeDtypeStruct((27, 128, 32), F32),
            jax.ShapeDtypeStruct((1728, 128), F32),
            jax.ShapeDtypeStruct((64, 1024), F32),
        ],
        in_specs=[VMEM] * 4,
        out_specs=[VMEM] * 4,
        scratch_shapes=[pltpu.VMEM(shape, dtype) for shape, dtype in scratch] + [dma(copies), dma(copies)],
        compiler_params=pltpu.CompilerParams(
            vmem_limit_bytes=LIMIT, collective_id=0, has_side_effects=True
        ),
    )(vt, ct, wl, w1)
    mapped = mo.reshape(depth, rows, 32, 128).transpose(2, 0, 1, 3)[None]
    return (mapped, g2o, g1o.reshape(27, 64, 128), vg.reshape(1, 64, depth, 2, 128))


def solution(mesh):
    placed = (
        P("sample", None, "spatial", "filter", None),
        P(),
        P(None, None, "filter"),
        P("sample", "filter", "spatial", None, None),
    )
    return jax.shard_map(
        on_device,
        mesh=mesh,
        in_specs=placed,
        out_specs=(
            P("sample", "filter", "spatial", None, None),
            P(None, None, "filter"),
            P(),
            P("sample", None, "spatial", "filter", None),
        ),
        check_vma=False,
    )
```

```python
import functools
import math

import jax
import jax.numpy as jnp
from jax import lax
from jax.experimental import pallas as pl
from jax.experimental.pallas import tpu as pltpu
from jax.sharding import PartitionSpec as P

MESH = pl.DeviceIdType.MESH
BF = jnp.bfloat16
F32 = jnp.float32
VMEM = pl.BlockSpec(memory_space=pltpu.VMEM)
LIMIT = 56 * 1024 * 1024


def remote(src, dst, send, recv, device):
    return pltpu.make_async_remote_copy(
        src_ref=src, dst_ref=dst, send_sem=send, recv_sem=recv, device_id=device, device_id_type=MESH
    )


def greet(partners):
    barrier = pltpu.get_barrier_semaphore()
    for partner in partners:
        pl.semaphore_signal(barrier, inc=1, device_id=partner, device_id_type=MESH)
    pl.semaphore_wait(barrier, len(partners))


def places():
    ns, nf, nm = lax.axis_size("spatial"), lax.axis_size("filter"), lax.axis_size("sample")
    s, f, m = lax.axis_index("spatial"), lax.axis_index("filter"), lax.axis_index("sample")
    return ns, nf, nm, s, f, m


def dma(n):
    return pltpu.SemaphoreType.DMA((n,))


def shifted(cells):
    wide = cells.astype(F32)
    lane = lax.broadcasted_iota(jnp.int32, wide.shape, 1)
    below = jnp.where(lane == 0, 0.0, pltpu.roll(wide, 1, 1)).astype(BF)
    above = jnp.where(lane == 127, 0.0, pltpu.roll(wide, 127, 1)).astype(BF)
    return below, cells, above


def spread(src, dst, flip):
    count, channels, _ = src.shape
    step = 6 if count % 6 == 0 else 4

    def body(i, carry):
        for u in range(step):
            below, here, above = shifted(src[i * step + u])
            first, last = (above, below) if flip else (below, above)
            dst[i * step + u, pl.ds(0, channels)] = first
            dst[i * step + u, pl.ds(channels, channels)] = here
            dst[i * step + u, pl.ds(2 * channels, channels)] = last
        return carry

    lax.fori_loop(0, count // step, body, 0)


def columns(ref, wide, rows_at, flip, pad):
    stack = []
    for sx in range(3):
        for sy in range(3):
            ox, oy = (2 - sx, 2 - sy) if flip else (sx, sy)
            stack.append(jnp.concatenate([ref[(x + ox) * wide + (y + oy)] for x, y in rows_at], axis=1))
    if pad:
        stack.append(jnp.zeros((pad, 128 * len(rows_at)), BF))
    return jnp.concatenate(stack, axis=0)


NT = (((1,), (1,)), ((), ()))


class Links:
    def __init__(self, send, recv):
        self.send, self.recv, self.used = send, recv, 0

    def __call__(self, src, dst, device):
        n = self.used
        self.used += 1
        return remote(src, dst, self.send.at[n], self.recv.at[n], device)


def start(copies):
    for copy in copies:
        copy.start()


def wait(copies):
    for copy in copies:
        copy.wait()


def zero(ref):
    ref[...] = jnp.zeros(ref.shape, ref.dtype)


class Summed:
    def __init__(self, links, at, rows, whole, from_core, half, from_peers, total, from_filter, held):
        self.links, self.at, self.rows = links, at, rows
        self.whole, self.from_core, self.half, self.from_peers = whole, from_core, half, from_peers
        self.total, self.from_filter, self.held = total, from_filter, held

    def core(self):
        ns, nf, nm, s, f, m = self.at
        span = self.half.shape[0]
        core = lax.rem(s, 2)
        partner = {"spatial": s + 1 - 2 * core}
        self.moving = [self.links(self.whole.at[pl.ds((1 - core) * span, span)], self.from_core, partner)]
        start(self.moving)

    def peers(self):
        ns, nf, nm, s, f, m = self.at
        span, rows = self.half.shape[0], self.rows
        core, count = lax.rem(s, 2), span // rows
        me = (s // 2) * nm + m
        wait(self.moving)
        self.half[...] = self.whole[pl.ds(core * span, span)] + self.from_core[...]
        self.targets = []
        self.moving = []
        for r in range(1, count):
            j = lax.rem(me + r, count)
            device = {"spatial": (j // nm) * 2 + core, "sample": lax.rem(j, nm)}
            self.targets.append(device)
            self.moving.append(self.links(self.half.at[pl.ds(j * rows, rows)], self.from_peers.at[r - 1], device))
        start(self.moving)

    def gather_sum(self):
        ns, nf, nm, s, f, m = self.at
        wait(self.moving)
        value = self.half[pl.ds(((s // 2) * nm + m) * self.rows, self.rows)]
        for r in range(len(self.moving)):
            value = value + self.from_peers[r]
        return value

    def filters(self):
        ns, nf, nm, s, f, m = self.at
        value = self.gather_sum()
        self.total[...] = value
        self.from_filter[f] = value
        self.moving = [
            self.links(self.total, self.from_filter.at[f], {"filter": lax.rem(f + r, nf)}) for r in range(1, nf)
        ]
        start(self.moving)

    def back(self):
        ns, nf, nm, s, f, m = self.at
        if self.from_filter is None:
            value = self.gather_sum()
        else:
            wait(self.moving)
            value = self.from_filter[0]
            for k in range(1, nf):
                value = value + self.from_filter[k]
        span, rows = self.half.shape[0], self.rows
        self.base = pl.ds(lax.rem(s, 2) * span, span)
        mine = pl.ds(lax.rem(s, 2) * span + ((s // 2) * nm + m) * rows, rows)
        self.held[mine] = value.astype(BF)
        self.moving = [self.links(self.held.at[mine], self.held.at[mine], device) for device in self.targets]
        start(self.moving)

    def across(self):
        s = self.at[3]
        wait(self.moving)
        self.moving = [
            self.links(self.held.at[self.base], self.held.at[self.base], {"spatial": s + 1 - 2 * lax.rem(s, 2)})
        ]
        start(self.moving)

    def finish(self):
        wait(self.moving)


DEPTH = 4


def around(block, padded):
    body, inner, two, pair = pl.ds(0, DEPTH), pl.ds(1, DEPTH), pl.ds(0, 2), pl.ds(1, 2)
    last = DEPTH - 1
    return [
        (block.at[body, 0], padded.at[inner, 3]), (block.at[body, 1], padded.at[inner, 0]),
        (block.at[0, two], padded.at[DEPTH + 1, pair]), (block.at[last, two], padded.at[0, pair]),
        (block.at[0, 0], padded.at[DEPTH + 1, 3]), (block.at[0, 1], padded.at[DEPTH + 1, 0]),
        (block.at[last, 0], padded.at[0, 3]), (block.at[last, 1], padded.at[0, 0]),
    ]


def clear_outside(padded, at):
    ns, nf, nm, s, f, m = at
    for place, end, plane in ((s, 0, 0), (s, ns - 1, DEPTH + 1)):
        @pl.when(place == end)
        def _():
            padded[plane] = jnp.zeros_like(padded[plane])
    for place, end, row in ((f, 0, 0), (f, nf - 1, 3)):
        @pl.when(place == end)
        def _():
            padded[:, row] = jnp.zeros_like(padded[:, row])


OWN = [(x, y) for x in range(DEPTH) for y in range(2)]


def whole_step(
    scaling, vt, ct, wl, w1, mo, g2o, g1o, vg,
    vs, vo, cx, cg, wg, v3, c3, x3, hs, pre, acc, w1t, w1v, wm, me, mr, bp, bh, b3, v3o, g2a,
    g1w, g1c, g1h, g1p, g1t, g1f, g1b, g2w, g2c, g2h, g2p, g2b, send, recv,
):
    at = ns, nf, nm, s, f, m = places()
    links = Links(send, recv)
    depth, rows = DEPTH, 2 * nf
    wide = rows + 2
    part = wl.shape[0] // ns
    nz = ns // 2
    core, z = lax.rem(s, 2), s // 2
    down, up = lax.rem(s + ns - 1, ns), lax.rem(s + 1, ns)
    left, right = lax.rem(f + nf - 1, nf), lax.rem(f + 1, nf)
    prev, after = {"spatial": down}, {"spatial": up}
    peers = [lax.rem(f + r, nf) for r in range(1, nf)]
    edges = [
        {"filter": left}, {"filter": right}, prev, after,
        {"spatial": down, "filter": left}, {"spatial": down, "filter": right},
        {"spatial": up, "filter": left}, {"spatial": up, "filter": right},
    ]
    group = []
    for r in range(1, nz * nm):
        j = lax.rem(z * nm + m + r, nz * nm)
        group.append({"spatial": (j // nm) * 2 + core, "sample": lax.rem(j, nm)})
    greet([{"filter": p} for p in peers] + edges[2:] + group)

    inner, body, two, pair = pl.ds(1, depth), pl.ds(0, depth), pl.ds(0, 2), pl.ds(1, 2)
    block = pl.ds(1 + 2 * f, 2)
    blocks = [links(vt, vs.at[inner, block], {"filter": p}) for p in peers]
    mine = pl.ds(s * part, part)
    halo = [links(ct.at[0], cx.at[depth + 1], prev), links(ct.at[depth - 1], cx.at[0], after)]
    weights = [links(wl.at[mine], wg.at[f, mine], {"filter": p}) for p in peers]
    cots = [links(ct.at[:, pl.ds(2 * p, 4)], cg.at[f, inner], {"filter": p}) for p in peers]
    corners = [links(src, dst, device) for (src, dst), device in zip(around(vt, vo), edges)]
    for copies in (weights, halo, corners, cots):
        start(copies)

    vs[:, 0] = jnp.zeros_like(vs[:, 0])
    vs[:, rows + 1] = jnp.zeros_like(vs[:, 0])
    vs[inner, block] = vt[...]
    cx[inner] = ct[...]
    cg[f, inner] = ct[:, pl.ds(2 * f, 4)]
    wg[f, mine] = wl[mine]
    w1t[...] = w1[...].T
    wlt = wl[...].T
    for sx in range(3):
        for sy in range(3):
            for sz in range(3):
                k = sx * 9 + sy * 3 + sz
                w1v[:, 128 * k : 128 * (k + 1)] = w1[64 * k : 64 * (k + 1)]
                j = 32 * (sx * 3 + sz)
                wm[j : j + 32, 128 * sy : 128 * (sy + 1)] = wlt[32 * k : 32 * (k + 1)]
    zero(hs)
    zero(me)
    zero(acc)
    zero(g2a)

    wait(weights)
    along = [
        links(wg.at[:, mine], wg.at[:, mine], {"spatial": lax.rem(z + r, nz) * 2 + core}) for r in range(1, nz)
    ]
    start(along)

    wait(halo)

    @pl.when(s == 0)
    def _():
        cx[0] = jnp.zeros_like(cx[0])

    @pl.when(s == ns - 1)
    def _():
        cx[depth + 1] = jnp.zeros_like(cx[0])

    cxr = cx.reshape((depth + 2) * wide, 32, 128)
    spread(cxr, x3, True)
    for plane in (0, depth + 1):
        cg[f, plane] = cx[plane, pl.ds(2 * f, 4)]

    wait(corners)
    vo[inner, pair] = vt[...]
    clear_outside(vo, at)
    spread(vo.reshape((depth + 2) * 4, 64, 128), v3o, False)
    for part_at in range(2):
        lanes = pl.ds(512 * part_at, 512)
        pre[:, lanes] = jnp.dot(
            w1t[...], columns(v3o, 4, OWN[4 * part_at : 4 * part_at + 4], False, 0), preferred_element_type=F32
        )

    forward = []
    for r, copy in enumerate(cots):
        copy.wait()
        k = lax.rem(f + nf - 1 - r, nf)
        pieces = [links(cg.at[k, 1], cg.at[k, depth + 1], prev), links(cg.at[k, depth], cg.at[k, 0], after)]
        start(pieces)
        forward += pieces

    start(blocks)
    cgr = cg.reshape(nf, (depth + 2) * 4, 32, 128)

    def inside(k, carry):
        spread(cgr.at[k, pl.ds(4, 4 * depth)], c3.at[k, pl.ds(4, 4 * depth)], True)
        return carry

    lax.fori_loop(0, nf, inside, 0)
    wait(along)
    across = []
    for k in range(nz):
        piece = pl.ds((2 * k + core) * part, part)
        across.append(links(wg.at[:, piece], wg.at[:, piece], {"spatial": s + 1 - 2 * core}))
    start(across)
    wait(across)
    wait(forward)

    @pl.when(s == 0)
    def _():
        cg[:, 0] = jnp.zeros_like(cg[:, 0])

    @pl.when(s == ns - 1)
    def _():
        cg[:, depth + 1] = jnp.zeros_like(cg[:, 0])

    def back(k, carry):
        for plane in (0, depth + 1):
            span = pl.ds(4 * plane, 4)
            spread(cgr.at[k, span], c3.at[k, span], True)
        for part_at in range(2):
            lanes = pl.ds(512 * part_at, 512)
            acc[:, lanes] += jnp.dot(
                wg[k], columns(c3.at[k], 4, OWN[4 * part_at : 4 * part_at + 4], True, 32), preferred_element_type=F32
            )
        return carry

    lax.fori_loop(0, nf, back, 0)
    for n, (x, y) in enumerate(OWN):
        u = pre[:, 128 * n : 128 * (n + 1)]
        sig = jax.nn.sigmoid(u)
        bp[x, y] = (acc[:, 128 * n : 128 * (n + 1)] * (sig * (1.0 + u * (1.0 - sig)))).astype(BF)
    cells = [links(src, dst, device) for (src, dst), device in zip(around(bp, bh), edges)]
    start(cells)
    bh[inner, pair] = bp[...]

    grads = jnp.concatenate([bp[x, y] for x, y in OWN], axis=1)
    for j in range(9):
        sx, sy = j // 3, j % 3
        field = jnp.concatenate([v3o[(x + sx) * 4 + y + sy] for x, y in OWN], axis=1)
        g1w[192 * j : 192 * (j + 1)] = lax.dot_general(field, grads, NT, preferred_element_type=F32)
    g1w[1728:] = jnp.zeros((g1w.shape[0] - 1728, 128), F32)
    one = Summed(links, at, g1t.shape[0], g1w, g1c, g1h, g1p, g1t, g1f, g1b)
    one.core()

    wait(blocks)
    row = pl.ds(1, rows)
    planes = [links(vs.at[1, row], vs.at[depth + 1, row], prev), links(vs.at[depth, row], vs.at[0, row], after)]
    start(planes)
    vsr = vs.reshape((depth + 2) * wide, 64, 128)
    spread(vsr.at[pl.ds(wide, depth * wide)], v3.at[pl.ds(wide, depth * wide)], False)
    lot = min(8, rows)
    times = rows // lot

    def first(i, carry):
        x, y = i // times, lax.rem(i, times) * lot
        value = jnp.dot(
            w1t[...], columns(v3, wide, [(x, y + j) for j in range(lot)], False, 0), preferred_element_type=F32
        )
        hidden = (value * jax.nn.sigmoid(value)).astype(BF)
        for j in range(lot):
            hs[x * wide + y + 1 + j] = hidden[:, 128 * j : 128 * (j + 1)]
        return carry

    lax.fori_loop(times, 3 * times, first, 0)
    one.peers()
    wait(planes)

    @pl.when(s == 0)
    def _():
        vs[0] = jnp.zeros_like(vs[0])

    @pl.when(s == ns - 1)
    def _():
        vs[depth + 1] = jnp.zeros_like(vs[0])

    for plane in (0, depth + 1):
        span = pl.ds(plane * wide, wide)
        spread(vsr.at[span], v3.at[span], False)
    lax.fori_loop(0, times, first, 0)
    lax.fori_loop(3 * times, 4 * times, first, 0)
    one.filters()

    def second_weights(i, carry):
        x, y = i // times, lax.rem(i, times) * lot
        here = jnp.concatenate([hs[x * wide + y + j + 1] for j in range(lot)], axis=1)
        field = columns(x3, wide, [(x, y + j) for j in range(lot)], True, 32)
        g2a[...] += lax.dot_general(here, field, NT, preferred_element_type=F32)
        return carry

    lax.fori_loop(0, 4 * times, second_weights, 0)
    for t in range(7):
        g2w[128 * t : 128 * (t + 1)] = g2a[:, 128 * t : 128 * (t + 1)]
    g2w[896:] = jnp.zeros((g2w.shape[0] - 896, 128), F32)
    other = Summed(links, at, g2p.shape[1], g2w, g2c, g2h, g2p, None, None, g2b)
    other.core()
    one.back()

    def second(i, carry):
        x, y = i // (rows // 4), lax.rem(i, rows // 4) * 4
        field = jnp.concatenate(
            [jnp.concatenate([hs[x * wide + y + j + sy] for j in range(4)], axis=1) for sy in range(3)],
            axis=0,
        )
        value = jnp.dot(wm[...], field, preferred_element_type=F32)
        lane = lax.broadcasted_iota(jnp.int32, (32, 128), 1)
        for sx in range(3):
            for j in range(4):
                lanes = slice(128 * j, 128 * (j + 1))
                base = 96 * sx
                below = pltpu.roll(value[base : base + 32, lanes], 1, 1)
                above = pltpu.roll(value[base + 64 : base + 96, lanes], 127, 1)
                me[(x + 2 - sx) * rows + y + j] += (
                    jnp.where(lane == 0, 0.0, below)
                    + value[base + 32 : base + 64, lanes]
                    + jnp.where(lane == 127, 0.0, above)
                )
        return carry

    turn = rows // 4
    lax.fori_loop(0, 2 * turn, second, 0)
    other.peers()
    one.across()
    lax.fori_loop(2 * turn, 4 * turn, second, 0)
    outer = [
        links(me.at[pl.ds(0, rows)], mr.at[1], prev),
        links(me.at[pl.ds((depth + 1) * rows, rows)], mr.at[0], after),
    ]
    start(outer)
    other.back()

    wait(cells)
    clear_outside(bh, at)
    spread(bh.reshape((depth + 2) * 4, 128, 128), b3, True)
    for part_at in range(2):
        lanes = pl.ds(512 * part_at, 512)
        vg[:, lanes] = jnp.dot(
            w1v[...], columns(b3, 4, OWN[4 * part_at : 4 * part_at + 4], True, 0), preferred_element_type=F32
        )
    other.across()
    one.finish()
    g1o[...] = g1b[0:1728].astype(F32) * scaling
    mo[...] = me[pl.ds(rows, depth * rows)]
    wait(outer)

    @pl.when(s > 0)
    def _():
        mo[pl.ds(0, rows)] += mr[0]

    @pl.when(s < ns - 1)
    def _():
        mo[pl.ds((depth - 1) * rows, rows)] += mr[1]

    other.finish()
    for k in range(27):
        tile = g2b[128 * (k // 4) : 128 * (k // 4 + 1)].astype(F32) * scaling
        g2o[k] = tile[:, 32 * (k % 4) : 32 * (k % 4 + 1)]


def on_device(volume, weight_first, weight_second, cotangent):
    ns, nf, nm = lax.axis_size("spatial"), lax.axis_size("filter"), lax.axis_size("sample")
    depth, rows = DEPTH, 2 * nf
    wide = rows + 2
    scaling = 1.0 / math.sqrt(nm * depth * ns * rows * 128)
    count = ns // 2 * nm

    vt = volume[0].transpose(1, 2, 0, 3)
    ct = jnp.pad(cotangent[0].transpose(1, 2, 0, 3), ((0, 0), (1, 1), (0, 0), (0, 0)))
    wl = jnp.pad(weight_second.transpose(1, 0, 2).reshape(128, 864), ((0, 0), (0, 32)))
    w1 = weight_first.reshape(1728, 128)

    len1 = -(-1728 // (32 * count)) * 16
    len2 = -(-1024 // (32 * count)) * 16
    slab = (depth + 2) * wide
    scratch = [
        ((depth + 2, wide, 64, 128), BF), ((depth + 2, 4, 64, 128), BF), ((depth + 2, wide, 32, 128), BF),
        ((nf, depth + 2, 4, 32, 128), BF), ((nf, 128, 896), BF),
        ((slab, 192, 128), BF), ((nf, 24, 96, 128), BF), ((slab, 96, 128), BF),
        ((depth * wide, 128, 128), BF), ((128, 1024), F32), ((128, 1024), F32),
        ((128, 1728), BF), ((64, 3456), BF), ((288, 384), BF),
        (((depth + 2) * rows, 32, 128), F32), ((2, rows, 32, 128), F32),
        ((depth, 2, 128, 128), BF), ((depth + 2, 4, 128, 128), BF), ((24, 384, 128), BF),
        ((24, 192, 128), BF), ((128, 896), F32),
        ((2 * count * len1, 128), F32), ((count * len1, 128), F32), ((count * len1, 128), F32),
        ((count - 1, len1, 128), F32), ((len1, 128), F32), ((nf, len1, 128), F32),
        ((2 * count * len1, 128), BF),
        ((2 * count * len2, 128), F32), ((count * len2, 128), F32), ((count * len2, 128), F32),
        ((count - 1, len2, 128), F32), ((2 * count * len2, 128), BF),
    ]
    copies = 128
    mo, g2o, g1o, vg = pl.pallas_call(
        functools.partial(whole_step, scaling),
        out_shape=[
            jax.ShapeDtypeStruct((depth * rows, 32, 128), F32),
            jax.ShapeDtypeStruct((27, 128, 32), F32),
            jax.ShapeDtypeStruct((1728, 128), F32),
            jax.ShapeDtypeStruct((64, 1024), F32),
        ],
        in_specs=[VMEM] * 4,
        out_specs=[VMEM] * 4,
        scratch_shapes=[pltpu.VMEM(shape, dtype) for shape, dtype in scratch] + [dma(copies), dma(copies)],
        compiler_params=pltpu.CompilerParams(
            vmem_limit_bytes=LIMIT, collective_id=0, has_side_effects=True
        ),
    )(vt, ct, wl, w1)
    mapped = mo.reshape(depth, rows, 32, 128).transpose(2, 0, 1, 3)[None]
    return (mapped, g2o, g1o.reshape(27, 64, 128), vg.reshape(1, 64, depth, 2, 128))


def solution(mesh):
    placed = (
        P("sample", None, "spatial", "filter", None),
        P(),
        P(None, None, "filter"),
        P("sample", "filter", "spatial", None, None),
    )
    return jax.shard_map(
        on_device,
        mesh=mesh,
        in_specs=placed,
        out_specs=(
            P("sample", "filter", "spatial", None, None),
            P(None, None, "filter"),
            P(),
            P("sample", None, "spatial", "filter", None),
        ),
        check_vma=False,
    )
```

```python
import functools
import math

import jax
import jax.numpy as jnp
from jax import lax
from jax.experimental import pallas as pl
from jax.experimental.pallas import tpu as pltpu
from jax.sharding import PartitionSpec as P

MESH = pl.DeviceIdType.MESH
BF = jnp.bfloat16
F32 = jnp.float32
VMEM = pl.BlockSpec(memory_space=pltpu.VMEM)
LIMIT = 56 * 1024 * 1024


def remote(src, dst, send, recv, device):
    return pltpu.make_async_remote_copy(
        src_ref=src, dst_ref=dst, send_sem=send, recv_sem=recv, device_id=device, device_id_type=MESH
    )


def greet(partners):
    barrier = pltpu.get_barrier_semaphore()
    for partner in partners:
        pl.semaphore_signal(barrier, inc=1, device_id=partner, device_id_type=MESH)
    pl.semaphore_wait(barrier, len(partners))


def places():
    ns, nf, nm = lax.axis_size("spatial"), lax.axis_size("filter"), lax.axis_size("sample")
    s, f, m = lax.axis_index("spatial"), lax.axis_index("filter"), lax.axis_index("sample")
    return ns, nf, nm, s, f, m


def dma(n):
    return pltpu.SemaphoreType.DMA((n,))


def shifted(cells):
    wide = cells.astype(F32)
    lane = lax.broadcasted_iota(jnp.int32, wide.shape, 1)
    below = jnp.where(lane == 0, 0.0, pltpu.roll(wide, 1, 1)).astype(BF)
    above = jnp.where(lane == 127, 0.0, pltpu.roll(wide, 127, 1)).astype(BF)
    return below, cells, above


def spread(src, dst, flip):
    count, channels, _ = src.shape
    step = 6 if count % 6 == 0 else 4

    def body(i, carry):
        for u in range(step):
            below, here, above = shifted(src[i * step + u])
            first, last = (above, below) if flip else (below, above)
            dst[i * step + u, pl.ds(0, channels)] = first
            dst[i * step + u, pl.ds(channels, channels)] = here
            dst[i * step + u, pl.ds(2 * channels, channels)] = last
        return carry

    lax.fori_loop(0, count // step, body, 0)


def columns(ref, wide, rows_at, flip, pad):
    stack = []
    for sx in range(3):
        for sy in range(3):
            ox, oy = (2 - sx, 2 - sy) if flip else (sx, sy)
            stack.append(jnp.concatenate([ref[(x + ox) * wide + (y + oy)] for x, y in rows_at], axis=1))
    if pad:
        stack.append(jnp.zeros((pad, 128 * len(rows_at)), BF))
    return jnp.concatenate(stack, axis=0)


NT = (((1,), (1,)), ((), ()))


class Links:
    def __init__(self, send, recv):
        self.send, self.recv, self.used = send, recv, 0

    def __call__(self, src, dst, device):
        n = self.used
        self.used += 1
        return remote(src, dst, self.send.at[n], self.recv.at[n], device)


def start(copies):
    for copy in copies:
        copy.start()


def wait(copies):
    for copy in copies:
        copy.wait()


def zero(ref):
    ref[...] = jnp.zeros(ref.shape, ref.dtype)


class Summed:
    def __init__(self, links, at, whole, rounded, arrived, column, split, split_in, ring, place, mine, ring_in, held):
        self.links, self.at, self.whole, self.rounded, self.arrived = links, at, whole, rounded, arrived
        self.column, self.split, self.split_in = column, split, split_in
        self.ring, self.place, self.mine, self.ring_in, self.held = ring, place, mine, ring_in, held
        self.rows, self.step = arrived.shape[1], mine.shape[0]

    def scatter(self):
        ns, nf, nm, s, f, m = self.at
        self.rounded[...] = self.whole[...].astype(BF)
        self.targets, self.moving = [], []
        for r in range(1, ns):
            j = lax.rem(s + r, ns)
            self.targets.append({"spatial": j})
            self.moving.append(
                self.links(self.rounded.at[pl.ds(j * self.rows, self.rows)], self.arrived.at[r - 1], {"spatial": j})
            )
        start(self.moving)

    def spatial_sum(self):
        wait(self.moving)
        value = self.whole[pl.ds(self.at[3] * self.rows, self.rows)]
        for r in range(len(self.targets)):
            value = value + self.arrived[r].astype(F32)
        return value

    def columns(self):
        self.split[...] = self.spatial_sum()
        self.moving = [
            self.links(self.split.at[pl.ds(y * self.step, self.step)], self.split_in.at[i], device)
            for i, (y, device) in enumerate(self.column)
        ]
        start(self.moving)

    def rings(self):
        if self.split is None:
            value = self.spatial_sum()
        else:
            wait(self.moving)
            value = self.split[pl.ds(self.at[4] // 2 * self.step, self.step)]
            for i in range(len(self.column)):
                value = value + self.split_in[i]
        self.mine[...] = value
        self.ring_in[self.place] = value
        self.moving = [self.links(self.mine, self.ring_in.at[self.place], device) for device in self.ring]
        start(self.moving)

    def back(self):
        wait(self.moving)
        value = self.ring_in[0]
        for i in range(1, self.ring_in.shape[0]):
            value = value + self.ring_in[i]
        base = self.at[3] * self.rows
        self.block = pl.ds(base, self.rows)
        if self.split is not None:
            here = pl.ds(base + self.at[4] // 2 * self.step, self.step)
            self.held[here] = value.astype(BF)
            self.moving = [self.links(self.held.at[here], self.held.at[here], device) for y, device in self.column]
            start(self.moving)
        else:
            self.held[self.block] = value.astype(BF)
            self.moving = []

    def spread(self):
        wait(self.moving)
        self.moving = [self.links(self.held.at[self.block], self.held.at[self.block], device) for device in self.targets]
        start(self.moving)

    def finish(self):
        wait(self.moving)


DEPTH = 4


def around(block, padded):
    body, inner, two, pair = pl.ds(0, DEPTH), pl.ds(1, DEPTH), pl.ds(0, 2), pl.ds(1, 2)
    last = DEPTH - 1
    return [
        (block.at[body, 0], padded.at[inner, 3]), (block.at[body, 1], padded.at[inner, 0]),
        (block.at[0, two], padded.at[DEPTH + 1, pair]), (block.at[last, two], padded.at[0, pair]),
        (block.at[0, 0], padded.at[DEPTH + 1, 3]), (block.at[0, 1], padded.at[DEPTH + 1, 0]),
        (block.at[last, 0], padded.at[0, 3]), (block.at[last, 1], padded.at[0, 0]),
    ]


def clear_outside(padded, at):
    ns, nf, nm, s, f, m = at
    for place, end, plane in ((s, 0, 0), (s, ns - 1, DEPTH + 1)):
        @pl.when(place == end)
        def _():
            padded[plane] = jnp.zeros_like(padded[plane])
    for place, end, row in ((f, 0, 0), (f, nf - 1, 3)):
        @pl.when(place == end)
        def _():
            padded[:, row] = jnp.zeros_like(padded[:, row])


OWN = [(x, y) for x in range(DEPTH) for y in range(2)]


def whole_step(
    scaling, vt, ct, wlt, w1, mo, g2o, g1o, vg,
    vs, vo, cx, cg, cp, cy, wg, v3, c3, x3, hs, pre, acc, w1t, w1v, wm, me, mr, bp, bh, b3, v3o, wl,
    g1w, g1s, g1p, g1q, g1y, g1m, g1r, g1b, g2w, g2s, g2p, g2m, g2r, g2b, send, recv,
):
    at = ns, nf, nm, s, f, m = places()
    links = Links(send, recv)
    depth, rows = DEPTH, 2 * nf
    wide = rows + 2
    part = 128 // ns
    nz = ns // 2
    core, z = lax.rem(s, 2), s // 2
    down, up = lax.rem(s + ns - 1, ns), lax.rem(s + 1, ns)
    left, right = lax.rem(f + nf - 1, nf), lax.rem(f + 1, nf)
    prev, after = {"spatial": down}, {"spatial": up}
    peers = [lax.rem(f + r, nf) for r in range(1, nf)]
    edges = [
        {"filter": left}, {"filter": right}, prev, after,
        {"spatial": down, "filter": left}, {"spatial": down, "filter": right},
        {"spatial": up, "filter": left}, {"spatial": up, "filter": right},
    ]
    ring = []
    for i in range(1, 2 * nm):
        j = lax.rem(lax.rem(f, 2) * nm + m + i, 2 * nm)
        ring.append({"filter": f - lax.rem(f, 2) + j // nm, "sample": lax.rem(j, nm)})
    other_sample = [{"sample": lax.rem(m + i, nm)} for i in range(1, nm)]
    group = [{"spatial": lax.rem(s + r, ns)} for r in range(1, ns)] + ring
    wl[...] = jnp.concatenate([wlt[...], jnp.zeros((32, 128), BF)], axis=0).T
    greet([{"filter": p} for p in peers] + edges[4:] + group)

    inner, body, two, pair = pl.ds(1, depth), pl.ds(0, depth), pl.ds(0, 2), pl.ds(1, 2)
    block = pl.ds(1 + 2 * f, 2)
    ny = nf // 2
    xl, yy = lax.rem(f, 2), f // 2
    fx = f + 1 - 2 * xl
    partner = {"filter": fx}
    ys = [lax.rem(yy + r, ny) for r in range(1, ny)]
    sources = [2 * lax.rem(yy + ny - r, ny) + xl for r in range(1, ny)]
    column = [{"filter": 2 * y + xl} for y in ys]
    lo, hi, glo, ghi = pl.ds(0, 2), pl.ds(2, 2), pl.ds(1, 2), pl.ds(3, 2)
    vol_x = links(vt, vs.at[inner, block], partner)
    vol_y = [links(vt, vs.at[inner, block], device) for device in column]
    mine = pl.ds(s * part, part)
    halo = [links(ct.at[0], cx.at[depth + 1], prev), links(ct.at[depth - 1], cx.at[0], after)]
    weights = [links(wl.at[mine], wg.at[f, mine], {"filter": p}) for p in peers]
    cot_x = links(ct.at[lo, pl.ds(2 - 2 * xl, rows)], cp, partner)
    cot_y = [links(ct.at[hi, pl.ds(4 * y, 6)], cy.at[i], column[i]) for i, y in enumerate(ys)]
    cots = [links(ct.at[hi, pl.ds(2 * fx, 4)], cg.at[f, ghi], partner)]
    cots += [links(ct.at[lo, pl.ds(4 * y + 2 * xl, 4)], cg.at[f, glo], column[i]) for i, y in enumerate(ys)]
    corners = [links(src, dst, device) for (src, dst), device in zip(around(vt, vo), edges)]
    for copies in (weights, [cot_x], cot_y, cots, corners, halo):
        start(copies)

    vs[:, 0] = jnp.zeros_like(vs[:, 0])
    vs[:, rows + 1] = jnp.zeros_like(vs[:, 0])
    vs[inner, block] = vt[...]
    cx[inner] = ct[...]
    cg[f, inner] = ct[:, pl.ds(2 * f, 4)]
    wg[f, mine] = wl[mine]
    w1t[...] = w1[...].T
    for sx in range(3):
        for sy in range(3):
            for sz in range(3):
                k = sx * 9 + sy * 3 + sz
                w1v[:, 128 * k : 128 * (k + 1)] = w1[64 * k : 64 * (k + 1)]
                j = 32 * (sx * 3 + sz)
                wm[j : j + 32, 128 * sy : 128 * (sy + 1)] = wlt[32 * k : 32 * (k + 1)]
    zero(hs)
    zero(me)
    zero(acc)
    zero(g2w)

    wait(weights)
    along = [
        links(wg.at[:, mine], wg.at[:, mine], {"spatial": lax.rem(z + r, nz) * 2 + core}) for r in range(1, nz)
    ]
    start(along)

    cot_x.wait()
    onward = [links(cp.at[:, pl.ds(4 * y, 4)], cg.at[fx, glo], column[i]) for i, y in enumerate(ys)]
    start(onward)
    cots += onward
    cg[fx, glo] = cp[:, pl.ds(4 * yy, 4)]
    for i, k in enumerate(sources):
        cot_y[i].wait()
        onward = links(cy.at[i, :, pl.ds(2 - 2 * xl, 4)], cg.at[k, ghi], partner)
        onward.start()
        cots.append(onward)
        cg[k, ghi] = cy[i, :, pl.ds(2 * xl, 4)]

    start([vol_x] + vol_y)

    wait(halo)

    @pl.when(s == 0)
    def _():
        cx[0] = jnp.zeros_like(cx[0])

    @pl.when(s == ns - 1)
    def _():
        cx[depth + 1] = jnp.zeros_like(cx[0])

    cxr = cx.reshape((depth + 2) * wide, 32, 128)
    spread(cxr, x3, True)
    wait(corners)
    vo[inner, pair] = vt[...]
    clear_outside(vo, at)
    spread(vo.reshape((depth + 2) * 4, 64, 128), v3o, False)
    for part_at in range(2):
        lanes = pl.ds(512 * part_at, 512)
        pre[:, lanes] = jnp.dot(
            w1t[...], columns(v3o, 4, OWN[4 * part_at : 4 * part_at + 4], False, 0), preferred_element_type=F32
        )

    wait(cots)
    forward = [links(cg.at[:, 1], cg.at[:, depth + 1], prev), links(cg.at[:, depth], cg.at[:, 0], after)]
    start(forward)
    cgr = cg.reshape(nf, (depth + 2) * 4, 32, 128)

    def inside(k, carry):
        spread(cgr.at[k, pl.ds(4, 4 * depth)], c3.at[k, pl.ds(4, 4 * depth)], True)
        return carry

    lax.fori_loop(0, nf, inside, 0)
    vol_x.wait()
    over = pl.ds(1 + 2 * fx, 2)
    blocks = [links(vs.at[glo, over], vs.at[glo, over], device) for device in column]
    start(blocks)
    for copy, k in zip(vol_y, sources):
        copy.wait()
        there = pl.ds(1 + 2 * k, 2)
        onward = links(vs.at[ghi, there], vs.at[ghi, there], partner)
        onward.start()
        blocks.append(onward)
    wait(along)
    across = []
    for k in range(nz):
        piece = pl.ds((2 * k + core) * part, part)
        across.append(links(wg.at[:, piece], wg.at[:, piece], {"spatial": s + 1 - 2 * core}))
    start(across)
    wait(across)
    wait(forward)

    @pl.when(s == 0)
    def _():
        cg[:, 0] = jnp.zeros_like(cg[:, 0])

    @pl.when(s == ns - 1)
    def _():
        cg[:, depth + 1] = jnp.zeros_like(cg[:, 0])

    def back(k, carry):
        for plane in (0, depth + 1):
            span = pl.ds(4 * plane, 4)
            spread(cgr.at[k, span], c3.at[k, span], True)
        for part_at in range(2):
            lanes = pl.ds(512 * part_at, 512)
            acc[:, lanes] += jnp.dot(
                wg[k], columns(c3.at[k], 4, OWN[4 * part_at : 4 * part_at + 4], True, 32), preferred_element_type=F32
            )
        return carry

    lax.fori_loop(0, nf, back, 0)
    for n, (x, y) in enumerate(OWN):
        u = pre[:, 128 * n : 128 * (n + 1)]
        sig = jax.nn.sigmoid(u)
        bp[x, y] = (acc[:, 128 * n : 128 * (n + 1)] * (sig * (1.0 + u * (1.0 - sig)))).astype(BF)
    cells = [links(src, dst, device) for (src, dst), device in zip(around(bp, bh), edges)]
    bh[inner, pair] = bp[...]

    grads = jnp.concatenate([bp[x, y] for x, y in OWN], axis=1)
    for j in range(9):
        sx, sy = j // 3, j % 3
        field = jnp.concatenate([v3o[(x + sx) * 4 + y + sy] for x, y in OWN], axis=1)
        g1w[192 * j : 192 * (j + 1)] = lax.dot_general(field, grads, NT, preferred_element_type=F32)
    g1w[1728:] = jnp.zeros((g1w.shape[0] - 1728, 128), F32)
    one = Summed(
        links, at, g1w, g1s, g1p, list(zip(ys, column)), g1q, g1y, ring, xl * nm + m, g1m, g1r, g1b
    )
    one.scatter()
    start(cells)

    wait(blocks)
    row = pl.ds(1, rows)
    planes = [links(vs.at[1, row], vs.at[depth + 1, row], prev), links(vs.at[depth, row], vs.at[0, row], after)]
    start(planes)
    vsr = vs.reshape((depth + 2) * wide, 64, 128)
    spread(vsr.at[pl.ds(wide, depth * wide)], v3.at[pl.ds(wide, depth * wide)], False)
    lot = min(8, rows)
    times = rows // lot

    def first(i, carry):
        x, y = i // times, lax.rem(i, times) * lot
        value = jnp.dot(
            w1t[...], columns(v3, wide, [(x, y + j) for j in range(lot)], False, 0), preferred_element_type=F32
        )
        hidden = (value * jax.nn.sigmoid(value)).astype(BF)
        for j in range(lot):
            hs[x * wide + y + 1 + j] = hidden[:, 128 * j : 128 * (j + 1)]
        return carry

    lax.fori_loop(times, 3 * times, first, 0)
    wait(planes)

    @pl.when(s == 0)
    def _():
        vs[0] = jnp.zeros_like(vs[0])

    @pl.when(s == ns - 1)
    def _():
        vs[depth + 1] = jnp.zeros_like(vs[0])

    for plane in (0, depth + 1):
        span = pl.ds(plane * wide, wide)
        spread(vsr.at[span], v3.at[span], False)
    lax.fori_loop(0, times, first, 0)
    lax.fori_loop(3 * times, 4 * times, first, 0)

    one.columns()

    def second_weights(i, carry):
        x, y = i // times, lax.rem(i, times) * lot
        here = jnp.concatenate([hs[x * wide + y + j + 1] for j in range(lot)], axis=1)
        field = columns(x3, wide, [(x, y + j) for j in range(lot)], True, 32)
        g2w[...] += lax.dot_general(field, here, NT, preferred_element_type=F32)
        return carry

    lax.fori_loop(0, 2 * times, second_weights, 0)
    one.rings()
    lax.fori_loop(2 * times, 4 * times, second_weights, 0)
    other = Summed(links, at, g2w, g2s, g2p, [], None, None, other_sample, m, g2m, g2r, g2b)
    other.scatter()
    one.back()

    def second(i, carry):
        x, y = i // (rows // 4), lax.rem(i, rows // 4) * 4
        field = jnp.concatenate(
            [jnp.concatenate([hs[x * wide + y + j + sy] for j in range(4)], axis=1) for sy in range(3)],
            axis=0,
        )
        value = jnp.dot(wm[...], field, preferred_element_type=F32)
        lane = lax.broadcasted_iota(jnp.int32, (32, 128), 1)
        for sx in range(3):
            for j in range(4):
                lanes = slice(128 * j, 128 * (j + 1))
                base = 96 * sx
                below = pltpu.roll(value[base : base + 32, lanes], 1, 1)
                above = pltpu.roll(value[base + 64 : base + 96, lanes], 127, 1)
                me[(x + 2 - sx) * rows + y + j] += (
                    jnp.where(lane == 0, 0.0, below)
                    + value[base + 32 : base + 64, lanes]
                    + jnp.where(lane == 127, 0.0, above)
                )
        return carry

    turn = rows // 4
    lax.fori_loop(0, 2 * turn, second, 0)
    one.spread()
    other.rings()
    lax.fori_loop(2 * turn, 4 * turn, second, 0)
    other.back()
    other.spread()
    outer = [
        links(me.at[pl.ds(0, rows)], mr.at[1], prev),
        links(me.at[pl.ds((depth + 1) * rows, rows)], mr.at[0], after),
    ]
    start(outer)

    wait(cells)
    clear_outside(bh, at)
    spread(bh.reshape((depth + 2) * 4, 128, 128), b3, True)
    for part_at in range(2):
        lanes = pl.ds(512 * part_at, 512)
        vg[:, lanes] = jnp.dot(
            w1v[...], columns(b3, 4, OWN[4 * part_at : 4 * part_at + 4], True, 0), preferred_element_type=F32
        )
    mo[...] = me[pl.ds(rows, depth * rows)]
    wait(outer)

    @pl.when(s > 0)
    def _():
        mo[pl.ds(0, rows)] += mr[0]

    @pl.when(s < ns - 1)
    def _():
        mo[pl.ds((depth - 1) * rows, rows)] += mr[1]

    other.finish()
    g2o[...] = g2b[0:864].astype(F32) * scaling
    one.finish()
    g1o[...] = g1b[0:1728].astype(F32) * scaling


def on_device(volume, weight_first, weight_second, cotangent):
    ns, nf, nm = lax.axis_size("spatial"), lax.axis_size("filter"), lax.axis_size("sample")
    depth, rows = DEPTH, 2 * nf
    wide = rows + 2
    scaling = 1.0 / math.sqrt(nm * depth * ns * rows * 128)

    vt = volume[0].transpose(1, 2, 0, 3)
    ct = jnp.pad(cotangent[0].transpose(1, 2, 0, 3), ((0, 0), (1, 1), (0, 0), (0, 0)))
    wlt = weight_second.transpose(0, 2, 1).reshape(864, 128)
    w1 = weight_first.reshape(1728, 128)

    columns_of = nf // 2
    step1 = -(-1728 // (16 * ns * columns_of)) * 16
    len1, len2 = step1 * columns_of, 896 // ns
    slab = (depth + 2) * wide
    scratch = [
        ((depth + 2, wide, 64, 128), BF), ((depth + 2, 4, 64, 128), BF), ((depth + 2, wide, 32, 128), BF),
        ((nf, depth + 2, 4, 32, 128), BF), ((2, rows, 32, 128), BF), ((max(nf // 2 - 1, 1), 2, 6, 32, 128), BF), ((nf, 128, 896), BF),
        ((slab, 192, 128), BF), ((nf, 24, 96, 128), BF), ((slab, 96, 128), BF),
        ((depth * wide, 128, 128), BF), ((128, 1024), F32), ((128, 1024), F32),
        ((128, 1728), BF), ((64, 3456), BF), ((288, 384), BF),
        (((depth + 2) * rows, 32, 128), F32), ((2, rows, 32, 128), F32),
        ((depth, 2, 128, 128), BF), ((depth + 2, 4, 128, 128), BF), ((24, 384, 128), BF),
        ((24, 192, 128), BF), ((128, 896), BF),
        ((ns * len1, 128), F32), ((ns * len1, 128), BF), ((ns - 1, len1, 128), BF), ((len1, 128), F32),
        ((max(columns_of - 1, 1), step1, 128), F32), ((step1, 128), F32), ((2 * nm, step1, 128), F32), ((ns * len1, 128), BF),
        ((ns * len2, 128), F32), ((ns * len2, 128), BF), ((ns - 1, len2, 128), BF),
        ((len2, 128), F32), ((nm, len2, 128), F32), ((ns * len2, 128), BF),
    ]
    copies = 160
    mo, g2o, g1o, vg = pl.pallas_call(
        functools.partial(whole_step, scaling),
        out_shape=[
            jax.ShapeDtypeStruct((depth * rows, 32, 128), F32),
            jax.ShapeDtypeStruct((864, 128), F32),
            jax.ShapeDtypeStruct((1728, 128), F32),
            jax.ShapeDtypeStruct((64, 1024), F32),
        ],
        in_specs=[VMEM] * 4,
        out_specs=[VMEM] * 4,
        scratch_shapes=[pltpu.VMEM(shape, dtype) for shape, dtype in scratch] + [dma(copies), dma(copies)],
        compiler_params=pltpu.CompilerParams(
            vmem_limit_bytes=LIMIT, collective_id=0, has_side_effects=True
        ),
    )(vt, ct, wlt, w1)
    mapped = mo.reshape(depth, rows, 32, 128).transpose(2, 0, 1, 3)[None]
    return (mapped, g2o.reshape(27, 32, 128).transpose(0, 2, 1), g1o.reshape(27, 64, 128), vg.reshape(1, 64, depth, 2, 128))


def solution(mesh):
    placed = (
        P("sample", None, "spatial", "filter", None),
        P(),
        P(None, None, "filter"),
        P("sample", "filter", "spatial", None, None),
    )
    return jax.shard_map(
        on_device,
        mesh=mesh,
        in_specs=placed,
        out_specs=(
            P("sample", "filter", "spatial", None, None),
            P(None, None, "filter"),
            P(),
            P("sample", None, "spatial", "filter", None),
        ),
        check_vma=False,
    )
```

```python
import functools
import math

import jax
import jax.numpy as jnp
from jax import lax
from jax.experimental import pallas as pl
from jax.experimental.pallas import tpu as pltpu
from jax.sharding import PartitionSpec as P

MESH = pl.DeviceIdType.MESH
BF = jnp.bfloat16
F32 = jnp.float32
VMEM = pl.BlockSpec(memory_space=pltpu.VMEM)
LIMIT = 56 * 1024 * 1024


def remote(src, dst, send, recv, device):
    return pltpu.make_async_remote_copy(
        src_ref=src, dst_ref=dst, send_sem=send, recv_sem=recv, device_id=device, device_id_type=MESH
    )


def greet(partners):
    barrier = pltpu.get_barrier_semaphore()
    for partner in partners:
        pl.semaphore_signal(barrier, inc=1, device_id=partner, device_id_type=MESH)
    pl.semaphore_wait(barrier, len(partners))


def places():
    ns, nf, nm = lax.axis_size("spatial"), lax.axis_size("filter"), lax.axis_size("sample")
    s, f, m = lax.axis_index("spatial"), lax.axis_index("filter"), lax.axis_index("sample")
    return ns, nf, nm, s, f, m


def dma(n):
    return pltpu.SemaphoreType.DMA((n,))


def shifted(cells):
    wide = cells.astype(F32)
    lane = lax.broadcasted_iota(jnp.int32, wide.shape, 1)
    below = jnp.where(lane == 0, 0.0, pltpu.roll(wide, 1, 1)).astype(BF)
    above = jnp.where(lane == 127, 0.0, pltpu.roll(wide, 127, 1)).astype(BF)
    return below, cells, above


def spread(src, dst, flip):
    count, channels, _ = src.shape
    step = 6 if count % 6 == 0 else 4

    def body(i, carry):
        for u in range(step):
            below, here, above = shifted(src[i * step + u])
            first, last = (above, below) if flip else (below, above)
            dst[i * step + u, pl.ds(0, channels)] = first
            dst[i * step + u, pl.ds(channels, channels)] = here
            dst[i * step + u, pl.ds(2 * channels, channels)] = last
        return carry

    lax.fori_loop(0, count // step, body, 0)


def columns(ref, wide, rows_at, flip, pad):
    stack = []
    for sx in range(3):
        for sy in range(3):
            ox, oy = (2 - sx, 2 - sy) if flip else (sx, sy)
            stack.append(jnp.concatenate([ref[(x + ox) * wide + (y + oy)] for x, y in rows_at], axis=1))
    if pad:
        stack.append(jnp.zeros((pad, 128 * len(rows_at)), BF))
    return jnp.concatenate(stack, axis=0)


NT = (((1,), (1,)), ((), ()))


class Links:
    def __init__(self, send, recv):
        self.send, self.recv, self.used = send, recv, 0

    def __call__(self, src, dst, device):
        n = self.used
        self.used += 1
        return remote(src, dst, self.send.at[n], self.recv.at[n], device)


def start(copies):
    for copy in copies:
        copy.start()


def wait(copies):
    for copy in copies:
        copy.wait()


def zero(ref):
    ref[...] = jnp.zeros(ref.shape, ref.dtype)


class Summed:
    def __init__(self, links, at, whole, rounded, arrived, column, split, split_in, ring, place, mine, ring_in, held):
        self.links, self.at, self.whole, self.rounded, self.arrived = links, at, whole, rounded, arrived
        self.column, self.split, self.split_in = column, split, split_in
        self.ring, self.place, self.mine, self.ring_in, self.held = ring, place, mine, ring_in, held
        self.rows, self.step = arrived.shape[1], mine.shape[0]

    def scatter(self):
        ns, nf, nm, s, f, m = self.at
        self.rounded[...] = self.whole[...].astype(BF)
        self.targets, self.moving = [], []
        for r in range(1, ns):
            j = lax.rem(s + r, ns)
            self.targets.append({"spatial": j})
            self.moving.append(
                self.links(self.rounded.at[pl.ds(j * self.rows, self.rows)], self.arrived.at[r - 1], {"spatial": j})
            )
        start(self.moving)

    def spatial_sum(self):
        wait(self.moving)
        value = self.whole[pl.ds(self.at[3] * self.rows, self.rows)]
        for r in range(len(self.targets)):
            value = value + self.arrived[r].astype(F32)
        return value

    def columns(self):
        self.split[...] = self.spatial_sum()
        self.moving = [
            self.links(self.split.at[pl.ds(y * self.step, self.step)], self.split_in.at[i], device)
            for i, (y, device) in enumerate(self.column)
        ]
        start(self.moving)

    def rings(self):
        if self.split is None:
            value = self.spatial_sum()
        else:
            wait(self.moving)
            value = self.split[pl.ds(self.at[4] // 2 * self.step, self.step)]
            for i in range(len(self.column)):
                value = value + self.split_in[i]
        self.mine[...] = value
        self.ring_in[self.place] = value
        self.moving = [self.links(self.mine, self.ring_in.at[self.place], device) for device in self.ring]
        start(self.moving)

    def back(self):
        wait(self.moving)
        value = self.ring_in[0]
        for i in range(1, self.ring_in.shape[0]):
            value = value + self.ring_in[i]
        base = self.at[3] * self.rows
        self.block = pl.ds(base, self.rows)
        if self.split is not None:
            here = pl.ds(base + self.at[4] // 2 * self.step, self.step)
            self.held[here] = value.astype(BF)
            self.moving = [self.links(self.held.at[here], self.held.at[here], device) for y, device in self.column]
            start(self.moving)
        else:
            self.held[self.block] = value.astype(BF)
            self.moving = []

    def spread(self):
        wait(self.moving)
        self.moving = [self.links(self.held.at[self.block], self.held.at[self.block], device) for device in self.targets]
        start(self.moving)

    def finish(self):
        wait(self.moving)


DEPTH = 4


def around(block, padded):
    body, inner, two, pair = pl.ds(0, DEPTH), pl.ds(1, DEPTH), pl.ds(0, 2), pl.ds(1, 2)
    last = DEPTH - 1
    return [
        (block.at[body, 0], padded.at[inner, 3]), (block.at[body, 1], padded.at[inner, 0]),
        (block.at[0, two], padded.at[DEPTH + 1, pair]), (block.at[last, two], padded.at[0, pair]),
        (block.at[0, 0], padded.at[DEPTH + 1, 3]), (block.at[0, 1], padded.at[DEPTH + 1, 0]),
        (block.at[last, 0], padded.at[0, 3]), (block.at[last, 1], padded.at[0, 0]),
    ]


def clear_outside(padded, at):
    ns, nf, nm, s, f, m = at
    for place, end, plane in ((s, 0, 0), (s, ns - 1, DEPTH + 1)):
        @pl.when(place == end)
        def _():
            padded[plane] = jnp.zeros_like(padded[plane])
    for place, end, row in ((f, 0, 0), (f, nf - 1, 3)):
        @pl.when(place == end)
        def _():
            padded[:, row] = jnp.zeros_like(padded[:, row])


OWN = [(x, y) for x in range(DEPTH) for y in range(2)]


def whole_step(
    scaling, vt, ct, wlt, w1, mo, g2o, g1o, vg,
    vs, vo, cx, cg, cp, cy, wg, v3, c3, x3, hs, pre, acc, w1t, w1v, wm, me, mr, bp, bh, b3, v3o, wl,
    g1w, g1s, g1p, g1q, g1y, g1m, g1r, g1b, g2w, g2s, g2p, g2m, g2r, g2b, send, recv,
):
    at = ns, nf, nm, s, f, m = places()
    links = Links(send, recv)
    depth, rows = DEPTH, 2 * nf
    wide = rows + 2
    part = 128 // ns
    nz = ns // 2
    core, z = lax.rem(s, 2), s // 2
    down, up = lax.rem(s + ns - 1, ns), lax.rem(s + 1, ns)
    left, right = lax.rem(f + nf - 1, nf), lax.rem(f + 1, nf)
    prev, after = {"spatial": down}, {"spatial": up}
    peers = [lax.rem(f + r, nf) for r in range(1, nf)]
    edges = [
        {"filter": left}, {"filter": right}, prev, after,
        {"spatial": down, "filter": left}, {"spatial": down, "filter": right},
        {"spatial": up, "filter": left}, {"spatial": up, "filter": right},
    ]
    ring = []
    for i in range(1, 2 * nm):
        j = lax.rem(lax.rem(f, 2) * nm + m + i, 2 * nm)
        ring.append({"filter": f - lax.rem(f, 2) + j // nm, "sample": lax.rem(j, nm)})
    other_sample = [{"sample": lax.rem(m + i, nm)} for i in range(1, nm)]
    group = [{"spatial": lax.rem(s + r, ns)} for r in range(1, ns)] + ring
    wl[...] = jnp.concatenate([wlt[...], jnp.zeros((32, 128), BF)], axis=0).T
    greet([{"filter": p} for p in peers] + edges[4:] + group)

    inner, body, two, pair = pl.ds(1, depth), pl.ds(0, depth), pl.ds(0, 2), pl.ds(1, 2)
    block = pl.ds(1 + 2 * f, 2)
    ny = nf // 2
    xl, yy = lax.rem(f, 2), f // 2
    fx = f + 1 - 2 * xl
    partner = {"filter": fx}
    ys = [lax.rem(yy + r, ny) for r in range(1, ny)]
    sources = [2 * lax.rem(yy + ny - r, ny) + xl for r in range(1, ny)]
    column = [{"filter": 2 * y + xl} for y in ys]
    lo, hi, glo, ghi = pl.ds(0, 2), pl.ds(2, 2), pl.ds(1, 2), pl.ds(3, 2)
    vol_x = links(vt, vs.at[inner, block], partner)
    vol_y = [links(vt, vs.at[inner, block], device) for device in column]
    mine = pl.ds(s * part, part)
    halo = [links(ct.at[0], cx.at[depth + 1], prev), links(ct.at[depth - 1], cx.at[0], after)]
    weights = [links(wl.at[mine], wg.at[f, mine], {"filter": p}) for p in peers]
    cot_x = links(ct.at[lo, pl.ds(2 - 2 * xl, rows)], cp, partner)
    cot_y = [links(ct.at[hi, pl.ds(4 * y, 6)], cy.at[i], column[i]) for i, y in enumerate(ys)]
    cots = [links(ct.at[hi, pl.ds(2 * fx, 4)], cg.at[f, ghi], partner)]
    cots += [links(ct.at[lo, pl.ds(4 * y + 2 * xl, 4)], cg.at[f, glo], column[i]) for i, y in enumerate(ys)]
    corners = [links(src, dst, device) for (src, dst), device in zip(around(vt, vo), edges)]
    for copies in (weights, [cot_x], cot_y, cots, corners, halo):
        start(copies)

    vs[:, 0] = jnp.zeros_like(vs[:, 0])
    vs[:, rows + 1] = jnp.zeros_like(vs[:, 0])
    vs[inner, block] = vt[...]
    cx[inner] = ct[...]
    cg[f, inner] = ct[:, pl.ds(2 * f, 4)]
    wg[f, mine] = wl[mine]
    w1t[...] = w1[...].T
    for sx in range(3):
        for sy in range(3):
            for sz in range(3):
                k = sx * 9 + sy * 3 + sz
                w1v[:, 128 * k : 128 * (k + 1)] = w1[64 * k : 64 * (k + 1)]
                j = 32 * (sx * 3 + sz)
                wm[j : j + 32, 128 * sy : 128 * (sy + 1)] = wlt[32 * k : 32 * (k + 1)]
    zero(hs)
    zero(me)
    zero(acc)
    zero(g2w)

    wait(weights)
    along = [
        links(wg.at[:, mine], wg.at[:, mine], {"spatial": lax.rem(z + r, nz) * 2 + core}) for r in range(1, nz)
    ]
    start(along)

    cot_x.wait()
    onward = [links(cp.at[:, pl.ds(4 * y, 4)], cg.at[fx, glo], column[i]) for i, y in enumerate(ys)]
    start(onward)
    cots += onward
    cg[fx, glo] = cp[:, pl.ds(4 * yy, 4)]
    for i, k in enumerate(sources):
        cot_y[i].wait()
        onward = links(cy.at[i, :, pl.ds(2 - 2 * xl, 4)], cg.at[k, ghi], partner)
        onward.start()
        cots.append(onward)
        cg[k, ghi] = cy[i, :, pl.ds(2 * xl, 4)]

    start([vol_x] + vol_y)

    wait(halo)

    @pl.when(s == 0)
    def _():
        cx[0] = jnp.zeros_like(cx[0])

    @pl.when(s == ns - 1)
    def _():
        cx[depth + 1] = jnp.zeros_like(cx[0])

    cxr = cx.reshape((depth + 2) * wide, 32, 128)
    spread(cxr, x3, True)
    wait(corners)
    vo[inner, pair] = vt[...]
    clear_outside(vo, at)
    spread(vo.reshape((depth + 2) * 4, 64, 128), v3o, False)
    for part_at in range(2):
        lanes = pl.ds(512 * part_at, 512)
        pre[:, lanes] = jnp.dot(
            w1t[...], columns(v3o, 4, OWN[4 * part_at : 4 * part_at + 4], False, 0), preferred_element_type=F32
        )

    wait(cots)
    forward = [links(cg.at[:, 1], cg.at[:, depth + 1], prev), links(cg.at[:, depth], cg.at[:, 0], after)]
    start(forward)
    cgr = cg.reshape(nf, (depth + 2) * 4, 32, 128)

    def inside(k, carry):
        spread(cgr.at[k, pl.ds(4, 4 * depth)], c3.at[k, pl.ds(4, 4 * depth)], True)
        return carry

    lax.fori_loop(0, nf, inside, 0)
    vol_x.wait()
    over = pl.ds(1 + 2 * fx, 2)
    blocks = [links(vs.at[glo, over], vs.at[glo, over], device) for device in column]
    start(blocks)
    for copy, k in zip(vol_y, sources):
        copy.wait()
        there = pl.ds(1 + 2 * k, 2)
        onward = links(vs.at[ghi, there], vs.at[ghi, there], partner)
        onward.start()
        blocks.append(onward)
    wait(along)
    across = []
    for k in range(nz):
        piece = pl.ds((2 * k + core) * part, part)
        across.append(links(wg.at[:, piece], wg.at[:, piece], {"spatial": s + 1 - 2 * core}))
    start(across)
    wait(across)
    wait(forward)

    @pl.when(s == 0)
    def _():
        cg[:, 0] = jnp.zeros_like(cg[:, 0])

    @pl.when(s == ns - 1)
    def _():
        cg[:, depth + 1] = jnp.zeros_like(cg[:, 0])

    wait(blocks)
    row = pl.ds(1, rows)
    planes = [links(vs.at[1, row], vs.at[depth + 1, row], prev), links(vs.at[depth, row], vs.at[0, row], after)]
    start(planes)
    def back(k, carry):
        for plane in (0, depth + 1):
            span = pl.ds(4 * plane, 4)
            spread(cgr.at[k, span], c3.at[k, span], True)
        for part_at in range(2):
            lanes = pl.ds(512 * part_at, 512)
            acc[:, lanes] += jnp.dot(
                wg[k], columns(c3.at[k], 4, OWN[4 * part_at : 4 * part_at + 4], True, 32), preferred_element_type=F32
            )
        return carry

    lax.fori_loop(0, nf, back, 0)
    for n, (x, y) in enumerate(OWN):
        u = pre[:, 128 * n : 128 * (n + 1)]
        sig = jax.nn.sigmoid(u)
        bp[x, y] = (acc[:, 128 * n : 128 * (n + 1)] * (sig * (1.0 + u * (1.0 - sig)))).astype(BF)
    cells = [links(src, dst, device) for (src, dst), device in zip(around(bp, bh), edges)]
    bh[inner, pair] = bp[...]

    grads = jnp.concatenate([bp[x, y] for x, y in OWN], axis=1)
    for j in range(9):
        sx, sy = j // 3, j % 3
        field = jnp.concatenate([v3o[(x + sx) * 4 + y + sy] for x, y in OWN], axis=1)
        g1w[192 * j : 192 * (j + 1)] = lax.dot_general(field, grads, NT, preferred_element_type=F32)
    g1w[1728:] = jnp.zeros((g1w.shape[0] - 1728, 128), F32)
    one = Summed(
        links, at, g1w, g1s, g1p, list(zip(ys, column)), g1q, g1y, ring, xl * nm + m, g1m, g1r, g1b
    )
    one.scatter()
    start(cells)

    vsr = vs.reshape((depth + 2) * wide, 64, 128)
    spread(vsr.at[pl.ds(wide, depth * wide)], v3.at[pl.ds(wide, depth * wide)], False)
    lot = min(8, rows)
    times = rows // lot

    def first(i, carry):
        x, y = i // times, lax.rem(i, times) * lot
        value = jnp.dot(
            w1t[...], columns(v3, wide, [(x, y + j) for j in range(lot)], False, 0), preferred_element_type=F32
        )
        hidden = (value * jax.nn.sigmoid(value)).astype(BF)
        for j in range(lot):
            hs[x * wide + y + 1 + j] = hidden[:, 128 * j : 128 * (j + 1)]
        return carry

    lax.fori_loop(times, 3 * times, first, 0)
    wait(planes)

    @pl.when(s == 0)
    def _():
        vs[0] = jnp.zeros_like(vs[0])

    @pl.when(s == ns - 1)
    def _():
        vs[depth + 1] = jnp.zeros_like(vs[0])

    for plane in (0, depth + 1):
        span = pl.ds(plane * wide, wide)
        spread(vsr.at[span], v3.at[span], False)
    lax.fori_loop(0, times, first, 0)
    lax.fori_loop(3 * times, 4 * times, first, 0)

    one.columns()

    def second_weights(i, carry):
        x, y = i // times, lax.rem(i, times) * lot
        here = jnp.concatenate([hs[x * wide + y + j + 1] for j in range(lot)], axis=1)
        field = columns(x3, wide, [(x, y + j) for j in range(lot)], True, 32)
        g2w[...] += lax.dot_general(field, here, NT, preferred_element_type=F32)
        return carry

    lax.fori_loop(0, 2 * times, second_weights, 0)
    one.rings()
    lax.fori_loop(2 * times, 4 * times, second_weights, 0)
    other = Summed(links, at, g2w, g2s, g2p, [], None, None, other_sample, m, g2m, g2r, g2b)
    other.scatter()
    one.back()

    def second(i, carry):
        x, y = i // (rows // 4), lax.rem(i, rows // 4) * 4
        field = jnp.concatenate(
            [jnp.concatenate([hs[x * wide + y + j + sy] for j in range(4)], axis=1) for sy in range(3)],
            axis=0,
        )
        value = jnp.dot(wm[...], field, preferred_element_type=F32)
        lane = lax.broadcasted_iota(jnp.int32, (32, 128), 1)
        for sx in range(3):
            for j in range(4):
                lanes = slice(128 * j, 128 * (j + 1))
                base = 96 * sx
                below = pltpu.roll(value[base : base + 32, lanes], 1, 1)
                above = pltpu.roll(value[base + 64 : base + 96, lanes], 127, 1)
                me[(x + 2 - sx) * rows + y + j] += (
                    jnp.where(lane == 0, 0.0, below)
                    + value[base + 32 : base + 64, lanes]
                    + jnp.where(lane == 127, 0.0, above)
                )
        return carry

    turn = rows // 4
    lax.fori_loop(0, 2 * turn, second, 0)
    one.spread()
    other.rings()
    lax.fori_loop(2 * turn, 4 * turn, second, 0)
    other.back()
    other.spread()
    outer = [
        links(me.at[pl.ds(0, rows)], mr.at[1], prev),
        links(me.at[pl.ds((depth + 1) * rows, rows)], mr.at[0], after),
    ]
    start(outer)

    wait(cells)
    clear_outside(bh, at)
    spread(bh.reshape((depth + 2) * 4, 128, 128), b3, True)
    for part_at in range(2):
        lanes = pl.ds(512 * part_at, 512)
        vg[:, lanes] = jnp.dot(
            w1v[...], columns(b3, 4, OWN[4 * part_at : 4 * part_at + 4], True, 0), preferred_element_type=F32
        )
    mo[...] = me[pl.ds(rows, depth * rows)]
    wait(outer)

    @pl.when(s > 0)
    def _():
        mo[pl.ds(0, rows)] += mr[0]

    @pl.when(s < ns - 1)
    def _():
        mo[pl.ds((depth - 1) * rows, rows)] += mr[1]

    other.finish()
    g2o[...] = g2b[0:864].astype(F32) * scaling
    one.finish()
    g1o[...] = g1b[0:1728].astype(F32) * scaling


def on_device(volume, weight_first, weight_second, cotangent):
    ns, nf, nm = lax.axis_size("spatial"), lax.axis_size("filter"), lax.axis_size("sample")
    depth, rows = DEPTH, 2 * nf
    wide = rows + 2
    scaling = 1.0 / math.sqrt(nm * depth * ns * rows * 128)

    vt = volume[0].transpose(1, 2, 0, 3)
    ct = jnp.pad(cotangent[0].transpose(1, 2, 0, 3), ((0, 0), (1, 1), (0, 0), (0, 0)))
    wlt = weight_second.transpose(0, 2, 1).reshape(864, 128)
    w1 = weight_first.reshape(1728, 128)

    columns_of = nf // 2
    step1 = -(-1728 // (16 * ns * columns_of)) * 16
    len1, len2 = step1 * columns_of, 896 // ns
    slab = (depth + 2) * wide
    scratch = [
        ((depth + 2, wide, 64, 128), BF), ((depth + 2, 4, 64, 128), BF), ((depth + 2, wide, 32, 128), BF),
        ((nf, depth + 2, 4, 32, 128), BF), ((2, rows, 32, 128), BF), ((max(nf // 2 - 1, 1), 2, 6, 32, 128), BF), ((nf, 128, 896), BF),
        ((slab, 192, 128), BF), ((nf, 24, 96, 128), BF), ((slab, 96, 128), BF),
        ((depth * wide, 128, 128), BF), ((128, 1024), F32), ((128, 1024), F32),
        ((128, 1728), BF), ((64, 3456), BF), ((288, 384), BF),
        (((depth + 2) * rows, 32, 128), F32), ((2, rows, 32, 128), F32),
        ((depth, 2, 128, 128), BF), ((depth + 2, 4, 128, 128), BF), ((24, 384, 128), BF),
        ((24, 192, 128), BF), ((128, 896), BF),
        ((ns * len1, 128), F32), ((ns * len1, 128), BF), ((ns - 1, len1, 128), BF), ((len1, 128), F32),
        ((max(columns_of - 1, 1), step1, 128), F32), ((step1, 128), F32), ((2 * nm, step1, 128), F32), ((ns * len1, 128), BF),
        ((ns * len2, 128), F32), ((ns * len2, 128), BF), ((ns - 1, len2, 128), BF),
        ((len2, 128), F32), ((nm, len2, 128), F32), ((ns * len2, 128), BF),
    ]
    copies = 160
    mo, g2o, g1o, vg = pl.pallas_call(
        functools.partial(whole_step, scaling),
        out_shape=[
            jax.ShapeDtypeStruct((depth * rows, 32, 128), F32),
            jax.ShapeDtypeStruct((864, 128), F32),
            jax.ShapeDtypeStruct((1728, 128), F32),
            jax.ShapeDtypeStruct((64, 1024), F32),
        ],
        in_specs=[VMEM] * 4,
        out_specs=[VMEM] * 4,
        scratch_shapes=[pltpu.VMEM(shape, dtype) for shape, dtype in scratch] + [dma(copies), dma(copies)],
        compiler_params=pltpu.CompilerParams(
            vmem_limit_bytes=LIMIT, collective_id=0, has_side_effects=True
        ),
    )(vt, ct, wlt, w1)
    mapped = mo.reshape(depth, rows, 32, 128).transpose(2, 0, 1, 3)[None]
    return (mapped, g2o.reshape(27, 32, 128).transpose(0, 2, 1), g1o.reshape(27, 64, 128), vg.reshape(1, 64, depth, 2, 128))


def solution(mesh):
    placed = (
        P("sample", None, "spatial", "filter", None),
        P(),
        P(None, None, "filter"),
        P("sample", "filter", "spatial", None, None),
    )
    return jax.shard_map(
        on_device,
        mesh=mesh,
        in_specs=placed,
        out_specs=(
            P("sample", "filter", "spatial", None, None),
            P(None, None, "filter"),
            P(),
            P("sample", None, "spatial", "filter", None),
        ),
        check_vma=False,
    )
```

```python
import functools
import math

import jax
import jax.numpy as jnp
from jax import lax
from jax.experimental import pallas as pl
from jax.experimental.pallas import tpu as pltpu
from jax.sharding import PartitionSpec as P

MESH = pl.DeviceIdType.MESH
BF = jnp.bfloat16
F32 = jnp.float32
VMEM = pl.BlockSpec(memory_space=pltpu.VMEM)
LIMIT = 56 * 1024 * 1024


def remote(src, dst, send, recv, device):
    return pltpu.make_async_remote_copy(
        src_ref=src, dst_ref=dst, send_sem=send, recv_sem=recv, device_id=device, device_id_type=MESH
    )


def greet(partners):
    barrier = pltpu.get_barrier_semaphore()
    for partner in partners:
        pl.semaphore_signal(barrier, inc=1, device_id=partner, device_id_type=MESH)
    pl.semaphore_wait(barrier, len(partners))


def places():
    ns, nf, nm = lax.axis_size("spatial"), lax.axis_size("filter"), lax.axis_size("sample")
    s, f, m = lax.axis_index("spatial"), lax.axis_index("filter"), lax.axis_index("sample")
    return ns, nf, nm, s, f, m


def dma(n):
    return pltpu.SemaphoreType.DMA((n,))


def shifted(cells):
    wide = cells.astype(F32)
    lane = lax.broadcasted_iota(jnp.int32, wide.shape, 1)
    below = jnp.where(lane == 0, 0.0, pltpu.roll(wide, 1, 1)).astype(BF)
    above = jnp.where(lane == 127, 0.0, pltpu.roll(wide, 127, 1)).astype(BF)
    return below, cells, above


def spread(src, dst, flip):
    count, channels, _ = src.shape
    step = 6 if count % 6 == 0 else 4

    def body(i, carry):
        for u in range(step):
            below, here, above = shifted(src[i * step + u])
            first, last = (above, below) if flip else (below, above)
            dst[i * step + u, pl.ds(0, channels)] = first
            dst[i * step + u, pl.ds(channels, channels)] = here
            dst[i * step + u, pl.ds(2 * channels, channels)] = last
        return carry

    lax.fori_loop(0, count // step, body, 0)


def columns(ref, wide, rows_at, flip, pad):
    stack = []
    for sx in range(3):
        for sy in range(3):
            ox, oy = (2 - sx, 2 - sy) if flip else (sx, sy)
            stack.append(jnp.concatenate([ref[(x + ox) * wide + (y + oy)] for x, y in rows_at], axis=1))
    if pad:
        stack.append(jnp.zeros((pad, 128 * len(rows_at)), BF))
    return jnp.concatenate(stack, axis=0)


NT = (((1,), (1,)), ((), ()))


class Links:
    def __init__(self, send, recv):
        self.send, self.recv, self.used = send, recv, 0

    def __call__(self, src, dst, device):
        n = self.used
        self.used += 1
        return remote(src, dst, self.send.at[n], self.recv.at[n], device)


def start(copies):
    for copy in copies:
        copy.start()


def wait(copies):
    for copy in copies:
        copy.wait()


def zero(ref):
    ref[...] = jnp.zeros(ref.shape, ref.dtype)


class Summed:
    def __init__(self, links, at, whole, rounded, arrived, column, split, split_in, ring, place, mine, ring_in, held):
        self.links, self.at, self.whole, self.rounded, self.arrived = links, at, whole, rounded, arrived
        self.column, self.split, self.split_in = column, split, split_in
        self.ring, self.place, self.mine, self.ring_in, self.held = ring, place, mine, ring_in, held
        self.rows, self.step = arrived.shape[1], mine.shape[0]

    def scatter(self):
        ns, nf, nm, s, f, m = self.at
        self.rounded[...] = self.whole[...].astype(BF)
        self.targets, self.moving = [], []
        for r in range(1, ns):
            j = lax.rem(s + r, ns)
            self.targets.append({"spatial": j})
            self.moving.append(
                self.links(self.rounded.at[pl.ds(j * self.rows, self.rows)], self.arrived.at[r - 1], {"spatial": j})
            )
        start(self.moving)

    def spatial_sum(self):
        wait(self.moving)
        value = self.whole[pl.ds(self.at[3] * self.rows, self.rows)]
        for r in range(len(self.targets)):
            value = value + self.arrived[r].astype(F32)
        return value

    def columns(self):
        self.split[...] = self.spatial_sum()
        self.moving = [
            self.links(self.split.at[pl.ds(y * self.step, self.step)], self.split_in.at[i], device)
            for i, (y, device) in enumerate(self.column)
        ]
        start(self.moving)

    def rings(self):
        if self.split is None:
            value = self.spatial_sum()
        else:
            wait(self.moving)
            value = self.split[pl.ds(self.at[4] // 2 * self.step, self.step)]
            for i in range(len(self.column)):
                value = value + self.split_in[i]
        self.mine[...] = value
        self.ring_in[self.place] = value
        self.moving = [self.links(self.mine, self.ring_in.at[self.place], device) for device in self.ring]
        start(self.moving)

    def back(self):
        wait(self.moving)
        value = self.ring_in[0]
        for i in range(1, self.ring_in.shape[0]):
            value = value + self.ring_in[i]
        base = self.at[3] * self.rows
        self.block = pl.ds(base, self.rows)
        if self.split is not None:
            here = pl.ds(base + self.at[4] // 2 * self.step, self.step)
            self.held[here] = value.astype(BF)
            self.moving = [self.links(self.held.at[here], self.held.at[here], device) for y, device in self.column]
            start(self.moving)
        else:
            self.held[self.block] = value.astype(BF)
            self.moving = []

    def spread(self):
        wait(self.moving)
        self.moving = [self.links(self.held.at[self.block], self.held.at[self.block], device) for device in self.targets]
        start(self.moving)

    def finish(self):
        wait(self.moving)


DEPTH = 4


def around(block, padded):
    body, inner, two, pair = pl.ds(0, DEPTH), pl.ds(1, DEPTH), pl.ds(0, 2), pl.ds(1, 2)
    last = DEPTH - 1
    return [
        (block.at[body, 0], padded.at[inner, 3]), (block.at[body, 1], padded.at[inner, 0]),
        (block.at[0, two], padded.at[DEPTH + 1, pair]), (block.at[last, two], padded.at[0, pair]),
        (block.at[0, 0], padded.at[DEPTH + 1, 3]), (block.at[0, 1], padded.at[DEPTH + 1, 0]),
        (block.at[last, 0], padded.at[0, 3]), (block.at[last, 1], padded.at[0, 0]),
    ]


def clear_outside(padded, at):
    ns, nf, nm, s, f, m = at
    for place, end, plane in ((s, 0, 0), (s, ns - 1, DEPTH + 1)):
        @pl.when(place == end)
        def _():
            padded[plane] = jnp.zeros_like(padded[plane])
    for place, end, row in ((f, 0, 0), (f, nf - 1, 3)):
        @pl.when(place == end)
        def _():
            padded[:, row] = jnp.zeros_like(padded[:, row])


OWN = [(x, y) for x in range(DEPTH) for y in range(2)]


def whole_step(
    scaling, vtr, ctr, wlt, w1, mo, g2o, g1o, vg,
    vs, vo, cx, cg, cp, cy, wg, v3, c3, x3, hs, pre, acc, w1t, w1v, wm, me, mr, bp, bh, b3, v3o, wl, vt,
    g1w, g1s, g1p, g1q, g1y, g1m, g1r, g1b, g2w, g2s, g2p, g2m, g2r, g2b, send, recv,
):
    at = ns, nf, nm, s, f, m = places()
    links = Links(send, recv)
    depth, rows = DEPTH, 2 * nf
    wide = rows + 2
    part = 128 // ns
    nz = ns // 2
    core, z = lax.rem(s, 2), s // 2
    down, up = lax.rem(s + ns - 1, ns), lax.rem(s + 1, ns)
    left, right = lax.rem(f + nf - 1, nf), lax.rem(f + 1, nf)
    prev, after = {"spatial": down}, {"spatial": up}
    peers = [lax.rem(f + r, nf) for r in range(1, nf)]
    edges = [
        {"filter": left}, {"filter": right}, prev, after,
        {"spatial": down, "filter": left}, {"spatial": down, "filter": right},
        {"spatial": up, "filter": left}, {"spatial": up, "filter": right},
    ]
    ring = []
    for i in range(1, 2 * nm):
        j = lax.rem(lax.rem(f, 2) * nm + m + i, 2 * nm)
        ring.append({"filter": f - lax.rem(f, 2) + j // nm, "sample": lax.rem(j, nm)})
    other_sample = [{"sample": lax.rem(m + i, nm)} for i in range(1, nm)]
    group = [{"spatial": lax.rem(s + r, ns)} for r in range(1, ns)] + ring
    cx[:, 0] = jnp.zeros_like(cx[:, 0])
    cx[:, 2 * nf + 1] = jnp.zeros_like(cx[:, 0])
    for x in range(DEPTH):
        cx[x + 1, pl.ds(1, 2 * nf)] = jnp.swapaxes(ctr[:, pl.ds(x * 2 * nf, 2 * nf)].astype(F32), 0, 1).astype(BF)
    ct = cx.at[pl.ds(1, DEPTH)]
    vt[...] = jnp.swapaxes(vtr[...].astype(F32), 0, 1).astype(BF).reshape(DEPTH, 2, 64, 128)
    wl[...] = jnp.concatenate([wlt[...], jnp.zeros((32, 128), BF)], axis=0).T
    greet([{"filter": p} for p in peers] + edges[4:] + group)

    inner, body, two, pair = pl.ds(1, depth), pl.ds(0, depth), pl.ds(0, 2), pl.ds(1, 2)
    block = pl.ds(1 + 2 * f, 2)
    ny = nf // 2
    xl, yy = lax.rem(f, 2), f // 2
    fx = f + 1 - 2 * xl
    partner = {"filter": fx}
    ys = [lax.rem(yy + r, ny) for r in range(1, ny)]
    sources = [2 * lax.rem(yy + ny - r, ny) + xl for r in range(1, ny)]
    column = [{"filter": 2 * y + xl} for y in ys]
    lo, hi, glo, ghi = pl.ds(0, 2), pl.ds(2, 2), pl.ds(1, 2), pl.ds(3, 2)
    vol_x = links(vt, vs.at[inner, block], partner)
    vol_y = [links(vt, vs.at[inner, block], device) for device in column]
    mine = pl.ds(s * part, part)
    row = pl.ds(1, rows)
    halo = [links(ct.at[0, row], cx.at[depth + 1, row], prev), links(ct.at[depth - 1, row], cx.at[0, row], after)]
    weights = [links(wl.at[mine], wg.at[f, mine], {"filter": p}) for p in peers]
    cot_x = links(ct.at[lo, pl.ds(2 - 2 * xl, rows)], cp, partner)
    cot_y = [links(ct.at[hi, pl.ds(4 * y, 6)], cy.at[i], column[i]) for i, y in enumerate(ys)]
    cots = [links(ct.at[hi, pl.ds(2 * fx, 4)], cg.at[f, ghi], partner)]
    cots += [links(ct.at[lo, pl.ds(4 * y + 2 * xl, 4)], cg.at[f, glo], column[i]) for i, y in enumerate(ys)]
    corners = [links(src, dst, device) for (src, dst), device in zip(around(vt, vo), edges)]
    for copies in (weights, [cot_x], cot_y, cots, corners, halo):
        start(copies)

    vs[:, 0] = jnp.zeros_like(vs[:, 0])
    vs[:, rows + 1] = jnp.zeros_like(vs[:, 0])
    vs[inner, block] = vt[...]
    cg[f, inner] = ct[:, pl.ds(2 * f, 4)]
    wg[f, mine] = wl[mine]
    w1t[...] = w1[...].T
    for sx in range(3):
        for sy in range(3):
            for sz in range(3):
                k = sx * 9 + sy * 3 + sz
                w1v[:, 128 * k : 128 * (k + 1)] = w1[64 * k : 64 * (k + 1)]
                j = 32 * (sx * 3 + sz)
                wm[j : j + 32, 128 * sy : 128 * (sy + 1)] = wlt[32 * k : 32 * (k + 1)]
    zero(hs)
    zero(me)
    zero(acc)
    zero(g2w)

    wait(weights)
    along = [
        links(wg.at[:, mine], wg.at[:, mine], {"spatial": lax.rem(z + r, nz) * 2 + core}) for r in range(1, nz)
    ]
    start(along)

    cot_x.wait()
    onward = [links(cp.at[:, pl.ds(4 * y, 4)], cg.at[fx, glo], column[i]) for i, y in enumerate(ys)]
    start(onward)
    cots += onward
    cg[fx, glo] = cp[:, pl.ds(4 * yy, 4)]
    for i, k in enumerate(sources):
        cot_y[i].wait()
        onward = links(cy.at[i, :, pl.ds(2 - 2 * xl, 4)], cg.at[k, ghi], partner)
        onward.start()
        cots.append(onward)
        cg[k, ghi] = cy[i, :, pl.ds(2 * xl, 4)]

    start([vol_x] + vol_y)

    wait(halo)

    @pl.when(s == 0)
    def _():
        cx[0] = jnp.zeros_like(cx[0])

    @pl.when(s == ns - 1)
    def _():
        cx[depth + 1] = jnp.zeros_like(cx[0])

    cxr = cx.reshape((depth + 2) * wide, 32, 128)
    spread(cxr, x3, True)
    wait(corners)
    vo[inner, pair] = vt[...]
    clear_outside(vo, at)
    spread(vo.reshape((depth + 2) * 4, 64, 128), v3o, False)
    for part_at in range(2):
        lanes = pl.ds(512 * part_at, 512)
        pre[:, lanes] = jnp.dot(
            w1t[...], columns(v3o, 4, OWN[4 * part_at : 4 * part_at + 4], False, 0), preferred_element_type=F32
        )

    wait(cots)
    forward = [links(cg.at[:, 1], cg.at[:, depth + 1], prev), links(cg.at[:, depth], cg.at[:, 0], after)]
    start(forward)
    cgr = cg.reshape(nf, (depth + 2) * 4, 32, 128)

    def inside(k, carry):
        spread(cgr.at[k, pl.ds(4, 4 * depth)], c3.at[k, pl.ds(4, 4 * depth)], True)
        return carry

    lax.fori_loop(0, nf, inside, 0)
    vol_x.wait()
    over = pl.ds(1 + 2 * fx, 2)
    blocks = [links(vs.at[glo, over], vs.at[glo, over], device) for device in column]
    start(blocks)
    for copy, k in zip(vol_y, sources):
        copy.wait()
        there = pl.ds(1 + 2 * k, 2)
        onward = links(vs.at[ghi, there], vs.at[ghi, there], partner)
        onward.start()
        blocks.append(onward)
    wait(along)
    across = []
    for k in range(nz):
        piece = pl.ds((2 * k + core) * part, part)
        across.append(links(wg.at[:, piece], wg.at[:, piece], {"spatial": s + 1 - 2 * core}))
    start(across)
    wait(across)
    wait(forward)

    @pl.when(s == 0)
    def _():
        cg[:, 0] = jnp.zeros_like(cg[:, 0])

    @pl.when(s == ns - 1)
    def _():
        cg[:, depth + 1] = jnp.zeros_like(cg[:, 0])

    wait(blocks)
    row = pl.ds(1, rows)
    planes = [links(vs.at[1, row], vs.at[depth + 1, row], prev), links(vs.at[depth, row], vs.at[0, row], after)]
    start(planes)
    def back(k, carry):
        for plane in (0, depth + 1):
            span = pl.ds(4 * plane, 4)
            spread(cgr.at[k, span], c3.at[k, span], True)
        for part_at in range(2):
            lanes = pl.ds(512 * part_at, 512)
            acc[:, lanes] += jnp.dot(
                wg[k], columns(c3.at[k], 4, OWN[4 * part_at : 4 * part_at + 4], True, 32), preferred_element_type=F32
            )
        return carry

    lax.fori_loop(0, nf, back, 0)
    for n, (x, y) in enumerate(OWN):
        u = pre[:, 128 * n : 128 * (n + 1)]
        sig = jax.nn.sigmoid(u)
        bp[x, y] = (acc[:, 128 * n : 128 * (n + 1)] * (sig * (1.0 + u * (1.0 - sig)))).astype(BF)
    cells = [links(src, dst, device) for (src, dst), device in zip(around(bp, bh), edges)]
    bh[inner, pair] = bp[...]

    grads = jnp.concatenate([bp[x, y] for x, y in OWN], axis=1)
    for j in range(9):
        sx, sy = j // 3, j % 3
        field = jnp.concatenate([v3o[(x + sx) * 4 + y + sy] for x, y in OWN], axis=1)
        g1w[192 * j : 192 * (j + 1)] = lax.dot_general(field, grads, NT, preferred_element_type=F32)
    g1w[1728:] = jnp.zeros((g1w.shape[0] - 1728, 128), F32)
    one = Summed(
        links, at, g1w, g1s, g1p, list(zip(ys, column)), g1q, g1y, ring, xl * nm + m, g1m, g1r, g1b
    )
    one.scatter()
    start(cells)

    vsr = vs.reshape((depth + 2) * wide, 64, 128)
    spread(vsr.at[pl.ds(wide, depth * wide)], v3.at[pl.ds(wide, depth * wide)], False)
    lot = min(8, rows)
    times = rows // lot

    def first(i, carry):
        x, y = i // times, lax.rem(i, times) * lot
        value = jnp.dot(
            w1t[...], columns(v3, wide, [(x, y + j) for j in range(lot)], False, 0), preferred_element_type=F32
        )
        hidden = (value * jax.nn.sigmoid(value)).astype(BF)
        for j in range(lot):
            hs[x * wide + y + 1 + j] = hidden[:, 128 * j : 128 * (j + 1)]
        return carry

    lax.fori_loop(times, 3 * times, first, 0)
    wait(planes)

    @pl.when(s == 0)
    def _():
        vs[0] = jnp.zeros_like(vs[0])

    @pl.when(s == ns - 1)
    def _():
        vs[depth + 1] = jnp.zeros_like(vs[0])

    for plane in (0, depth + 1):
        span = pl.ds(plane * wide, wide)
        spread(vsr.at[span], v3.at[span], False)
    lax.fori_loop(0, times, first, 0)
    lax.fori_loop(3 * times, 4 * times, first, 0)

    one.columns()

    def second_weights(i, carry):
        x, y = i // times, lax.rem(i, times) * lot
        here = jnp.concatenate([hs[x * wide + y + j + 1] for j in range(lot)], axis=1)
        field = columns(x3, wide, [(x, y + j) for j in range(lot)], True, 32)
        g2w[...] += lax.dot_general(field, here, NT, preferred_element_type=F32)
        return carry

    lax.fori_loop(0, 2 * times, second_weights, 0)
    one.rings()
    lax.fori_loop(2 * times, 4 * times, second_weights, 0)
    other = Summed(links, at, g2w, g2s, g2p, [], None, None, other_sample, m, g2m, g2r, g2b)
    other.scatter()
    one.back()

    def second(i, carry):
        x, y = i // (rows // 4), lax.rem(i, rows // 4) * 4
        field = jnp.concatenate(
            [jnp.concatenate([hs[x * wide + y + j + sy] for j in range(4)], axis=1) for sy in range(3)],
            axis=0,
        )
        value = jnp.dot(wm[...], field, preferred_element_type=F32)
        lane = lax.broadcasted_iota(jnp.int32, (32, 128), 1)
        for sx in range(3):
            for j in range(4):
                lanes = slice(128 * j, 128 * (j + 1))
                base = 96 * sx
                below = pltpu.roll(value[base : base + 32, lanes], 1, 1)
                above = pltpu.roll(value[base + 64 : base + 96, lanes], 127, 1)
                me[(x + 2 - sx) * rows + y + j] += (
                    jnp.where(lane == 0, 0.0, below)
                    + value[base + 32 : base + 64, lanes]
                    + jnp.where(lane == 127, 0.0, above)
                )
        return carry

    turn = rows // 4
    lax.fori_loop(0, 2 * turn, second, 0)
    one.spread()
    other.rings()
    lax.fori_loop(2 * turn, 4 * turn, second, 0)
    other.back()
    other.spread()
    outer = [
        links(me.at[pl.ds(0, rows)], mr.at[1], prev),
        links(me.at[pl.ds((depth + 1) * rows, rows)], mr.at[0], after),
    ]
    start(outer)

    wait(cells)
    clear_outside(bh, at)
    spread(bh.reshape((depth + 2) * 4, 128, 128), b3, True)
    for part_at in range(2):
        value = jnp.dot(
            w1v[...], columns(b3, 4, OWN[4 * part_at : 4 * part_at + 4], True, 0), preferred_element_type=F32
        )
        for j in range(4):
            vg[:, 4 * part_at + j] = value[:, 128 * j : 128 * (j + 1)]
    wait(outer)

    @pl.when(s > 0)
    def _():
        me[pl.ds(rows, rows)] += mr[0]

    @pl.when(s < ns - 1)
    def _():
        me[pl.ds(depth * rows, rows)] += mr[1]

    for x in range(depth):
        mo[:, pl.ds(x * rows, rows)] = jnp.swapaxes(me[pl.ds((x + 1) * rows, rows)], 0, 1)
    other.finish()
    g2o[...] = g2b[0:864].astype(F32) * scaling
    one.finish()
    g1o[...] = g1b[0:1728].astype(F32) * scaling


def on_device(volume, weight_first, weight_second, cotangent):
    ns, nf, nm = lax.axis_size("spatial"), lax.axis_size("filter"), lax.axis_size("sample")
    depth, rows = DEPTH, 2 * nf
    wide = rows + 2
    scaling = 1.0 / math.sqrt(nm * depth * ns * rows * 128)

    vt = volume.reshape(64, 2 * depth, 128)
    ct = cotangent.reshape(32, depth * rows, 128)
    wlt = weight_second.transpose(0, 2, 1).reshape(864, 128)
    w1 = weight_first.reshape(1728, 128)

    columns_of = nf // 2
    step1 = -(-1728 // (16 * ns * columns_of)) * 16
    len1, len2 = step1 * columns_of, 896 // ns
    slab = (depth + 2) * wide
    scratch = [
        ((depth + 2, wide, 64, 128), BF), ((depth + 2, 4, 64, 128), BF), ((depth + 2, wide, 32, 128), BF),
        ((nf, depth + 2, 4, 32, 128), BF), ((2, rows, 32, 128), BF), ((max(nf // 2 - 1, 1), 2, 6, 32, 128), BF), ((nf, 128, 896), BF),
        ((slab, 192, 128), BF), ((nf, 24, 96, 128), BF), ((slab, 96, 128), BF),
        ((depth * wide, 128, 128), BF), ((128, 1024), F32), ((128, 1024), F32),
        ((128, 1728), BF), ((64, 3456), BF), ((288, 384), BF),
        (((depth + 2) * rows, 32, 128), F32), ((2, rows, 32, 128), F32),
        ((depth, 2, 128, 128), BF), ((depth + 2, 4, 128, 128), BF), ((24, 384, 128), BF),
        ((24, 192, 128), BF), ((128, 896), BF), ((depth, 2, 64, 128), BF),
        ((ns * len1, 128), F32), ((ns * len1, 128), BF), ((ns - 1, len1, 128), BF), ((len1, 128), F32),
        ((max(columns_of - 1, 1), step1, 128), F32), ((step1, 128), F32), ((2 * nm, step1, 128), F32), ((ns * len1, 128), BF),
        ((ns * len2, 128), F32), ((ns * len2, 128), BF), ((ns - 1, len2, 128), BF),
        ((len2, 128), F32), ((nm, len2, 128), F32), ((ns * len2, 128), BF),
    ]
    copies = 160
    mo, g2o, g1o, vg = pl.pallas_call(
        functools.partial(whole_step, scaling),
        out_shape=[
            jax.ShapeDtypeStruct((32, depth * rows, 128), F32),
            jax.ShapeDtypeStruct((864, 128), F32),
            jax.ShapeDtypeStruct((1728, 128), F32),
            jax.ShapeDtypeStruct((64, 2 * depth, 128), F32),
        ],
        in_specs=[VMEM] * 4,
        out_specs=[VMEM] * 4,
        scratch_shapes=[pltpu.VMEM(shape, dtype) for shape, dtype in scratch] + [dma(copies), dma(copies)],
        compiler_params=pltpu.CompilerParams(
            vmem_limit_bytes=LIMIT, collective_id=0, has_side_effects=True
        ),
    )(vt, ct, wlt, w1)
    mapped = mo.reshape(1, 32, depth, rows, 128)
    return (mapped, g2o.reshape(27, 32, 128).transpose(0, 2, 1), g1o.reshape(27, 64, 128), vg.reshape(1, 64, depth, 2, 128))


def solution(mesh):
    placed = (
        P("sample", None, "spatial", "filter", None),
        P(),
        P(None, None, "filter"),
        P("sample", "filter", "spatial", None, None),
    )
    return jax.shard_map(
        on_device,
        mesh=mesh,
        in_specs=placed,
        out_specs=(
            P("sample", "filter", "spatial", None, None),
            P(None, None, "filter"),
            P(),
            P("sample", None, "spatial", "filter", None),
        ),
        check_vma=False,
    )
```

```python
import functools
import math

import jax
import jax.numpy as jnp
from jax import lax
from jax.experimental import pallas as pl
from jax.experimental.pallas import tpu as pltpu
from jax.sharding import PartitionSpec as P

MESH = pl.DeviceIdType.MESH
BF = jnp.bfloat16
F32 = jnp.float32
VMEM = pl.BlockSpec(memory_space=pltpu.VMEM)
LIMIT = 56 * 1024 * 1024


def remote(src, dst, send, recv, device):
    return pltpu.make_async_remote_copy(
        src_ref=src, dst_ref=dst, send_sem=send, recv_sem=recv, device_id=device, device_id_type=MESH
    )


def greet(partners):
    barrier = pltpu.get_barrier_semaphore()
    for partner in partners:
        pl.semaphore_signal(barrier, inc=1, device_id=partner, device_id_type=MESH)
    pl.semaphore_wait(barrier, len(partners))


def places():
    ns, nf, nm = lax.axis_size("spatial"), lax.axis_size("filter"), lax.axis_size("sample")
    s, f, m = lax.axis_index("spatial"), lax.axis_index("filter"), lax.axis_index("sample")
    return ns, nf, nm, s, f, m


def dma(n):
    return pltpu.SemaphoreType.DMA((n,))


def shifted(cells):
    wide = cells.astype(F32)
    lane = lax.broadcasted_iota(jnp.int32, wide.shape, 1)
    below = jnp.where(lane == 0, 0.0, pltpu.roll(wide, 1, 1)).astype(BF)
    above = jnp.where(lane == 127, 0.0, pltpu.roll(wide, 127, 1)).astype(BF)
    return below, cells, above


def spread(src, dst, flip):
    count, channels, _ = src.shape
    step = 6 if count % 6 == 0 else 4

    def body(i, carry):
        for u in range(step):
            below, here, above = shifted(src[i * step + u])
            first, last = (above, below) if flip else (below, above)
            dst[i * step + u, pl.ds(0, channels)] = first
            dst[i * step + u, pl.ds(channels, channels)] = here
            dst[i * step + u, pl.ds(2 * channels, channels)] = last
        return carry

    lax.fori_loop(0, count // step, body, 0)


def columns(ref, wide, rows_at, flip, pad):
    stack = []
    for sx in range(3):
        for sy in range(3):
            ox, oy = (2 - sx, 2 - sy) if flip else (sx, sy)
            stack.append(jnp.concatenate([ref[(x + ox) * wide + (y + oy)] for x, y in rows_at], axis=1))
    if pad:
        stack.append(jnp.zeros((pad, 128 * len(rows_at)), BF))
    return jnp.concatenate(stack, axis=0)


NT = (((1,), (1,)), ((), ()))


class Links:
    def __init__(self, send, recv):
        self.send, self.recv, self.used = send, recv, 0

    def __call__(self, src, dst, device):
        n = self.used
        self.used += 1
        return remote(src, dst, self.send.at[n], self.recv.at[n], device)


def start(copies):
    for copy in copies:
        copy.start()


def wait(copies):
    for copy in copies:
        copy.wait()


def zero(ref):
    ref[...] = jnp.zeros(ref.shape, ref.dtype)


class Summed:
    def __init__(self, links, at, whole, rounded, arrived, column, split, split_in, ring, place, mine, ring_in, held):
        self.links, self.at, self.whole, self.rounded, self.arrived = links, at, whole, rounded, arrived
        self.column, self.split, self.split_in = column, split, split_in
        self.ring, self.place, self.mine, self.ring_in, self.held = ring, place, mine, ring_in, held
        self.rows, self.step = arrived.shape[1], mine.shape[0]

    def scatter(self):
        ns, nf, nm, s, f, m = self.at
        self.rounded[...] = self.whole[...].astype(BF)
        self.targets, self.moving = [], []
        for r in range(1, ns):
            j = lax.rem(s + r, ns)
            self.targets.append({"spatial": j})
            self.moving.append(
                self.links(self.rounded.at[pl.ds(j * self.rows, self.rows)], self.arrived.at[r - 1], {"spatial": j})
            )
        start(self.moving)

    def spatial_sum(self):
        wait(self.moving)
        value = self.whole[pl.ds(self.at[3] * self.rows, self.rows)]
        for r in range(len(self.targets)):
            value = value + self.arrived[r].astype(F32)
        return value

    def columns(self):
        self.split[...] = self.spatial_sum()
        self.moving = [
            self.links(self.split.at[pl.ds(y * self.step, self.step)], self.split_in.at[i], device)
            for i, (y, device) in enumerate(self.column)
        ]
        start(self.moving)

    def rings(self):
        if self.split is None:
            value = self.spatial_sum()
        else:
            wait(self.moving)
            value = self.split[pl.ds(self.at[4] // 2 * self.step, self.step)]
            for i in range(len(self.column)):
                value = value + self.split_in[i]
        self.mine[...] = value
        self.ring_in[self.place] = value
        self.moving = [self.links(self.mine, self.ring_in.at[self.place], device) for device in self.ring]
        start(self.moving)

    def back(self):
        wait(self.moving)
        value = self.ring_in[0]
        for i in range(1, self.ring_in.shape[0]):
            value = value + self.ring_in[i]
        base = self.at[3] * self.rows
        self.block = pl.ds(base, self.rows)
        if self.split is not None:
            here = pl.ds(base + self.at[4] // 2 * self.step, self.step)
            self.held[here] = value.astype(BF)
            self.moving = [self.links(self.held.at[here], self.held.at[here], device) for y, device in self.column]
            start(self.moving)
        else:
            self.held[self.block] = value.astype(BF)
            self.moving = []

    def spread(self):
        wait(self.moving)
        self.moving = [self.links(self.held.at[self.block], self.held.at[self.block], device) for device in self.targets]
        start(self.moving)

    def finish(self):
        wait(self.moving)


DEPTH = 4


def around(block, padded):
    body, inner, two, pair = pl.ds(0, DEPTH), pl.ds(1, DEPTH), pl.ds(0, 2), pl.ds(1, 2)
    last = DEPTH - 1
    return [
        (block.at[body, 0], padded.at[inner, 3]), (block.at[body, 1], padded.at[inner, 0]),
        (block.at[0, two], padded.at[DEPTH + 1, pair]), (block.at[last, two], padded.at[0, pair]),
        (block.at[0, 0], padded.at[DEPTH + 1, 3]), (block.at[0, 1], padded.at[DEPTH + 1, 0]),
        (block.at[last, 0], padded.at[0, 3]), (block.at[last, 1], padded.at[0, 0]),
    ]


def clear_outside(padded, at):
    ns, nf, nm, s, f, m = at
    for place, end, plane in ((s, 0, 0), (s, ns - 1, DEPTH + 1)):
        @pl.when(place == end)
        def _():
            padded[plane] = jnp.zeros_like(padded[plane])
    for place, end, row in ((f, 0, 0), (f, nf - 1, 3)):
        @pl.when(place == end)
        def _():
            padded[:, row] = jnp.zeros_like(padded[:, row])


OWN = [(x, y) for x in range(DEPTH) for y in range(2)]


def whole_step(
    scaling, vtr, ctr, wlt, w1, mo, g2o, g1o, vg,
    vs, vo, cx, cg, cp, cy, wg, v3, c3, x3, hs, pre, acc, w1t, w1v, wm, me, mr, bp, bh, b3, v3o, wl, vt,
    g1w, g1s, g1p, g1q, g1y, g1m, g1r, g1b, g2w, g2s, g2p, g2m, g2r, g2b, send, recv,
):
    at = ns, nf, nm, s, f, m = places()
    links = Links(send, recv)
    depth, rows = DEPTH, 2 * nf
    wide = rows + 2
    part = 128 // ns
    nz = ns // 2
    core, z = lax.rem(s, 2), s // 2
    down, up = lax.rem(s + ns - 1, ns), lax.rem(s + 1, ns)
    left, right = lax.rem(f + nf - 1, nf), lax.rem(f + 1, nf)
    prev, after = {"spatial": down}, {"spatial": up}
    peers = [lax.rem(f + r, nf) for r in range(1, nf)]
    edges = [
        {"filter": left}, {"filter": right}, prev, after,
        {"spatial": down, "filter": left}, {"spatial": down, "filter": right},
        {"spatial": up, "filter": left}, {"spatial": up, "filter": right},
    ]
    ring = []
    for i in range(1, 2 * nm):
        j = lax.rem(lax.rem(f, 2) * nm + m + i, 2 * nm)
        ring.append({"filter": f - lax.rem(f, 2) + j // nm, "sample": lax.rem(j, nm)})
    other_sample = [{"sample": lax.rem(m + i, nm)} for i in range(1, nm)]
    group = [{"spatial": lax.rem(s + r, ns)} for r in range(1, ns)] + ring
    cx[:, 0] = jnp.zeros_like(cx[:, 0])
    cx[:, 2 * nf + 1] = jnp.zeros_like(cx[:, 0])
    for x in range(DEPTH):
        cx[x + 1, pl.ds(1, 2 * nf)] = jnp.swapaxes(ctr[:, pl.ds(x * 2 * nf, 2 * nf)].astype(F32), 0, 1).astype(BF)
    ct = cx.at[pl.ds(1, DEPTH)]
    vt[...] = jnp.swapaxes(vtr[...].astype(F32), 0, 1).astype(BF).reshape(DEPTH, 2, 64, 128)
    wl[...] = jnp.concatenate([wlt[...], jnp.zeros((32, 128), BF)], axis=0).T
    greet([{"filter": p} for p in peers] + edges[4:] + group)

    inner, body, two, pair = pl.ds(1, depth), pl.ds(0, depth), pl.ds(0, 2), pl.ds(1, 2)
    block = pl.ds(1 + 2 * f, 2)
    ny = nf // 2
    xl, yy = lax.rem(f, 2), f // 2
    fx = f + 1 - 2 * xl
    partner = {"filter": fx}
    ys = [lax.rem(yy + r, ny) for r in range(1, ny)]
    sources = [2 * lax.rem(yy + ny - r, ny) + xl for r in range(1, ny)]
    column = [{"filter": 2 * y + xl} for y in ys]
    lo, hi, glo, ghi = pl.ds(0, 2), pl.ds(2, 2), pl.ds(1, 2), pl.ds(3, 2)
    vol_x = links(vt, vs.at[inner, block], partner)
    vol_y = [links(vt, vs.at[inner, block], device) for device in column]
    mine = pl.ds(s * part, part)
    row = pl.ds(1, rows)
    halo = [links(ct.at[0, row], cx.at[depth + 1, row], prev), links(ct.at[depth - 1, row], cx.at[0, row], after)]
    weights = [links(wl.at[mine], wg.at[f, mine], {"filter": p}) for p in peers]
    cot_x = links(ct.at[lo, pl.ds(2 - 2 * xl, rows)], cp, partner)
    cot_y = [links(ct.at[hi, pl.ds(4 * y, 6)], cy.at[i], column[i]) for i, y in enumerate(ys)]
    cots = [links(ct.at[hi, pl.ds(2 * fx, 4)], cg.at[f, ghi], partner)]
    cots += [links(ct.at[lo, pl.ds(4 * y + 2 * xl, 4)], cg.at[f, glo], column[i]) for i, y in enumerate(ys)]
    corners = [links(src, dst, device) for (src, dst), device in zip(around(vt, vo), edges)]
    for copies in (weights, [cot_x], cot_y, cots, corners, halo):
        start(copies)

    vs[:, 0] = jnp.zeros_like(vs[:, 0])
    vs[:, rows + 1] = jnp.zeros_like(vs[:, 0])
    vs[inner, block] = vt[...]
    cg[f, inner] = ct[:, pl.ds(2 * f, 4)]
    wg[f, mine] = wl[mine]
    w1t[...] = w1[...].T
    for sx in range(3):
        for sy in range(3):
            for sz in range(3):
                k = sx * 9 + sy * 3 + sz
                w1v[:, 128 * k : 128 * (k + 1)] = w1[64 * k : 64 * (k + 1)]
                j = 32 * (sx * 3 + sz)
                wm[j : j + 32, 128 * sy : 128 * (sy + 1)] = wlt[32 * k : 32 * (k + 1)]
    zero(hs)
    zero(me)
    zero(acc)
    zero(g2w)

    wait(weights)
    along = [
        links(wg.at[:, mine], wg.at[:, mine], {"spatial": lax.rem(z + r, nz) * 2 + core}) for r in range(1, nz)
    ]
    start(along)

    cot_x.wait()
    onward = [links(cp.at[:, pl.ds(4 * y, 4)], cg.at[fx, glo], column[i]) for i, y in enumerate(ys)]
    start(onward)
    cots += onward
    cg[fx, glo] = cp[:, pl.ds(4 * yy, 4)]
    for i, k in enumerate(sources):
        cot_y[i].wait()
        onward = links(cy.at[i, :, pl.ds(2 - 2 * xl, 4)], cg.at[k, ghi], partner)
        onward.start()
        cots.append(onward)
        cg[k, ghi] = cy[i, :, pl.ds(2 * xl, 4)]

    start([vol_x] + vol_y)

    wait(halo)

    @pl.when(s == 0)
    def _():
        cx[0] = jnp.zeros_like(cx[0])

    @pl.when(s == ns - 1)
    def _():
        cx[depth + 1] = jnp.zeros_like(cx[0])

    cxr = cx.reshape((depth + 2) * wide, 32, 128)
    spread(cxr, x3, True)
    wait(corners)
    vo[inner, pair] = vt[...]
    clear_outside(vo, at)
    spread(vo.reshape((depth + 2) * 4, 64, 128), v3o, False)
    for part_at in range(2):
        lanes = pl.ds(512 * part_at, 512)
        pre[:, lanes] = jnp.dot(
            w1t[...], columns(v3o, 4, OWN[4 * part_at : 4 * part_at + 4], False, 0), preferred_element_type=F32
        )

    wait(cots)
    forward = [links(cg.at[:, 1], cg.at[:, depth + 1], prev), links(cg.at[:, depth], cg.at[:, 0], after)]
    start(forward)
    cgr = cg.reshape(nf, (depth + 2) * 4, 32, 128)

    def inside(k, carry):
        spread(cgr.at[k, pl.ds(4, 4 * depth)], c3.at[k, pl.ds(4, 4 * depth)], True)
        return carry

    lax.fori_loop(0, nf, inside, 0)
    vol_x.wait()
    over = pl.ds(1 + 2 * fx, 2)
    blocks = [links(vs.at[glo, over], vs.at[glo, over], device) for device in column]
    start(blocks)
    for copy, k in zip(vol_y, sources):
        copy.wait()
        there = pl.ds(1 + 2 * k, 2)
        onward = links(vs.at[ghi, there], vs.at[ghi, there], partner)
        onward.start()
        blocks.append(onward)
    wait(along)
    across = []
    for k in range(nz):
        piece = pl.ds((2 * k + core) * part, part)
        across.append(links(wg.at[:, piece], wg.at[:, piece], {"spatial": s + 1 - 2 * core}))
    start(across)
    wait(across)
    wait(forward)

    @pl.when(s == 0)
    def _():
        cg[:, 0] = jnp.zeros_like(cg[:, 0])

    @pl.when(s == ns - 1)
    def _():
        cg[:, depth + 1] = jnp.zeros_like(cg[:, 0])

    wait(blocks)
    row = pl.ds(1, rows)
    planes = [links(vs.at[1, row], vs.at[depth + 1, row], prev), links(vs.at[depth, row], vs.at[0, row], after)]
    start(planes)
    def back(k, carry):
        for plane in (0, depth + 1):
            span = pl.ds(4 * plane, 4)
            spread(cgr.at[k, span], c3.at[k, span], True)
        for part_at in range(2):
            lanes = pl.ds(512 * part_at, 512)
            acc[:, lanes] += jnp.dot(
                wg[k], columns(c3.at[k], 4, OWN[4 * part_at : 4 * part_at + 4], True, 32), preferred_element_type=F32
            )
        return carry

    lax.fori_loop(0, nf, back, 0)
    for n, (x, y) in enumerate(OWN):
        u = pre[:, 128 * n : 128 * (n + 1)]
        sig = jax.nn.sigmoid(u)
        bp[x, y] = (acc[:, 128 * n : 128 * (n + 1)] * (sig * (1.0 + u * (1.0 - sig)))).astype(BF)
    cells = [links(src, dst, device) for (src, dst), device in zip(around(bp, bh), edges)]
    bh[inner, pair] = bp[...]

    grads = jnp.concatenate([bp[x, y] for x, y in OWN], axis=1)
    for j in range(9):
        sx, sy = j // 3, j % 3
        field = jnp.concatenate([v3o[(x + sx) * 4 + y + sy] for x, y in OWN], axis=1)
        g1w[192 * j : 192 * (j + 1)] = lax.dot_general(field, grads, NT, preferred_element_type=F32)
    g1w[1728:] = jnp.zeros((g1w.shape[0] - 1728, 128), F32)
    one = Summed(
        links, at, g1w, g1s, g1p, list(zip(ys, column)), g1q, g1y, ring, xl * nm + m, g1m, g1r, g1b
    )
    one.scatter()
    start(cells)

    vsr = vs.reshape((depth + 2) * wide, 64, 128)
    spread(vsr.at[pl.ds(wide, depth * wide)], v3.at[pl.ds(wide, depth * wide)], False)
    lot = min(8, rows)
    times = rows // lot

    def first(i, carry):
        x, y = i // times, lax.rem(i, times) * lot
        value = jnp.dot(
            w1t[...], columns(v3, wide, [(x, y + j) for j in range(lot)], False, 0), preferred_element_type=F32
        )
        hidden = (value * jax.nn.sigmoid(value)).astype(BF)
        for j in range(lot):
            hs[x * wide + y + 1 + j] = hidden[:, 128 * j : 128 * (j + 1)]
        return carry

    lax.fori_loop(times, 3 * times, first, 0)
    wait(planes)

    @pl.when(s == 0)
    def _():
        vs[0] = jnp.zeros_like(vs[0])

    @pl.when(s == ns - 1)
    def _():
        vs[depth + 1] = jnp.zeros_like(vs[0])

    for plane in (0, depth + 1):
        span = pl.ds(plane * wide, wide)
        spread(vsr.at[span], v3.at[span], False)
    lax.fori_loop(0, times, first, 0)
    lax.fori_loop(3 * times, 4 * times, first, 0)

    one.columns()

    def second_weights(i, carry):
        x, y = i // times, lax.rem(i, times) * lot
        here = jnp.concatenate([hs[x * wide + y + j + 1] for j in range(lot)], axis=1)
        field = columns(x3, wide, [(x, y + j) for j in range(lot)], True, 32)
        g2w[...] += lax.dot_general(field, here, NT, preferred_element_type=F32)
        return carry

    lax.fori_loop(0, 2 * times, second_weights, 0)
    one.rings()
    lax.fori_loop(2 * times, 4 * times, second_weights, 0)
    other = Summed(links, at, g2w, g2s, g2p, [], None, None, other_sample, m, g2m, g2r, g2b)
    other.scatter()
    one.back()

    def second(i, carry):
        x, y = i // (rows // 4), lax.rem(i, rows // 4) * 4
        field = jnp.concatenate(
            [jnp.concatenate([hs[x * wide + y + j + sy] for j in range(4)], axis=1) for sy in range(3)],
            axis=0,
        )
        value = jnp.dot(wm[...], field, preferred_element_type=F32)
        lane = lax.broadcasted_iota(jnp.int32, (32, 128), 1)
        for sx in range(3):
            for j in range(4):
                lanes = slice(128 * j, 128 * (j + 1))
                base = 96 * sx
                below = pltpu.roll(value[base : base + 32, lanes], 1, 1)
                above = pltpu.roll(value[base + 64 : base + 96, lanes], 127, 1)
                me[(x + 2 - sx) * rows + y + j] += (
                    jnp.where(lane == 0, 0.0, below)
                    + value[base + 32 : base + 64, lanes]
                    + jnp.where(lane == 127, 0.0, above)
                )
        return carry

    turn = rows // 4
    lax.fori_loop(0, 2 * turn, second, 0)
    one.spread()
    other.rings()
    lax.fori_loop(2 * turn, 4 * turn, second, 0)
    other.back()
    other.spread()
    outer = [
        links(me.at[pl.ds(0, rows)], mr.at[1], prev),
        links(me.at[pl.ds((depth + 1) * rows, rows)], mr.at[0], after),
    ]
    start(outer)

    wait(cells)
    clear_outside(bh, at)
    spread(bh.reshape((depth + 2) * 4, 128, 128), b3, True)
    for part_at in range(2):
        value = jnp.dot(
            w1v[...], columns(b3, 4, OWN[4 * part_at : 4 * part_at + 4], True, 0), preferred_element_type=F32
        )
        for j in range(4):
            vg[:, 4 * part_at + j] = value[:, 128 * j : 128 * (j + 1)]
    wait(outer)

    @pl.when(s > 0)
    def _():
        me[pl.ds(rows, rows)] += mr[0]

    @pl.when(s < ns - 1)
    def _():
        me[pl.ds(depth * rows, rows)] += mr[1]

    for x in range(depth):
        mo[:, pl.ds(x * rows, rows)] = jnp.swapaxes(me[pl.ds((x + 1) * rows, rows)], 0, 1)
    other.finish()
    g2o[...] = g2b[0:864].astype(F32) * scaling
    one.finish()
    g1o[...] = g1b[0:1728].astype(F32) * scaling


def on_device(volume, weight_first, weight_second, cotangent):
    ns, nf, nm = lax.axis_size("spatial"), lax.axis_size("filter"), lax.axis_size("sample")
    depth, rows = DEPTH, 2 * nf
    wide = rows + 2
    scaling = 1.0 / math.sqrt(nm * depth * ns * rows * 128)

    vt = volume.reshape(64, 2 * depth, 128)
    ct = cotangent.reshape(32, depth * rows, 128)
    wlt = weight_second.transpose(0, 2, 1).reshape(864, 128)
    w1 = weight_first.reshape(1728, 128)

    columns_of = nf // 2
    step1 = -(-1728 // (16 * ns * columns_of)) * 16
    len1, len2 = step1 * columns_of, 896 // ns
    slab = (depth + 2) * wide
    scratch = [
        ((depth + 2, wide, 64, 128), BF), ((depth + 2, 4, 64, 128), BF), ((depth + 2, wide, 32, 128), BF),
        ((nf, depth + 2, 4, 32, 128), BF), ((2, rows, 32, 128), BF), ((max(nf // 2 - 1, 1), 2, 6, 32, 128), BF), ((nf, 128, 896), BF),
        ((slab, 192, 128), BF), ((nf, 24, 96, 128), BF), ((slab, 96, 128), BF),
        ((depth * wide, 128, 128), BF), ((128, 1024), F32), ((128, 1024), F32),
        ((128, 1728), BF), ((64, 3456), BF), ((288, 384), BF),
        (((depth + 2) * rows, 32, 128), F32), ((2, rows, 32, 128), F32),
        ((depth, 2, 128, 128), BF), ((depth + 2, 4, 128, 128), BF), ((24, 384, 128), BF),
        ((24, 192, 128), BF), ((128, 896), BF), ((depth, 2, 64, 128), BF),
        ((ns * len1, 128), F32), ((ns * len1, 128), BF), ((ns - 1, len1, 128), BF), ((len1, 128), F32),
        ((max(columns_of - 1, 1), step1, 128), F32), ((step1, 128), F32), ((2 * nm, step1, 128), F32), ((ns * len1, 128), BF),
        ((ns * len2, 128), F32), ((ns * len2, 128), BF), ((ns - 1, len2, 128), BF),
        ((len2, 128), F32), ((nm, len2, 128), F32), ((ns * len2, 128), BF),
    ]
    copies = 160
    mo, g2o, g1o, vg = pl.pallas_call(
        functools.partial(whole_step, scaling),
        out_shape=[
            pltpu.VMEM((32, depth * rows, 128), F32),
            pltpu.VMEM((864, 128), F32),
            pltpu.VMEM((1728, 128), F32),
            pltpu.VMEM((64, 2 * depth, 128), F32),
        ],
        in_specs=[VMEM] * 4,
        out_specs=[VMEM] * 4,
        scratch_shapes=[pltpu.VMEM(shape, dtype) for shape, dtype in scratch] + [dma(copies), dma(copies)],
        compiler_params=pltpu.CompilerParams(
            vmem_limit_bytes=LIMIT, collective_id=0, has_side_effects=True
        ),
    )(vt, ct, wlt, w1)
    mapped = mo.reshape(1, 32, depth, rows, 128)
    return (mapped, g2o.reshape(27, 32, 128).transpose(0, 2, 1), g1o.reshape(27, 64, 128), vg.reshape(1, 64, depth, 2, 128))


def solution(mesh):
    placed = (
        P("sample", None, "spatial", "filter", None),
        P(),
        P(None, None, "filter"),
        P("sample", "filter", "spatial", None, None),
    )
    return jax.shard_map(
        on_device,
        mesh=mesh,
        in_specs=placed,
        out_specs=(
            P("sample", "filter", "spatial", None, None),
            P(None, None, "filter"),
            P(),
            P("sample", None, "spatial", "filter", None),
        ),
        check_vma=False,
    )
```

```python
import functools
import math

import jax
import jax.numpy as jnp
from jax import lax
from jax.experimental import pallas as pl
from jax.experimental.pallas import tpu as pltpu
from jax.sharding import PartitionSpec as P

MESH = pl.DeviceIdType.MESH
BF = jnp.bfloat16
F32 = jnp.float32
VMEM = pl.BlockSpec(memory_space=pltpu.VMEM)
LIMIT = 56 * 1024 * 1024


def remote(src, dst, send, recv, device):
    return pltpu.make_async_remote_copy(
        src_ref=src, dst_ref=dst, send_sem=send, recv_sem=recv, device_id=device, device_id_type=MESH
    )


def greet(partners):
    barrier = pltpu.get_barrier_semaphore()
    for partner in partners:
        pl.semaphore_signal(barrier, inc=1, device_id=partner, device_id_type=MESH)
    pl.semaphore_wait(barrier, len(partners))


def places():
    ns, nf, nm = lax.axis_size("spatial"), lax.axis_size("filter"), lax.axis_size("sample")
    s, f, m = lax.axis_index("spatial"), lax.axis_index("filter"), lax.axis_index("sample")
    return ns, nf, nm, s, f, m


def dma(n):
    return pltpu.SemaphoreType.DMA((n,))


def shifted(cells):
    wide = cells.astype(F32)
    lane = lax.broadcasted_iota(jnp.int32, wide.shape, 1)
    below = jnp.where(lane == 0, 0.0, pltpu.roll(wide, 1, 1)).astype(BF)
    above = jnp.where(lane == 127, 0.0, pltpu.roll(wide, 127, 1)).astype(BF)
    return below, cells, above


def spread(src, dst, flip):
    count, channels, _ = src.shape
    step = 6 if count % 6 == 0 else 4

    def body(i, carry):
        for u in range(step):
            below, here, above = shifted(src[i * step + u])
            first, last = (above, below) if flip else (below, above)
            dst[i * step + u, pl.ds(0, channels)] = first
            dst[i * step + u, pl.ds(channels, channels)] = here
            dst[i * step + u, pl.ds(2 * channels, channels)] = last
        return carry

    lax.fori_loop(0, count // step, body, 0)


def columns(ref, wide, rows_at, flip, pad):
    stack = []
    for sx in range(3):
        for sy in range(3):
            ox, oy = (2 - sx, 2 - sy) if flip else (sx, sy)
            stack.append(jnp.concatenate([ref[(x + ox) * wide + (y + oy)] for x, y in rows_at], axis=1))
    if pad:
        stack.append(jnp.zeros((pad, 128 * len(rows_at)), BF))
    return jnp.concatenate(stack, axis=0)


NT = (((1,), (1,)), ((), ()))


class Links:
    def __init__(self, send, recv):
        self.send, self.recv, self.used = send, recv, 0

    def __call__(self, src, dst, device):
        n = self.used
        self.used += 1
        return remote(src, dst, self.send.at[n], self.recv.at[n], device)


def start(copies):
    for copy in copies:
        copy.start()


def wait(copies):
    for copy in copies:
        copy.wait()


def zero(ref):
    ref[...] = jnp.zeros(ref.shape, ref.dtype)


class Summed:
    def __init__(self, links, at, whole, rounded, arrived, column, split, split_in, ring, place, mine, ring_in, held):
        self.links, self.at, self.whole, self.rounded, self.arrived = links, at, whole, rounded, arrived
        self.column, self.split, self.split_in = column, split, split_in
        self.ring, self.place, self.mine, self.ring_in, self.held = ring, place, mine, ring_in, held
        self.rows, self.step = arrived.shape[1], mine.shape[0]

    def scatter(self):
        ns, nf, nm, s, f, m = self.at
        self.rounded[...] = self.whole[...].astype(BF)
        self.targets, self.moving = [], []
        for r in range(1, ns):
            j = lax.rem(s + r, ns)
            self.targets.append({"spatial": j})
            self.moving.append(
                self.links(self.rounded.at[pl.ds(j * self.rows, self.rows)], self.arrived.at[r - 1], {"spatial": j})
            )
        start(self.moving)

    def spatial_sum(self):
        wait(self.moving)
        value = self.whole[pl.ds(self.at[3] * self.rows, self.rows)]
        for r in range(len(self.targets)):
            value = value + self.arrived[r].astype(F32)
        return value

    def columns(self):
        self.split[...] = self.spatial_sum()
        self.moving = [
            self.links(self.split.at[pl.ds(y * self.step, self.step)], self.split_in.at[i], device)
            for i, (y, device) in enumerate(self.column)
        ]
        start(self.moving)

    def rings(self):
        if self.split is None:
            value = self.spatial_sum()
        else:
            wait(self.moving)
            value = self.split[pl.ds(self.at[4] // 2 * self.step, self.step)]
            for i in range(len(self.column)):
                value = value + self.split_in[i]
        self.mine[...] = value
        self.ring_in[self.place] = value
        self.moving = [self.links(self.mine, self.ring_in.at[self.place], device) for device in self.ring]
        start(self.moving)

    def back(self):
        wait(self.moving)
        value = self.ring_in[0]
        for i in range(1, self.ring_in.shape[0]):
            value = value + self.ring_in[i]
        base = self.at[3] * self.rows
        self.block = pl.ds(base, self.rows)
        if self.split is not None:
            here = pl.ds(base + self.at[4] // 2 * self.step, self.step)
            self.held[here] = value.astype(BF)
            self.moving = [self.links(self.held.at[here], self.held.at[here], device) for y, device in self.column]
            start(self.moving)
        else:
            self.held[self.block] = value.astype(BF)
            self.moving = []

    def spread(self):
        wait(self.moving)
        self.moving = [self.links(self.held.at[self.block], self.held.at[self.block], device) for device in self.targets]
        start(self.moving)

    def finish(self):
        wait(self.moving)


DEPTH = 4


def around(block, padded):
    body, inner, two, pair = pl.ds(0, DEPTH), pl.ds(1, DEPTH), pl.ds(0, 2), pl.ds(1, 2)
    last = DEPTH - 1
    return [
        (block.at[body, 0], padded.at[inner, 3]), (block.at[body, 1], padded.at[inner, 0]),
        (block.at[0, two], padded.at[DEPTH + 1, pair]), (block.at[last, two], padded.at[0, pair]),
        (block.at[0, 0], padded.at[DEPTH + 1, 3]), (block.at[0, 1], padded.at[DEPTH + 1, 0]),
        (block.at[last, 0], padded.at[0, 3]), (block.at[last, 1], padded.at[0, 0]),
    ]


def clear_outside(padded, at):
    ns, nf, nm, s, f, m = at
    for place, end, plane in ((s, 0, 0), (s, ns - 1, DEPTH + 1)):
        @pl.when(place == end)
        def _():
            padded[plane] = jnp.zeros_like(padded[plane])
    for place, end, row in ((f, 0, 0), (f, nf - 1, 3)):
        @pl.when(place == end)
        def _():
            padded[:, row] = jnp.zeros_like(padded[:, row])


OWN = [(x, y) for x in range(DEPTH) for y in range(2)]


def whole_step(
    scaling, vtr, ctr, wlt, w1, mo, g2o, g1o, vg,
    vs, vo, cx, cg, cp, cy, wg, v3, c3, x3, hs, pre, acc, w1t, w1v, wm, me, mr, bp, bh, b3, v3o, wl, vt,
    g1w, g1s, g1p, g1q, g1y, g1m, g1r, g1b, g2w, g2s, g2p, g2m, g2r, g2b, send, recv,
):
    at = ns, nf, nm, s, f, m = places()
    links = Links(send, recv)
    depth, rows = DEPTH, 2 * nf
    wide = rows + 2
    part = 128 // ns
    nz = ns // 2
    core, z = lax.rem(s, 2), s // 2
    down, up = lax.rem(s + ns - 1, ns), lax.rem(s + 1, ns)
    left, right = lax.rem(f + nf - 1, nf), lax.rem(f + 1, nf)
    prev, after = {"spatial": down}, {"spatial": up}
    peers = [lax.rem(f + r, nf) for r in range(1, nf)]
    edges = [
        {"filter": left}, {"filter": right}, prev, after,
        {"spatial": down, "filter": left}, {"spatial": down, "filter": right},
        {"spatial": up, "filter": left}, {"spatial": up, "filter": right},
    ]
    ring = []
    for i in range(1, 2 * nm):
        j = lax.rem(lax.rem(f, 2) * nm + m + i, 2 * nm)
        ring.append({"filter": f - lax.rem(f, 2) + j // nm, "sample": lax.rem(j, nm)})
    other_sample = [{"sample": lax.rem(m + i, nm)} for i in range(1, nm)]
    group = [{"spatial": lax.rem(s + r, ns)} for r in range(1, ns)] + ring
    cx[:, 0] = jnp.zeros_like(cx[:, 0])
    cx[:, 2 * nf + 1] = jnp.zeros_like(cx[:, 0])
    for x in range(DEPTH):
        cx[x + 1, pl.ds(1, 2 * nf)] = jnp.swapaxes(ctr[:, pl.ds(x * 2 * nf, 2 * nf)].astype(F32), 0, 1).astype(BF)
    ct = cx.at[pl.ds(1, DEPTH)]
    vt[...] = jnp.swapaxes(vtr[...].astype(F32), 0, 1).astype(BF).reshape(DEPTH, 2, 64, 128)
    wl[...] = jnp.concatenate([wlt[...], jnp.zeros((32, 128), BF)], axis=0).T
    greet([{"filter": p} for p in peers] + edges[4:] + group)

    inner, body, two, pair = pl.ds(1, depth), pl.ds(0, depth), pl.ds(0, 2), pl.ds(1, 2)
    block = pl.ds(1 + 2 * f, 2)
    ny = nf // 2
    xl, yy = lax.rem(f, 2), f // 2
    fx = f + 1 - 2 * xl
    partner = {"filter": fx}
    ys = [lax.rem(yy + r, ny) for r in range(1, ny)]
    sources = [2 * lax.rem(yy + ny - r, ny) + xl for r in range(1, ny)]
    column = [{"filter": 2 * y + xl} for y in ys]
    lo, hi, glo, ghi = pl.ds(0, 2), pl.ds(2, 2), pl.ds(1, 2), pl.ds(3, 2)
    vol_x = links(vt, vs.at[inner, block], partner)
    vol_y = [links(vt, vs.at[inner, block], device) for device in column]
    mine = pl.ds(s * part, part)
    row = pl.ds(1, rows)
    halo = [links(ct.at[0, row], cx.at[depth + 1, row], prev), links(ct.at[depth - 1, row], cx.at[0, row], after)]
    weights = [links(wl.at[mine], wg.at[f, mine], {"filter": p}) for p in peers]
    cot_x = links(ct.at[lo, pl.ds(2 - 2 * xl, rows)], cp, partner)
    cot_y = [links(ct.at[hi, pl.ds(4 * y, 6)], cy.at[i], column[i]) for i, y in enumerate(ys)]
    cots = [links(ct.at[hi, pl.ds(2 * fx, 4)], cg.at[f, ghi], partner)]
    cots += [links(ct.at[lo, pl.ds(4 * y + 2 * xl, 4)], cg.at[f, glo], column[i]) for i, y in enumerate(ys)]
    corners = [links(src, dst, device) for (src, dst), device in zip(around(vt, vo), edges)]
    for copies in (weights, [cot_x], cot_y, cots, corners, halo):
        start(copies)

    vs[:, 0] = jnp.zeros_like(vs[:, 0])
    vs[:, rows + 1] = jnp.zeros_like(vs[:, 0])
    vs[inner, block] = vt[...]
    cg[f, inner] = ct[:, pl.ds(2 * f, 4)]
    wg[f, mine] = wl[mine]
    w1t[...] = w1[...].T
    for sx in range(3):
        for sy in range(3):
            for sz in range(3):
                k = sx * 9 + sy * 3 + sz
                w1v[:, 128 * k : 128 * (k + 1)] = w1[64 * k : 64 * (k + 1)]
                j = 32 * (sx * 3 + sz)
                wm[j : j + 32, 128 * sy : 128 * (sy + 1)] = wlt[32 * k : 32 * (k + 1)]
    zero(hs)
    zero(me)
    zero(acc)
    zero(g2w)

    wait(weights)
    along = [
        links(wg.at[:, mine], wg.at[:, mine], {"spatial": lax.rem(z + r, nz) * 2 + core}) for r in range(1, nz)
    ]
    start(along)

    cot_x.wait()
    onward = [links(cp.at[:, pl.ds(4 * y, 4)], cg.at[fx, glo], column[i]) for i, y in enumerate(ys)]
    start(onward)
    cots += onward
    cg[fx, glo] = cp[:, pl.ds(4 * yy, 4)]
    for i, k in enumerate(sources):
        cot_y[i].wait()
        onward = links(cy.at[i, :, pl.ds(2 - 2 * xl, 4)], cg.at[k, ghi], partner)
        onward.start()
        cots.append(onward)
        cg[k, ghi] = cy[i, :, pl.ds(2 * xl, 4)]

    start([vol_x] + vol_y)

    wait(halo)

    @pl.when(s == 0)
    def _():
        cx[0] = jnp.zeros_like(cx[0])

    @pl.when(s == ns - 1)
    def _():
        cx[depth + 1] = jnp.zeros_like(cx[0])

    cxr = cx.reshape((depth + 2) * wide, 32, 128)
    spread(cxr, x3, True)
    wait(corners)
    vo[inner, pair] = vt[...]
    clear_outside(vo, at)
    spread(vo.reshape((depth + 2) * 4, 64, 128), v3o, False)
    for part_at in range(2):
        lanes = pl.ds(512 * part_at, 512)
        pre[:, lanes] = jnp.dot(
            w1t[...], columns(v3o, 4, OWN[4 * part_at : 4 * part_at + 4], False, 0), preferred_element_type=F32
        )

    wait(cots)
    forward = [links(cg.at[:, 1], cg.at[:, depth + 1], prev), links(cg.at[:, depth], cg.at[:, 0], after)]
    start(forward)
    cgr = cg.reshape(nf, (depth + 2) * 4, 32, 128)

    def inside(k, carry):
        spread(cgr.at[k, pl.ds(4, 4 * depth)], c3.at[k, pl.ds(4, 4 * depth)], True)
        return carry

    lax.fori_loop(0, nf, inside, 0)
    vol_x.wait()
    over = pl.ds(1 + 2 * fx, 2)
    blocks = [links(vs.at[glo, over], vs.at[glo, over], device) for device in column]
    start(blocks)
    for copy, k in zip(vol_y, sources):
        copy.wait()
        there = pl.ds(1 + 2 * k, 2)
        onward = links(vs.at[ghi, there], vs.at[ghi, there], partner)
        onward.start()
        blocks.append(onward)
    wait(along)
    across = []
    for k in range(nz):
        piece = pl.ds((2 * k + core) * part, part)
        across.append(links(wg.at[:, piece], wg.at[:, piece], {"spatial": s + 1 - 2 * core}))
    start(across)
    wait(across)
    wait(forward)

    @pl.when(s == 0)
    def _():
        cg[:, 0] = jnp.zeros_like(cg[:, 0])

    @pl.when(s == ns - 1)
    def _():
        cg[:, depth + 1] = jnp.zeros_like(cg[:, 0])

    wait(blocks)
    row = pl.ds(1, rows)
    planes = [links(vs.at[1, row], vs.at[depth + 1, row], prev), links(vs.at[depth, row], vs.at[0, row], after)]
    start(planes)
    def back(k, carry):
        for plane in (0, depth + 1):
            span = pl.ds(4 * plane, 4)
            spread(cgr.at[k, span], c3.at[k, span], True)
        for part_at in range(2):
            lanes = pl.ds(512 * part_at, 512)
            acc[:, lanes] += jnp.dot(
                wg[k], columns(c3.at[k], 4, OWN[4 * part_at : 4 * part_at + 4], True, 32), preferred_element_type=F32
            )
        return carry

    lax.fori_loop(0, nf, back, 0)
    for n, (x, y) in enumerate(OWN):
        u = pre[:, 128 * n : 128 * (n + 1)]
        sig = jax.nn.sigmoid(u)
        bp[x, y] = (acc[:, 128 * n : 128 * (n + 1)] * (sig * (1.0 + u * (1.0 - sig)))).astype(BF)
    cells = [links(src, dst, device) for (src, dst), device in zip(around(bp, bh), edges)]
    bh[inner, pair] = bp[...]

    grads = jnp.concatenate([bp[x, y] for x, y in OWN], axis=1)
    for j in range(9):
        sx, sy = j // 3, j % 3
        field = jnp.concatenate([v3o[(x + sx) * 4 + y + sy] for x, y in OWN], axis=1)
        g1w[192 * j : 192 * (j + 1)] = lax.dot_general(field, grads, NT, preferred_element_type=F32)
    g1w[1728:] = jnp.zeros((g1w.shape[0] - 1728, 128), F32)
    one = Summed(
        links, at, g1w, g1s, g1p, list(zip(ys, column)), g1q, g1y, ring, xl * nm + m, g1m, g1r, g1b
    )
    one.scatter()
    start(cells)

    vsr = vs.reshape((depth + 2) * wide, 64, 128)
    spread(vsr.at[pl.ds(wide, depth * wide)], v3.at[pl.ds(wide, depth * wide)], False)
    lot = min(8, rows)
    times = rows // lot

    def first(i, carry):
        x, y = i // times, lax.rem(i, times) * lot
        value = jnp.dot(
            w1t[...], columns(v3, wide, [(x, y + j) for j in range(lot)], False, 0), preferred_element_type=F32
        )
        hidden = (value * jax.nn.sigmoid(value)).astype(BF)
        for j in range(lot):
            hs[x * wide + y + 1 + j] = hidden[:, 128 * j : 128 * (j + 1)]
        return carry

    lax.fori_loop(times, 3 * times, first, 0)
    wait(planes)

    @pl.when(s == 0)
    def _():
        vs[0] = jnp.zeros_like(vs[0])

    @pl.when(s == ns - 1)
    def _():
        vs[depth + 1] = jnp.zeros_like(vs[0])

    for plane in (0, depth + 1):
        span = pl.ds(plane * wide, wide)
        spread(vsr.at[span], v3.at[span], False)
    lax.fori_loop(0, times, first, 0)
    lax.fori_loop(3 * times, 4 * times, first, 0)

    one.columns()

    def second_weights(i, carry):
        x, y = i // times, lax.rem(i, times) * lot
        here = jnp.concatenate([hs[x * wide + y + j + 1] for j in range(lot)], axis=1)
        field = columns(x3, wide, [(x, y + j) for j in range(lot)], True, 32)
        g2w[...] += lax.dot_general(field, here, NT, preferred_element_type=F32)
        return carry

    lax.fori_loop(0, 2 * times, second_weights, 0)
    one.rings()
    lax.fori_loop(2 * times, 4 * times, second_weights, 0)
    other = Summed(links, at, g2w, g2s, g2p, [], None, None, other_sample, m, g2m, g2r, g2b)
    other.scatter()
    one.back()

    def second(i, carry):
        x, y = i // (times), lax.rem(i, times) * lot
        field = jnp.concatenate(
            [jnp.concatenate([hs[x * wide + y + j + sy] for j in range(lot)], axis=1) for sy in range(3)],
            axis=0,
        )
        value = jnp.dot(wm[...], field, preferred_element_type=F32)
        lane = lax.broadcasted_iota(jnp.int32, (32, 128), 1)
        for sx in range(3):
            for j in range(lot):
                lanes = slice(128 * j, 128 * (j + 1))
                base = 96 * sx
                below = pltpu.roll(value[base : base + 32, lanes], 1, 1)
                above = pltpu.roll(value[base + 64 : base + 96, lanes], 127, 1)
                me[(x + 2 - sx) * rows + y + j] += (
                    jnp.where(lane == 0, 0.0, below)
                    + value[base + 32 : base + 64, lanes]
                    + jnp.where(lane == 127, 0.0, above)
                )
        return carry

    turn = times
    lax.fori_loop(0, 2 * turn, second, 0)
    one.spread()
    other.rings()
    lax.fori_loop(2 * turn, 4 * turn, second, 0)
    other.back()
    other.spread()
    outer = [
        links(me.at[pl.ds(0, rows)], mr.at[1], prev),
        links(me.at[pl.ds((depth + 1) * rows, rows)], mr.at[0], after),
    ]
    start(outer)

    wait(cells)
    clear_outside(bh, at)
    spread(bh.reshape((depth + 2) * 4, 128, 128), b3, True)
    for part_at in range(2):
        value = jnp.dot(
            w1v[...], columns(b3, 4, OWN[4 * part_at : 4 * part_at + 4], True, 0), preferred_element_type=F32
        )
        for j in range(4):
            vg[:, 4 * part_at + j] = value[:, 128 * j : 128 * (j + 1)]
    wait(outer)

    @pl.when(s > 0)
    def _():
        me[pl.ds(rows, rows)] += mr[0]

    @pl.when(s < ns - 1)
    def _():
        me[pl.ds(depth * rows, rows)] += mr[1]

    for x in range(depth):
        mo[:, pl.ds(x * rows, rows)] = jnp.swapaxes(me[pl.ds((x + 1) * rows, rows)], 0, 1)
    other.finish()
    g2o[...] = g2b[0:864].astype(F32) * scaling
    one.finish()
    g1o[...] = g1b[0:1728].astype(F32) * scaling


def on_device(volume, weight_first, weight_second, cotangent):
    ns, nf, nm = lax.axis_size("spatial"), lax.axis_size("filter"), lax.axis_size("sample")
    depth, rows = DEPTH, 2 * nf
    wide = rows + 2
    scaling = 1.0 / math.sqrt(nm * depth * ns * rows * 128)

    vt = volume.reshape(64, 2 * depth, 128)
    ct = cotangent.reshape(32, depth * rows, 128)
    wlt = weight_second.transpose(0, 2, 1).reshape(864, 128)
    w1 = weight_first.reshape(1728, 128)

    columns_of = nf // 2
    step1 = -(-1728 // (16 * ns * columns_of)) * 16
    len1, len2 = step1 * columns_of, 896 // ns
    slab = (depth + 2) * wide
    scratch = [
        ((depth + 2, wide, 64, 128), BF), ((depth + 2, 4, 64, 128), BF), ((depth + 2, wide, 32, 128), BF),
        ((nf, depth + 2, 4, 32, 128), BF), ((2, rows, 32, 128), BF), ((max(nf // 2 - 1, 1), 2, 6, 32, 128), BF), ((nf, 128, 896), BF),
        ((slab, 192, 128), BF), ((nf, 24, 96, 128), BF), ((slab, 96, 128), BF),
        ((depth * wide, 128, 128), BF), ((128, 1024), F32), ((128, 1024), F32),
        ((128, 1728), BF), ((64, 3456), BF), ((288, 384), BF),
        (((depth + 2) * rows, 32, 128), F32), ((2, rows, 32, 128), F32),
        ((depth, 2, 128, 128), BF), ((depth + 2, 4, 128, 128), BF), ((24, 384, 128), BF),
        ((24, 192, 128), BF), ((128, 896), BF), ((depth, 2, 64, 128), BF),
        ((ns * len1, 128), F32), ((ns * len1, 128), BF), ((ns - 1, len1, 128), BF), ((len1, 128), F32),
        ((max(columns_of - 1, 1), step1, 128), F32), ((step1, 128), F32), ((2 * nm, step1, 128), F32), ((ns * len1, 128), BF),
        ((ns * len2, 128), F32), ((ns * len2, 128), BF), ((ns - 1, len2, 128), BF),
        ((len2, 128), F32), ((nm, len2, 128), F32), ((ns * len2, 128), BF),
    ]
    copies = 160
    mo, g2o, g1o, vg = pl.pallas_call(
        functools.partial(whole_step, scaling),
        out_shape=[
            pltpu.VMEM((32, depth * rows, 128), F32),
            pltpu.VMEM((864, 128), F32),
            pltpu.VMEM((1728, 128), F32),
            pltpu.VMEM((64, 2 * depth, 128), F32),
        ],
        in_specs=[VMEM] * 4,
        out_specs=[VMEM] * 4,
        scratch_shapes=[pltpu.VMEM(shape, dtype) for shape, dtype in scratch] + [dma(copies), dma(copies)],
        compiler_params=pltpu.CompilerParams(
            vmem_limit_bytes=LIMIT, collective_id=0, has_side_effects=True
        ),
    )(vt, ct, wlt, w1)
    mapped = mo.reshape(1, 32, depth, rows, 128)
    return (mapped, g2o.reshape(27, 32, 128).transpose(0, 2, 1), g1o.reshape(27, 64, 128), vg.reshape(1, 64, depth, 2, 128))


def solution(mesh):
    placed = (
        P("sample", None, "spatial", "filter", None),
        P(),
        P(None, None, "filter"),
        P("sample", "filter", "spatial", None, None),
    )
    return jax.shard_map(
        on_device,
        mesh=mesh,
        in_specs=placed,
        out_specs=(
            P("sample", "filter", "spatial", None, None),
            P(None, None, "filter"),
            P(),
            P("sample", None, "spatial", "filter", None),
        ),
        check_vma=False,
    )
```
